512 devices in a mesh: gx: 16 (over z, y_hi), gy: 4 (over y_lo), gz: 8 (over x, core).
Axes of the slice: x: 4, y: 8 (y_hi: 2, y_lo: 4; y = y_hi * 4 + y_lo), z: 8, core: 2. Of those that a mesh axis runs over, the one named last changes fastest.
Arguments:
- places: float32 [4096, 3], P(('gx', 'gy', 'gz')), may hold values from 0 to 1
- scalars: float32 [4096, 256], P(('gx', 'gy', 'gz')), may hold values from -6 to 6
- vectors: float32 [4096, 3, 256], P(('gx', 'gy', 'gz')), may hold values from -6 to 6
- species: int32 [4096], P(('gx', 'gy', 'gz')), may hold values from 0 to 3
- bound_rows: int32 [4096], P(('gx', 'gy', 'gz')), may hold values from 0 to 7, as said below
- bound_count: int32 [512], P(('gx', 'gy', 'gz')), may hold values from 4 to 8, as said below
- neighbour_ids: int32 [16, 4096], P(None, ('gx', 'gy', 'gz')), may hold values from 0 to 223, as said below
- neighbour_count: int32 [4096], P(('gx', 'gy', 'gz')), may hold values from 3 to 16, as said below
- radial_first: bfloat16 [8, 64], replicated, may hold values from -2 to 2
- radial_second: bfloat16 [64, 64], replicated, may hold values from -0.75 to 0.75
- radial_third: bfloat16 [64, 1536], replicated, may hold values from -0.75 to 0.75
- energy_table: float32 [4, 256], replicated, may hold values from -6 to 6
- vector_gains: float32 [256], replicated, may hold values from -3 to 3
Outputs:
- atom_energy: float32 [4096], P(('gx', 'gy', 'gz'))
- forces: float32 [4096, 3], P(('gx', 'gy', 'gz'))
- grad_scalars: float32 [4096, 256], P(('gx', 'gy', 'gz'))
- grad_vectors: float32 [4096, 3, 256], P(('gx', 'gy', 'gz'))
The draws below stay inside these ranges and needn't reach their ends.
Inputs may be any that keep to these rules, and one draw needn't show every extreme that they name: `bound_rows`: per domain, 8 distinct indices of its own atoms (0 to 7). `bound_count`: some domain has all 8 slots live. `neighbour_ids`: below 8: an owned atom other than the atom itself; otherwise 8 + t * 8 + b for ghost block t, never the centre block 13, and any slot b, live or not. `neighbour_count`: slots k below the count are listed neighbours. Domains differ in their largest count; some atom has 16.
All inputs are finite; a program needn't handle non-finite values.
Results may differ from the reference program's by a relative error of at most 0.014.
Values sent between devices are 32-bit elements; how exact they have to be, the bound alone decides.
A program may use at most 64 MiB of HBM per device.

```python
import jax
import jax.numpy as jnp
from jax import lax

ATOMS_DEV = 8
BOUNDARY = 8
NEIGHBOURS = 16
CHANNELS = 256
RADIAL_HIDDEN = 64
GAUSSIANS = 8
SPECIES = 4
RADIAL_OUT = 1536
ATOMS_ALL = 4096
N_GX = 16
N_GY = 4
N_GZ = 8


def draw_bound_rows(key, part):
    domains = N_GX * N_GY * N_GZ
    scores = jax.random.randint(key, (domains, ATOMS_DEV), 0, 1 << 20) * ATOMS_DEV + jnp.arange(ATOMS_DEV).astype(jnp.int32)[None]
    order = jnp.argsort(scores, axis=1, stable=True)
    return order[:, :BOUNDARY].reshape(-1).astype(jnp.int32)


def draw_bound_count(key, part):
    domains = N_GX * N_GY * N_GZ
    key_one, key_two = jax.random.split(jax.random.fold_in(key, 11))
    counts = jax.random.randint(key_one, (domains,), BOUNDARY // 2, BOUNDARY + 1)
    fullest = jax.random.randint(key_two, (), 0, domains)
    return jnp.where(jnp.arange(domains) == fullest, BOUNDARY, counts).astype(jnp.int32)


def draw_neighbour_ids(key, part):
    domains = N_GX * N_GY * N_GZ
    total = domains * ATOMS_DEV
    keys = jax.random.split(jax.random.fold_in(key, 23), 4)
    local = jnp.arange(total).astype(jnp.int32) % ATOMS_DEV
    pick = jax.random.randint(keys[0], (NEIGHBOURS, total), 0, 10)
    owned_pick = (local[None] + 1 + jax.random.randint(keys[1], (NEIGHBOURS, total), 0, ATOMS_DEV - 1)) % ATOMS_DEV
    block = jax.random.randint(keys[2], (NEIGHBOURS, total), 0, 26)
    block = block + (block >= 13).astype(jnp.int32)
    slot = jax.random.randint(keys[3], (NEIGHBOURS, total), 0, BOUNDARY)
    ghost_pick = ATOMS_DEV + block * BOUNDARY + slot
    return jnp.where(pick < 3, owned_pick, ghost_pick).astype(jnp.int32)


def draw_neighbour_count(key, part):
    domains = N_GX * N_GY * N_GZ
    keys = jax.random.split(jax.random.fold_in(key, 37), 4)
    ceiling = jax.random.randint(keys[0], (domains,), NEIGHBOURS // 4, NEIGHBOURS + 1)
    fullest = jax.random.randint(keys[1], (), 0, domains)
    ceiling = jnp.where(jnp.arange(domains) == fullest, NEIGHBOURS, ceiling)
    halfway = ceiling // 2
    spread = jax.random.randint(keys[2], (domains, ATOMS_DEV), 0, 1 << 20)
    counts = halfway[:, None] + 1 + spread % (ceiling - halfway)[:, None]
    peak = jax.random.randint(keys[3], (domains,), 0, ATOMS_DEV)
    counts = jnp.where(jnp.arange(ATOMS_DEV)[None] == peak[:, None], ceiling[:, None], counts)
    return counts.reshape(-1).astype(jnp.int32)


def plant(values, rng, low, top_value):
    place = [jax.random.randint(jax.random.fold_in(rng, axis), (), 0, length) for axis, length in enumerate(values.shape)]
    longest = values.shape.index(max(values.shape))
    next_to = place[:longest] + [(place[longest] + 1) % values.shape[longest]] + place[longest + 1:]
    return values.at[tuple(place)].set(low).at[tuple(next_to)].set(top_value)


def level_of(stream_key, extent, shards, smallest, high):
    gain = 1.0
    for axis_at, parts in shards:
        draws = jax.random.uniform(jax.random.fold_in(jax.random.fold_in(stream_key, 6), axis_at), (parts,), jnp.float32, smallest / len(shards), high / len(shards))
        gain = gain * jnp.repeat(jnp.exp(draws), extent[axis_at] // parts).reshape((-1,) + (1,) * (len(extent) - 1 - axis_at))
    return gain


def normal_values(rng, dims, scale, limit, cuts=(), kind=jnp.bfloat16):
    entries = jax.random.normal(rng, dims, jnp.float32) * scale
    if len(cuts) > 0:
        entries = level_of(rng, dims, cuts, -0.22, 0.18) * entries
    return jnp.clip(entries, min=-limit, max=limit).astype(kind)


def setup_inputs(seed: int = 0) -> dict:
    key_list = jax.random.split(jax.random.key(seed), 14)
    return {
        "places": jnp.clip(1.0 * jax.random.uniform(key_list[0], (ATOMS_ALL, 3), jnp.float32) ** level_of(key_list[0], (ATOMS_ALL, 3), ((0, 512),), -0.2, 0.2), 0.0, 1.0),
        "scalars": normal_values(key_list[1], (ATOMS_ALL, CHANNELS), 1.0, 6.0, ((0, 512),), jnp.float32),
        "vectors": normal_values(key_list[2], (ATOMS_ALL, 3, CHANNELS), 1.0, 6.0, ((0, 512),), jnp.float32),
        "species": plant(jax.random.randint(key_list[3], (ATOMS_ALL,), 0, SPECIES), jax.random.fold_in(key_list[3], 1), 0, SPECIES - 1).astype(jnp.int32),
        "bound_rows": draw_bound_rows(jax.random.fold_in(key_list[13], 71), 0),
        "bound_count": draw_bound_count(jax.random.fold_in(key_list[13], 71), 0),
        "neighbour_ids": draw_neighbour_ids(jax.random.fold_in(key_list[13], 71), 0),
        "neighbour_count": draw_neighbour_count(jax.random.fold_in(key_list[13], 71), 0),
        "radial_first": normal_values(key_list[8], (GAUSSIANS, RADIAL_HIDDEN), GAUSSIANS ** -0.5, 2.0),
        "radial_second": normal_values(key_list[9], (RADIAL_HIDDEN, RADIAL_HIDDEN), RADIAL_HIDDEN ** -0.5, 0.75),
        "radial_third": normal_values(key_list[10], (RADIAL_HIDDEN, RADIAL_OUT), RADIAL_HIDDEN ** -0.5, 0.75),
        "energy_table": normal_values(key_list[11], (SPECIES, CHANNELS), 1.0, 6.0, (), jnp.float32),
        "vector_gains": normal_values(key_list[12], (CHANNELS,), 0.5, 3.0, (), jnp.float32),
    }


SOFTENING = 0.25
SHARPNESS = 2.0
FIRST_CENTRE = 0.5
SPACING = 0.4
EDGE = 1.0

def edge_messages(row_table, index_rows, usable, radial_first, radial_second, radial_third):
    slot_rows, atoms_here = index_rows.shape
    channels = (row_table.shape[1] - 3) // 4
    owned_places = row_table[:atoms_here, :3]
    far_rows = row_table[index_rows]
    separation = far_rows[:, :, :3] - owned_places[None]
    distance = jnp.sqrt(lax.optimization_barrier(jnp.sum(separation * separation, axis=2)) + SOFTENING)
    direction = separation / distance[:, :, None]
    centres = FIRST_CENTRE + SPACING * jnp.arange(radial_first.shape[0]).astype(jnp.float32)
    gauss_basis = jnp.exp(-SHARPNESS * (distance[:, :, None] - centres) ** 2)
    flat_basis = gauss_basis.reshape(slot_rows * atoms_here, -1).astype(jnp.bfloat16)
    hidden_one = jax.nn.silu(jnp.dot(flat_basis, radial_first, preferred_element_type=jnp.float32)).astype(jnp.bfloat16)
    hidden_two = jax.nn.silu(jnp.dot(hidden_one, radial_second, preferred_element_type=jnp.float32)).astype(jnp.bfloat16)
    path_weights = jnp.dot(hidden_two, radial_third, preferred_element_type=jnp.float32).reshape(slot_rows, atoms_here, 6, channels)
    far_scalars = far_rows[:, :, 3:3 + channels]
    far_vectors = far_rows[:, :, 3 + channels:].reshape(slot_rows, atoms_here, 3, channels)
    projected = lax.optimization_barrier(jnp.sum(direction[:, :, :, None] * far_vectors, axis=2))
    crossed = jnp.stack([far_vectors[:, :, 1] * direction[:, :, 2:3] - far_vectors[:, :, 2] * direction[:, :, 1:2], far_vectors[:, :, 2] * direction[:, :, 0:1] - far_vectors[:, :, 0] * direction[:, :, 2:3], far_vectors[:, :, 0] * direction[:, :, 1:2] - far_vectors[:, :, 1] * direction[:, :, 0:1]], axis=2)
    scalar_message = path_weights[:, :, 0] * far_scalars + path_weights[:, :, 1] * projected
    vector_message = path_weights[:, :, 2:3] * far_scalars[:, :, None] * direction[:, :, :, None] + path_weights[:, :, 3:4] * far_vectors + path_weights[:, :, 4:5] * crossed + path_weights[:, :, 5:6] * (direction[:, :, :, None] * projected[:, :, None] - far_vectors / 3.0)
    weight = usable[:, :, None]
    return (lax.optimization_barrier(jnp.sum(weight * scalar_message, axis=0)), lax.optimization_barrier(jnp.sum(weight[:, :, :, None] * vector_message, axis=0)))

def atom_energy_of(scalar_out, vector_out, species_here, energy_table, vector_gains):
    channels = scalar_out.shape[1]
    onehot = (species_here[:, None] == jnp.arange(energy_table.shape[0]).astype(jnp.int32)[None]).astype(jnp.float32)
    species_coeff = jnp.dot(onehot, energy_table, precision=lax.Precision.HIGHEST)
    squares = lax.optimization_barrier(jnp.sum(vector_out * vector_out, axis=1))
    return (lax.optimization_barrier(jnp.sum(species_coeff * jax.nn.silu(scalar_out), axis=1)) + lax.optimization_barrier(jnp.sum(vector_gains * squares, axis=1))) * channels ** (-0.25)

def reference(places, scalars, vectors, species, bound_rows, bound_count, neighbour_ids, neighbour_count, radial_first, radial_second, radial_third, energy_table, vector_gains):
    domains = N_GX * N_GY * N_GZ
    scale = NEIGHBOURS ** (-0.5)
    ids_all = neighbour_ids.reshape(NEIGHBOURS, domains, ATOMS_DEV).transpose(1, 0, 2)
    usable_all = (jnp.arange(NEIGHBOURS).astype(jnp.int32)[None, :, None] < neighbour_count.reshape(domains, 1, ATOMS_DEV)).astype(jnp.float32)
    species_all = species.reshape(domains, ATOMS_DEV)
    boundary_idx = bound_rows.reshape(domains, BOUNDARY)
    alive_mask = (jnp.arange(BOUNDARY).astype(jnp.int32)[None] < bound_count[:, None]).astype(jnp.float32)

    def one_domain(inputs):
        row_table, ids_here, usable_here, species_here = inputs
        summed_scalar, summed_vector = edge_messages(row_table, ids_here, usable_here, radial_first, radial_second, radial_third)
        owned_rows = row_table[:ATOMS_DEV]
        scalar_out = owned_rows[:, 3:3 + CHANNELS] + scale * summed_scalar
        vector_out = owned_rows[:, 3 + CHANNELS:].reshape(ATOMS_DEV, 3, CHANNELS) + scale * summed_vector
        return atom_energy_of(scalar_out, vector_out, species_here, energy_table, vector_gains)

    def all_energy(places_in, scalars_in, vectors_in):
        owned_rows = jnp.concatenate([places_in, scalars_in, vectors_in.reshape(ATOMS_ALL, 3 * CHANNELS)], axis=1)
        owned_rows = owned_rows.reshape(domains, ATOMS_DEV, -1)
        packets = jnp.take_along_axis(owned_rows, boundary_idx[:, :, None], axis=1) * alive_mask[:, :, None]
        packet_grid = packets.reshape(N_GX, N_GY, N_GZ, BOUNDARY, -1)
        blocks = []
        for along_x in (-1, 0, 1):
            for along_y in (-1, 0, 1):
                for along_z in (-1, 0, 1):
                    rolled = jnp.roll(packet_grid, (-along_x, -along_y, -along_z), (0, 1, 2))
                    displace = jnp.array([along_x, along_y, along_z], jnp.float32) * EDGE
                    rolled = jnp.concatenate([rolled[..., :3] + displace, rolled[..., 3:]], axis=-1)
                    blocks.append(rolled.reshape(domains, BOUNDARY, -1))
        ghosts = jnp.concatenate(blocks, axis=1)
        tables = jnp.concatenate([owned_rows, ghosts], axis=1)
        energies = lax.map(jax.checkpoint(one_domain), (tables, ids_all, usable_all, species_all))
        return energies.reshape(-1)
    energies, pullback = jax.vjp(all_energy, places, scalars, vectors)
    grad_places, grad_scalars, grad_vectors = pullback(jnp.ones_like(energies))
    return (energies, -grad_places, grad_scalars, grad_vectors)
```

```python
import functools

import jax
import jax.numpy as jnp
from jax import lax
from jax.experimental import pallas as pl
from jax.experimental.pallas import tpu as pltpu
from jax.sharding import PartitionSpec as P

SOFTENING = 0.25
SHARPNESS = 2.0
FIRST_CENTRE = 0.5
SPACING = 0.4
EDGE = 1.0

MESH = pl.DeviceIdType.MESH
HIGHEST = lax.Precision.HIGHEST
NT = (((1,), (1,)), ((), ()))

OWN, NEAR, FAR = 9, 12, 15
SELF = 10
RAW = 27


def sigmoid(x):
    return 1.0 / (1.0 + jnp.exp(-x))


def column(row):
    n = row.shape[1]
    eye = lax.broadcasted_iota(jnp.int32, (n, n), 0) == lax.broadcasted_iota(jnp.int32, (n, n), 1)
    return jnp.sum(jnp.where(eye, jnp.broadcast_to(row, (n, n)), 0.0), axis=1, keepdims=True)


def row_of(col):
    n = col.shape[0]
    eye = lax.broadcasted_iota(jnp.int32, (n, n), 0) == lax.broadcasted_iota(jnp.int32, (n, n), 1)
    return jnp.sum(jnp.where(eye, jnp.broadcast_to(col, (n, n)), 0.0), axis=0, keepdims=True)


def kernel(
    sizes,
    count_ref,
    places_ref,
    scalars_ref,
    vectors_ref,
    species_ref,
    bound_ref,
    ids_ref,
    ncount_ref,
    first_ref,
    second_ref,
    third_ref,
    energy_table_ref,
    gains_ref,
    energy_ref,
    forces_ref,
    gscal_ref,
    gvec_ref,
    table,
    grads,
    from_z,
    from_x,
    from_y,
    hot,
    hot_t,
    far,
    weights,
    units,
    turn,
    edge_grads,
    weight_grads,
    send_sem,
    recv_sem,
    back_send,
    back_recv,
):
    nx, ny, nz = sizes
    atoms, channels = scalars_ref.shape
    slots = ids_ref.shape[1]
    edges = slots * atoms
    width = 4 * channels
    gx, gy, gz = lax.axis_index("gx"), lax.axis_index("gy"), lax.axis_index("gz")
    odd = lax.rem(gx, 2)
    sign = 1 - 2 * odd
    near = gx + sign
    ahead = lax.rem(gx + 2 * sign + nx, nx)
    behind = lax.rem(gx - 2 * sign + nx, nx)
    up, down = lax.rem(gy + 1, ny), lax.rem(gy + ny - 1, ny)
    right, left = lax.rem(gz + 1, nz), lax.rem(gz + nz - 1, nz)

    barrier = pltpu.get_barrier_semaphore()
    partners = [
        (near, down, gz),
        (near, gy, gz),
        (near, up, gz),
        (gx, down, gz),
        (gx, up, gz),
        (ahead, gy, gz),
        (behind, gy, gz),
        (gx, gy, left),
        (gx, gy, right),
    ]
    for partner in partners:
        pl.semaphore_signal(barrier, inc=1, device_id=partner, device_id_type=MESH)

    lane = lax.broadcasted_iota(jnp.int32, (atoms, 128), 1)
    sub = lax.broadcasted_iota(jnp.int32, (atoms, 1), 0)
    own_places = jnp.zeros((atoms, 128), jnp.float32)
    for a in range(3):
        own_places = jnp.where(lane == a, column(places_ref[a : a + 1, :]), own_places)
    table[RAW, :, 0:channels] = scalars_ref[...]
    for a in range(3):
        table[RAW, :, (a + 1) * channels : (a + 2) * channels] = vectors_ref[a]
    table[RAW, :, width:] = own_places
    bound = column(bound_ref[...].astype(jnp.float32))
    alive = sub < count_ref[0]
    picks = [(bound == float(i)) & alive for i in range(atoms)]
    for c in range(0, width + 128, 128):
        block = table[RAW, :, c : c + 128]
        packet = jnp.zeros((atoms, 128), jnp.float32)
        for i in range(atoms):
            packet = jnp.where(picks[i], block[i : i + 1, :], packet)
        table[SELF, :, c : c + 128] = packet

    pl.semaphore_wait(barrier, len(partners))

    def copy(index, source, target, partner, sems=(send_sem, recv_sem)):
        made = pltpu.make_async_remote_copy(
            src_ref=source,
            dst_ref=target,
            send_sem=sems[0].at[index],
            recv_sem=sems[1].at[index],
            device_id=partner,
            device_id_type=MESH,
        )
        made.start()
        return made

    def blocks(ref, start, count=3):
        return ref.at[pl.ds(start, count)]

    sends = []
    to_near = [
        copy(2 + n, blocks(table, SELF, 1), blocks(table, NEAR + n, 1), (near, place, gz))
        for n, place in ((0, up), (1, gy), (2, down))
    ]
    to_side = [
        copy(0, blocks(table, SELF, 1), blocks(table, OWN, 1), (gx, up, gz)),
        copy(1, blocks(table, SELF, 1), blocks(table, OWN + 2, 1), (gx, down, gz)),
    ]

    ids = ids_ref[...]
    ghost = jnp.maximum(ids - atoms, 0)
    t = lax.shift_right_logical(ghost, 3)
    one = lambda test: jnp.where(test, 1, 0)
    ox = one(t >= 9) + one(t >= 18) - 1
    rest = t - 9 * (ox + 1)
    oy = one(rest >= 3) + one(rest >= 6) - 1
    oz = rest - 3 * (oy + 1) - 1
    group = jnp.where(ox == 0, 0, jnp.where(ox == sign, 1, 2))
    mapped = 8 * (9 * (oz + 1) + 3 * group + (oy + 1)) + (ghost & 7)
    mapped = jnp.where(ids < atoms, 8 * RAW + ids, mapped)
    rows = 8 * (RAW + 1)
    row_iota = lax.broadcasted_iota(jnp.int32, (atoms, rows), 1)
    hot_f32 = jnp.concatenate(
        [jnp.where(mapped[:, k : k + 1] == row_iota, 1.0, 0.0) for k in range(slots)], axis=0
    )
    hot[...] = hot_f32
    hot_t[...] = hot_f32.T

    for made in to_side:
        made.wait()
    sends.append(copy(6, blocks(table, OWN), blocks(table, 0), (gx, gy, right)))
    sends.append(copy(7, blocks(table, OWN), blocks(table, 18), (gx, gy, left)))
    for made in to_near:
        made.wait()
    ahead_copy = copy(5, blocks(table, NEAR), blocks(table, FAR), (ahead, gy, gz))
    sends.append(copy(8, blocks(table, NEAR), blocks(table, 3), (gx, gy, right)))
    sends.append(copy(9, blocks(table, NEAR), blocks(table, 21), (gx, gy, left)))
    ahead_copy.wait()
    sends.append(copy(10, blocks(table, FAR), blocks(table, 6), (gx, gy, right)))
    sends.append(copy(11, blocks(table, FAR), blocks(table, 24), (gx, gy, left)))
    for made in sends:
        made.wait()

    fsign = sign.astype(jnp.float32)
    unit = [jnp.where(lane == a, EDGE, 0.0) for a in range(3)]
    moved = []
    for z in (-1.0, 0.0, 1.0):
        for g in (0.0, fsign, -fsign):
            for y in (-1.0, 0.0, 1.0):
                moved.append(unit[0] * g + unit[1] * y + unit[2] * z)
    moved.append(jnp.zeros((atoms, 128), jnp.float32))
    positions = jnp.concatenate(
        [table[n, :, width:] + moved[n] for n in range(RAW + 1)], axis=0
    )
    picked = jnp.dot(hot[...], positions, precision=HIGHEST, preferred_element_type=jnp.float32)
    apart = picked.reshape(slots, atoms, 128) - own_places[None]
    distance = jnp.sqrt(jnp.sum(apart * apart, axis=2, keepdims=True) + SOFTENING)
    inverse = 1.0 / distance
    for a in range(3):
        units[a] = jnp.broadcast_to(apart[:, :, a : a + 1] * inverse, (slots, atoms, 128))
    distance = distance.reshape(edges, 1)
    gaussians = first_ref.shape[0]
    centres = FIRST_CENTRE + SPACING * lax.broadcasted_iota(
        jnp.int32, (edges, gaussians), 1
    ).astype(jnp.float32)
    gap = distance - centres
    gauss = jnp.exp(-SHARPNESS * gap * gap)
    pre_one = jnp.dot(
        gauss.astype(jnp.bfloat16), first_ref[...], preferred_element_type=jnp.float32
    )
    gate_one = sigmoid(pre_one)
    hidden_one = (pre_one * gate_one).astype(jnp.bfloat16)
    pre_two = jnp.dot(hidden_one, second_ref[...], preferred_element_type=jnp.float32)
    gate_two = sigmoid(pre_two)
    ncount = column(ncount_ref[...].astype(jnp.float32))
    listed = jnp.concatenate(
        [jnp.where(ncount > float(k), 1.0, 0.0) for k in range(slots)], axis=0
    )
    hidden_two = (pre_two * gate_two * listed).astype(jnp.bfloat16)
    weights[...] = jnp.dot(
        hidden_two, third_ref[...], preferred_element_type=jnp.float32
    ).reshape(slots, atoms, 6 * channels)

    features = table[:, :, 0:width].reshape(rows, width).astype(jnp.bfloat16)
    far[...] = jnp.dot(
        hot[...].astype(jnp.bfloat16), features, preferred_element_type=jnp.float32
    ).reshape(slots, atoms, width)

    step = 2
    scale = slots ** (-0.5)
    quarter = channels ** (-0.25)
    species = column(species_ref[...].astype(jnp.float32))
    energy = jnp.zeros((atoms, 1), jnp.float32)
    cotans = []
    halves = channels // 128

    def loads(ks, h):
        w = [weights[ks, :, n * channels + h * 128 : n * channels + h * 128 + 128] for n in range(6)]
        s = far[ks, :, h * 128 : h * 128 + 128]
        v = [
            far[ks, :, (a + 1) * channels + h * 128 : (a + 1) * channels + h * 128 + 128]
            for a in range(3)
        ]
        u = [units[a, ks] for a in range(3)]
        return w, s, v, u

    def cross(x, y):
        return [
            x[1] * y[2] - x[2] * y[1],
            x[2] * y[0] - x[0] * y[2],
            x[0] * y[1] - x[1] * y[0],
        ]

    def dot3(x, y):
        return x[0] * y[0] + x[1] * y[1] + x[2] * y[2]

    for h in range(halves):
        cut = slice(h * 128, h * 128 + 128)

        def forward(n, carry, h=h):
            ks = pl.ds(n * step, step)
            w, s, v, u = loads(ks, h)
            q = dot3(u, v)
            turned = cross(v, u)
            along = w[2] * s + w[5] * q
            straight = w[3] - w[5] * (1.0 / 3.0)
            out = [carry[0] + jnp.sum(w[0] * s + w[1] * q, axis=0)]
            for a in range(3):
                out.append(
                    carry[1 + a]
                    + jnp.sum(along * u[a] + straight * v[a] + w[4] * turned[a], axis=0)
                )
            return tuple(out)

        zero = jnp.zeros((atoms, 128), jnp.float32)
        sums = lax.fori_loop(0, slots // step, forward, (zero,) * 4)
        s_out = scalars_ref[:, cut] + scale * sums[0]
        v_out = [vectors_ref[a, :, cut] + scale * sums[1 + a] for a in range(3)]
        coeff = jnp.zeros((atoms, 128), jnp.float32)
        for z in range(energy_table_ref.shape[0]):
            coeff = jnp.where(species == float(z), energy_table_ref[z : z + 1, cut], coeff)
        gains = gains_ref[:, cut]
        gate = sigmoid(s_out)
        part = coeff * (s_out * gate) + gains * dot3(v_out, v_out)
        energy = energy + jnp.sum(part, axis=1, keepdims=True)
        cs = quarter * coeff * (gate * (1.0 + s_out * (1.0 - gate)))
        cv = [(2.0 * quarter) * gains * v for v in v_out]
        cotans.append((cs, cv))
    energy_ref[...] = row_of(energy * quarter)

    for h in range(halves):
        cs, cv = cotans[h]
        gs = (scale * cs)[None]
        gv = [(scale * c)[None] for c in cv]

        def backward(n, carry, h=h, gs=gs, gv=gv):
            ks = pl.ds(n * step, step)
            row = pl.ds(pl.multiple_of(n * step * atoms, step * atoms), step * atoms)
            w, s, v, u = loads(ks, h)
            q = dot3(u, v)
            turned = cross(v, u)
            p = dot3(gv, u)
            same = dot3(gv, v)

            def put(ref, block, value):
                ref[row, block * channels + h * 128 : block * channels + h * 128 + 128] = (
                    value.reshape(step * atoms, 128).astype(jnp.bfloat16)
                )

            put(weight_grads, 0, gs * s)
            put(weight_grads, 1, gs * q)
            put(weight_grads, 2, s * p)
            put(weight_grads, 3, same)
            put(weight_grads, 4, dot3(gv, turned))
            put(weight_grads, 5, p * q - same * (1.0 / 3.0))
            dq = w[1] * gs + w[5] * p
            straight = w[3] - w[5] * (1.0 / 3.0)
            put(edge_grads, 0, w[0] * gs + w[2] * p)
            back = cross(u, gv)
            along = w[2] * s + w[5] * q
            spun = cross(gv, v)
            for a in range(3):
                put(edge_grads, 1 + a, dq * u[a] + straight * gv[a] + w[4] * back[a])
                piece = dq * v[a] + along * gv[a] + w[4] * spun[a]
                if h == 0:
                    turn[a, ks] = piece
                else:
                    turn[a, ks] += piece
            return carry

        lax.fori_loop(0, slots // step, backward, 0)

    summed = jnp.dot(
        hot_t[...].astype(jnp.bfloat16), edge_grads[...], preferred_element_type=jnp.float32
    )
    grads[:, :, 0:width] = summed.reshape(RAW + 1, atoms, width)

    d_two = lax.dot_general(
        weight_grads[...], third_ref[...], NT, preferred_element_type=jnp.float32
    )
    d_two = d_two * listed * (gate_two * (1.0 + pre_two * (1.0 - gate_two)))
    d_one = lax.dot_general(
        d_two.astype(jnp.bfloat16), second_ref[...], NT, preferred_element_type=jnp.float32
    )
    d_one = d_one * (gate_one * (1.0 + pre_one * (1.0 - gate_one)))
    d_gauss = lax.dot_general(
        d_one.astype(jnp.bfloat16), first_ref[...], NT, preferred_element_type=jnp.float32
    )
    d_distance = jnp.sum(
        d_gauss * gauss * gap * (-2.0 * SHARPNESS), axis=1, keepdims=True
    ).reshape(slots, atoms, 1)
    d_unit = [jnp.sum(turn[a], axis=2, keepdims=True) for a in range(3)]
    u = [units[a, :, :, 0:1] for a in range(3)]
    radial = d_distance - dot3(d_unit, u) * inverse
    lanes = lax.broadcasted_iota(jnp.int32, (slots, atoms, 128), 2)
    d_apart = jnp.zeros((slots, atoms, 128), jnp.float32)
    for a in range(3):
        d_apart = jnp.where(lanes == a, d_unit[a] * inverse + radial * u[a], d_apart)
    pulled = jnp.dot(
        hot_t[...],
        d_apart.reshape(edges, 128),
        precision=HIGHEST,
        preferred_element_type=jnp.float32,
    )
    grads[:, :, width:] = pulled.reshape(RAW + 1, atoms, 128)

    back = (back_send, back_recv)
    returns = []
    for g in (2, 1, 0):
        returns.append(
            (
                copy(6 + 2 * g, blocks(grads, 3 * g), blocks(from_z, 3 * g), (gx, gy, left), back),
                copy(
                    7 + 2 * g,
                    blocks(grads, 18 + 3 * g),
                    blocks(from_z, 9 + 3 * g),
                    (gx, gy, right),
                    back,
                ),
            )
        )
    pending = []

    def fold(g):
        for made in returns[2 - g]:
            made.wait()
        total = grads[OWN + 3 * g : OWN + 3 * g + 3]
        return total + from_z[3 * g : 3 * g + 3] + from_z[9 + 3 * g : 12 + 3 * g]

    grads[FAR : FAR + 3] = fold(2)
    far_copy = copy(5, blocks(grads, FAR), blocks(from_x, 0), (behind, gy, gz), back)
    near_sum = fold(1)
    far_copy.wait()
    grads[NEAR : NEAR + 3] = near_sum + from_x[...]
    for n, place in ((0, down), (1, gy), (2, up)):
        pending.append(
            copy(
                2 + n,
                blocks(grads, NEAR + n, 1),
                blocks(from_y, 4 - n, 1),
                (near, place, gz),
                back,
            )
        )
    grads[OWN : OWN + 3] = fold(0)
    pending.append(copy(0, blocks(grads, OWN, 1), blocks(from_y, 0, 1), (gx, down, gz), back))
    pending.append(copy(1, blocks(grads, OWN + 2, 1), blocks(from_y, 1, 1), (gx, up, gz), back))
    for made in pending:
        made.wait()

    def final(c):
        cut = slice(c, c + 128)
        total = grads[SELF, :, cut]
        for n in range(5):
            total = total + from_y[n, :, cut]
        total = jnp.where(alive, total, 0.0)
        back_home = grads[RAW, :, cut]
        for b in range(atoms):
            back_home = back_home + jnp.where(homes[b], total[b : b + 1, :], 0.0)
        return back_home

    homes = [bound_ref[:, b : b + 1] == sub for b in range(atoms)]
    for h in range(halves):
        cs, cv = cotans[h]
        cut = slice(h * 128, h * 128 + 128)
        gscal_ref[:, cut] = final(h * 128) + cs
        for a in range(3):
            gvec_ref[a, :, cut] = final((a + 1) * channels + h * 128) + cv[a]
    pull = jnp.sum(d_apart, axis=0) - final(width)
    for a in range(3):
        forces_ref[a : a + 1, :] = row_of(pull[:, a : a + 1])


def shards(sizes):
    def run(
        places,
        scalars,
        vectors,
        species,
        bound_rows,
        bound_count,
        neighbour_ids,
        neighbour_count,
        radial_first,
        radial_second,
        radial_third,
        energy_table,
        vector_gains,
    ):
        atoms, channels = scalars.shape
        slots = neighbour_ids.shape[0]
        edges = slots * atoms
        packed = 4 * channels + 128
        vmem = pl.BlockSpec(memory_space=pltpu.VMEM)
        f32 = jnp.float32
        energies, forces, grad_scalars, grad_vectors = pl.pallas_call(
            functools.partial(kernel, sizes),
            out_shape=(
                jax.ShapeDtypeStruct((1, atoms), f32),
                jax.ShapeDtypeStruct((3, atoms), f32),
                jax.ShapeDtypeStruct((atoms, channels), f32),
                jax.ShapeDtypeStruct((3, atoms, channels), f32),
            ),
            in_specs=[pl.BlockSpec(memory_space=pltpu.SMEM)] + [vmem] * 12,
            out_specs=(vmem,) * 4,
            scratch_shapes=[
                pltpu.VMEM((RAW + 1, atoms, packed), f32),
                pltpu.VMEM((RAW + 1, atoms, packed), f32),
                pltpu.VMEM((18, atoms, packed), f32),
                pltpu.VMEM((3, atoms, packed), f32),
                pltpu.VMEM((5, atoms, packed), f32),
                pltpu.VMEM((edges, 8 * (RAW + 1)), f32),
                pltpu.VMEM((8 * (RAW + 1), edges), f32),
                pltpu.VMEM((slots, atoms, 4 * channels), f32),
                pltpu.VMEM((slots, atoms, 6 * channels), f32),
                pltpu.VMEM((3, slots, atoms, 128), f32),
                pltpu.VMEM((3, slots, atoms, 128), f32),
                pltpu.VMEM((edges, 4 * channels), jnp.bfloat16),
                pltpu.VMEM((edges, 6 * channels), jnp.bfloat16),
                pltpu.SemaphoreType.DMA((12,)),
                pltpu.SemaphoreType.DMA((12,)),
                pltpu.SemaphoreType.DMA((12,)),
                pltpu.SemaphoreType.DMA((12,)),
            ],
            compiler_params=pltpu.CompilerParams(
                collective_id=0, has_side_effects=True, vmem_limit_bytes=48 * 1024 * 1024
            ),
        )(
            bound_count,
            places.T,
            scalars,
            vectors.transpose(1, 0, 2),
            species.reshape(1, -1),
            bound_rows.reshape(1, -1),
            neighbour_ids.T,
            neighbour_count.reshape(1, -1),
            radial_first,
            radial_second,
            radial_third,
            energy_table,
            vector_gains.reshape(1, -1),
        )
        return energies.reshape(-1), forces.T, grad_scalars, grad_vectors.transpose(1, 0, 2)

    return run


def solution(mesh):
    spread = ("gx", "gy", "gz")
    in_specs = (
        P(spread, None),
        P(spread, None),
        P(spread, None, None),
        P(spread),
        P(spread),
        P(spread),
        P(None, spread),
        P(spread),
        P(),
        P(),
        P(),
        P(),
        P(),
    )
    out_specs = (P(spread), P(spread, None), P(spread, None), P(spread, None, None))
    sizes = tuple(mesh.shape[axis] for axis in spread)
    return jax.shard_map(
        shards(sizes), mesh=mesh, in_specs=in_specs, out_specs=out_specs, check_vma=False
    )
```

```python
import functools

import jax
import jax.numpy as jnp
from jax import lax
from jax.experimental import pallas as pl
from jax.experimental.pallas import tpu as pltpu
from jax.sharding import PartitionSpec as P

SOFTENING = 0.25
SHARPNESS = 2.0
FIRST_CENTRE = 0.5
SPACING = 0.4
EDGE = 1.0

MESH = pl.DeviceIdType.MESH
HIGHEST = lax.Precision.HIGHEST
NT = (((1,), (1,)), ((), ()))

OWN, NEAR, FAR = 9, 12, 15
SELF = 10
RAW = 27


def sigmoid(x):
    return 1.0 / (1.0 + jnp.exp(-x))


def column(row):
    n = row.shape[1]
    eye = lax.broadcasted_iota(jnp.int32, (n, n), 0) == lax.broadcasted_iota(jnp.int32, (n, n), 1)
    return jnp.sum(jnp.where(eye, jnp.broadcast_to(row, (n, n)), 0.0), axis=1, keepdims=True)


def row_of(col):
    n = col.shape[0]
    eye = lax.broadcasted_iota(jnp.int32, (n, n), 0) == lax.broadcasted_iota(jnp.int32, (n, n), 1)
    return jnp.sum(jnp.where(eye, jnp.broadcast_to(col, (n, n)), 0.0), axis=0, keepdims=True)


def kernel(
    sizes,
    count_ref,
    places_hbm,
    scalars_hbm,
    vectors_hbm,
    species_hbm,
    bound_hbm,
    ids_hbm,
    ncount_hbm,
    first_hbm,
    second_hbm,
    third_hbm,
    energy_table_hbm,
    gains_hbm,
    energy_ref,
    forces_ref,
    gscal_ref,
    gvec_ref,
    places_ref,
    species_ref,
    bound_ref,
    ids_ref,
    ncount_ref,
    first_ref,
    second_ref,
    third_ref,
    energy_table_ref,
    gains_ref,
    load_sem,
    table,
    grads,
    from_z,
    from_x,
    from_y,
    hot,
    hot_t,
    far,
    weights,
    units,
    turn,
    edge_grads,
    weight_grads,
    send_sem,
    recv_sem,
    back_send,
    back_recv,
):
    nx, ny, nz = sizes
    atoms, channels = scalars_hbm.shape
    slots = ids_ref.shape[1]
    edges = slots * atoms
    width = 4 * channels
    gx, gy, gz = lax.axis_index("gx"), lax.axis_index("gy"), lax.axis_index("gz")
    odd = lax.rem(gx, 2)
    sign = 1 - 2 * odd
    near = gx + sign
    ahead = lax.rem(gx + 2 * sign + nx, nx)
    behind = lax.rem(gx - 2 * sign + nx, nx)
    up, down = lax.rem(gy + 1, ny), lax.rem(gy + ny - 1, ny)
    right, left = lax.rem(gz + 1, nz), lax.rem(gz + nz - 1, nz)

    barrier = pltpu.get_barrier_semaphore()
    partners = [
        (near, down, gz),
        (near, gy, gz),
        (near, up, gz),
        (gx, down, gz),
        (gx, up, gz),
        (ahead, gy, gz),
        (behind, gy, gz),
        (gx, gy, left),
        (gx, gy, right),
    ]
    for partner in partners:
        pl.semaphore_signal(barrier, inc=1, device_id=partner, device_id_type=MESH)

    loads_first = [
        (scalars_hbm, table.at[RAW, :, pl.ds(0, channels)]),
        (vectors_hbm.at[0], table.at[RAW, :, pl.ds(channels, channels)]),
        (vectors_hbm.at[1], table.at[RAW, :, pl.ds(2 * channels, channels)]),
        (vectors_hbm.at[2], table.at[RAW, :, pl.ds(3 * channels, channels)]),
        (places_hbm, places_ref),
        (bound_hbm, bound_ref),
    ]
    loads_later = [
        (ids_hbm, ids_ref),
        (first_hbm, first_ref),
        (second_hbm, second_ref),
        (third_hbm, third_ref),
        (ncount_hbm, ncount_ref),
        (species_hbm, species_ref),
        (energy_table_hbm, energy_table_ref),
        (gains_hbm, gains_ref),
    ]
    incoming = []
    for n, (source, target) in enumerate(loads_first + loads_later):
        made = pltpu.make_async_copy(source, target, load_sem.at[n])
        made.start()
        incoming.append(made)

    for made in incoming[: len(loads_first)]:
        made.wait()
    lane = lax.broadcasted_iota(jnp.int32, (atoms, 128), 1)
    sub = lax.broadcasted_iota(jnp.int32, (atoms, 1), 0)
    own_places = jnp.zeros((atoms, 128), jnp.float32)
    for a in range(3):
        own_places = jnp.where(lane == a, column(places_ref[a : a + 1, :]), own_places)
    table[RAW, :, width:] = own_places
    bound = column(bound_ref[...].astype(jnp.float32))
    alive = sub < count_ref[0]
    picks = [(bound == float(i)) & alive for i in range(atoms)]
    for c in range(0, width + 128, 128):
        block = table[RAW, :, c : c + 128]
        packet = jnp.zeros((atoms, 128), jnp.float32)
        for i in range(atoms):
            packet = jnp.where(picks[i], block[i : i + 1, :], packet)
        table[SELF, :, c : c + 128] = packet

    pl.semaphore_wait(barrier, len(partners))

    def copy(index, source, target, partner, sems=(send_sem, recv_sem)):
        made = pltpu.make_async_remote_copy(
            src_ref=source,
            dst_ref=target,
            send_sem=sems[0].at[index],
            recv_sem=sems[1].at[index],
            device_id=partner,
            device_id_type=MESH,
        )
        made.start()
        return made

    def blocks(ref, start, count=3):
        return ref.at[pl.ds(start, count)]

    sends = []
    to_near = [
        copy(2 + n, blocks(table, SELF, 1), blocks(table, NEAR + n, 1), (near, place, gz))
        for n, place in ((0, up), (1, gy), (2, down))
    ]
    to_side = [
        copy(0, blocks(table, SELF, 1), blocks(table, OWN, 1), (gx, up, gz)),
        copy(1, blocks(table, SELF, 1), blocks(table, OWN + 2, 1), (gx, down, gz)),
    ]

    for made in incoming[len(loads_first) :]:
        made.wait()

    ids = ids_ref[...]
    ghost = jnp.maximum(ids - atoms, 0)
    t = lax.shift_right_logical(ghost, 3)
    one = lambda test: jnp.where(test, 1, 0)
    ox = one(t >= 9) + one(t >= 18) - 1
    rest = t - 9 * (ox + 1)
    oy = one(rest >= 3) + one(rest >= 6) - 1
    oz = rest - 3 * (oy + 1) - 1
    group = jnp.where(ox == 0, 0, jnp.where(ox == sign, 1, 2))
    mapped = 8 * (9 * (oz + 1) + 3 * group + (oy + 1)) + (ghost & 7)
    mapped = jnp.where(ids < atoms, 8 * RAW + ids, mapped)
    rows = 8 * (RAW + 1)
    row_iota = lax.broadcasted_iota(jnp.int32, (atoms, rows), 1)
    hot_f32 = jnp.concatenate(
        [jnp.where(mapped[:, k : k + 1] == row_iota, 1.0, 0.0) for k in range(slots)], axis=0
    )
    hot[...] = hot_f32
    hot_t[...] = hot_f32.T

    for made in to_side:
        made.wait()
    sends.append(copy(6, blocks(table, OWN), blocks(table, 0), (gx, gy, right)))
    sends.append(copy(7, blocks(table, OWN), blocks(table, 18), (gx, gy, left)))
    for made in to_near:
        made.wait()
    ahead_copy = copy(5, blocks(table, NEAR), blocks(table, FAR), (ahead, gy, gz))
    sends.append(copy(8, blocks(table, NEAR), blocks(table, 3), (gx, gy, right)))
    sends.append(copy(9, blocks(table, NEAR), blocks(table, 21), (gx, gy, left)))
    ahead_copy.wait()
    sends.append(copy(10, blocks(table, FAR), blocks(table, 6), (gx, gy, right)))
    sends.append(copy(11, blocks(table, FAR), blocks(table, 24), (gx, gy, left)))
    for made in sends:
        made.wait()

    fsign = sign.astype(jnp.float32)
    unit = [jnp.where(lane == a, EDGE, 0.0) for a in range(3)]
    moved = []
    for z in (-1.0, 0.0, 1.0):
        for g in (0.0, fsign, -fsign):
            for y in (-1.0, 0.0, 1.0):
                moved.append(unit[0] * g + unit[1] * y + unit[2] * z)
    moved.append(jnp.zeros((atoms, 128), jnp.float32))
    positions = jnp.concatenate(
        [table[n, :, width:] + moved[n] for n in range(RAW + 1)], axis=0
    )
    picked = jnp.dot(hot[...], positions, precision=HIGHEST, preferred_element_type=jnp.float32)
    apart = picked.reshape(slots, atoms, 128) - own_places[None]
    distance = jnp.sqrt(jnp.sum(apart * apart, axis=2, keepdims=True) + SOFTENING)
    inverse = 1.0 / distance
    for a in range(3):
        units[a] = jnp.broadcast_to(apart[:, :, a : a + 1] * inverse, (slots, atoms, 128))
    distance = distance.reshape(edges, 1)
    gaussians = first_ref.shape[0]
    centres = FIRST_CENTRE + SPACING * lax.broadcasted_iota(
        jnp.int32, (edges, gaussians), 1
    ).astype(jnp.float32)
    gap = distance - centres
    gauss = jnp.exp(-SHARPNESS * gap * gap)
    pre_one = jnp.dot(
        gauss.astype(jnp.bfloat16), first_ref[...], preferred_element_type=jnp.float32
    )
    gate_one = sigmoid(pre_one)
    hidden_one = (pre_one * gate_one).astype(jnp.bfloat16)
    pre_two = jnp.dot(hidden_one, second_ref[...], preferred_element_type=jnp.float32)
    gate_two = sigmoid(pre_two)
    ncount = column(ncount_ref[...].astype(jnp.float32))
    listed = jnp.concatenate(
        [jnp.where(ncount > float(k), 1.0, 0.0) for k in range(slots)], axis=0
    )
    hidden_two = (pre_two * gate_two * listed).astype(jnp.bfloat16)
    weights[...] = jnp.dot(
        hidden_two, third_ref[...], preferred_element_type=jnp.float32
    ).reshape(slots, atoms, 6 * channels)

    features = table[:, :, 0:width].reshape(rows, width).astype(jnp.bfloat16)
    far[...] = jnp.dot(
        hot[...].astype(jnp.bfloat16), features, preferred_element_type=jnp.float32
    ).reshape(slots, atoms, width)

    step = 2
    scale = slots ** (-0.5)
    quarter = channels ** (-0.25)
    species = column(species_ref[...].astype(jnp.float32))
    energy = jnp.zeros((atoms, 1), jnp.float32)
    cotans = []
    halves = channels // 128

    def loads(ks, h):
        w = [weights[ks, :, n * channels + h * 128 : n * channels + h * 128 + 128] for n in range(6)]
        s = far[ks, :, h * 128 : h * 128 + 128]
        v = [
            far[ks, :, (a + 1) * channels + h * 128 : (a + 1) * channels + h * 128 + 128]
            for a in range(3)
        ]
        u = [units[a, ks] for a in range(3)]
        return w, s, v, u

    def cross(x, y):
        return [
            x[1] * y[2] - x[2] * y[1],
            x[2] * y[0] - x[0] * y[2],
            x[0] * y[1] - x[1] * y[0],
        ]

    def dot3(x, y):
        return x[0] * y[0] + x[1] * y[1] + x[2] * y[2]

    for h in range(halves):
        cut = slice(h * 128, h * 128 + 128)

        def forward(n, carry, h=h):
            ks = pl.ds(n * step, step)
            w, s, v, u = loads(ks, h)
            q = dot3(u, v)
            turned = cross(v, u)
            along = w[2] * s + w[5] * q
            straight = w[3] - w[5] * (1.0 / 3.0)
            out = [carry[0] + jnp.sum(w[0] * s + w[1] * q, axis=0)]
            for a in range(3):
                out.append(
                    carry[1 + a]
                    + jnp.sum(along * u[a] + straight * v[a] + w[4] * turned[a], axis=0)
                )
            return tuple(out)

        zero = jnp.zeros((atoms, 128), jnp.float32)
        sums = lax.fori_loop(0, slots // step, forward, (zero,) * 4)
        s_out = table[RAW, :, cut] + scale * sums[0]
        v_out = [table[RAW, :, (a + 1) * channels + h * 128 : (a + 1) * channels + h * 128 + 128] + scale * sums[1 + a] for a in range(3)]
        coeff = jnp.zeros((atoms, 128), jnp.float32)
        for z in range(energy_table_ref.shape[0]):
            coeff = jnp.where(species == float(z), energy_table_ref[z : z + 1, cut], coeff)
        gains = gains_ref[:, cut]
        gate = sigmoid(s_out)
        part = coeff * (s_out * gate) + gains * dot3(v_out, v_out)
        energy = energy + jnp.sum(part, axis=1, keepdims=True)
        cs = quarter * coeff * (gate * (1.0 + s_out * (1.0 - gate)))
        cv = [(2.0 * quarter) * gains * v for v in v_out]
        cotans.append((cs, cv))
    energy_ref[...] = row_of(energy * quarter)

    for h in range(halves):
        cs, cv = cotans[h]
        gs = (scale * cs)[None]
        gv = [(scale * c)[None] for c in cv]

        def backward(n, carry, h=h, gs=gs, gv=gv):
            ks = pl.ds(n * step, step)
            row = pl.ds(pl.multiple_of(n * step * atoms, step * atoms), step * atoms)
            w, s, v, u = loads(ks, h)
            q = dot3(u, v)
            turned = cross(v, u)
            p = dot3(gv, u)
            same = dot3(gv, v)

            def put(ref, block, value):
                ref[row, block * channels + h * 128 : block * channels + h * 128 + 128] = (
                    value.reshape(step * atoms, 128).astype(jnp.bfloat16)
                )

            put(weight_grads, 0, gs * s)
            put(weight_grads, 1, gs * q)
            put(weight_grads, 2, s * p)
            put(weight_grads, 3, same)
            put(weight_grads, 4, dot3(gv, turned))
            put(weight_grads, 5, p * q - same * (1.0 / 3.0))
            dq = w[1] * gs + w[5] * p
            straight = w[3] - w[5] * (1.0 / 3.0)
            put(edge_grads, 0, w[0] * gs + w[2] * p)
            back = cross(u, gv)
            along = w[2] * s + w[5] * q
            spun = cross(gv, v)
            for a in range(3):
                put(edge_grads, 1 + a, dq * u[a] + straight * gv[a] + w[4] * back[a])
                piece = dq * v[a] + along * gv[a] + w[4] * spun[a]
                if h == 0:
                    turn[a, ks] = piece
                else:
                    turn[a, ks] += piece
            return carry

        lax.fori_loop(0, slots // step, backward, 0)

    summed = jnp.dot(
        hot_t[...].astype(jnp.bfloat16), edge_grads[...], preferred_element_type=jnp.float32
    )
    grads[:, :, 0:width] = summed.reshape(RAW + 1, atoms, width)

    d_two = lax.dot_general(
        weight_grads[...], third_ref[...], NT, preferred_element_type=jnp.float32
    )
    d_two = d_two * listed * (gate_two * (1.0 + pre_two * (1.0 - gate_two)))
    d_one = lax.dot_general(
        d_two.astype(jnp.bfloat16), second_ref[...], NT, preferred_element_type=jnp.float32
    )
    d_one = d_one * (gate_one * (1.0 + pre_one * (1.0 - gate_one)))
    d_gauss = lax.dot_general(
        d_one.astype(jnp.bfloat16), first_ref[...], NT, preferred_element_type=jnp.float32
    )
    d_distance = jnp.sum(
        d_gauss * gauss * gap * (-2.0 * SHARPNESS), axis=1, keepdims=True
    ).reshape(slots, atoms, 1)
    d_unit = [jnp.sum(turn[a], axis=2, keepdims=True) for a in range(3)]
    u = [units[a, :, :, 0:1] for a in range(3)]
    radial = d_distance - dot3(d_unit, u) * inverse
    lanes = lax.broadcasted_iota(jnp.int32, (slots, atoms, 128), 2)
    d_apart = jnp.zeros((slots, atoms, 128), jnp.float32)
    for a in range(3):
        d_apart = jnp.where(lanes == a, d_unit[a] * inverse + radial * u[a], d_apart)
    pulled = jnp.dot(
        hot_t[...],
        d_apart.reshape(edges, 128),
        precision=HIGHEST,
        preferred_element_type=jnp.float32,
    )
    grads[:, :, width:] = pulled.reshape(RAW + 1, atoms, 128)

    back = (back_send, back_recv)
    returns = []
    for g in (2, 1, 0):
        returns.append(
            (
                copy(6 + 2 * g, blocks(grads, 3 * g), blocks(from_z, 3 * g), (gx, gy, left), back),
                copy(
                    7 + 2 * g,
                    blocks(grads, 18 + 3 * g),
                    blocks(from_z, 9 + 3 * g),
                    (gx, gy, right),
                    back,
                ),
            )
        )
    pending = []

    def fold(g):
        for made in returns[2 - g]:
            made.wait()
        total = grads[OWN + 3 * g : OWN + 3 * g + 3]
        return total + from_z[3 * g : 3 * g + 3] + from_z[9 + 3 * g : 12 + 3 * g]

    grads[FAR : FAR + 3] = fold(2)
    far_copy = copy(5, blocks(grads, FAR), blocks(from_x, 0), (behind, gy, gz), back)
    near_sum = fold(1)
    far_copy.wait()
    grads[NEAR : NEAR + 3] = near_sum + from_x[...]
    for n, place in ((0, down), (1, gy), (2, up)):
        pending.append(
            copy(
                2 + n,
                blocks(grads, NEAR + n, 1),
                blocks(from_y, 4 - n, 1),
                (near, place, gz),
                back,
            )
        )
    grads[OWN : OWN + 3] = fold(0)
    pending.append(copy(0, blocks(grads, OWN, 1), blocks(from_y, 0, 1), (gx, down, gz), back))
    pending.append(copy(1, blocks(grads, OWN + 2, 1), blocks(from_y, 1, 1), (gx, up, gz), back))
    for made in pending:
        made.wait()

    def final(c):
        cut = slice(c, c + 128)
        total = grads[SELF, :, cut]
        for n in range(5):
            total = total + from_y[n, :, cut]
        total = jnp.where(alive, total, 0.0)
        back_home = grads[RAW, :, cut]
        for b in range(atoms):
            back_home = back_home + jnp.where(homes[b], total[b : b + 1, :], 0.0)
        return back_home

    homes = [bound_ref[:, b : b + 1] == sub for b in range(atoms)]
    for h in range(halves):
        cs, cv = cotans[h]
        cut = slice(h * 128, h * 128 + 128)
        gscal_ref[:, cut] = final(h * 128) + cs
        for a in range(3):
            gvec_ref[a, :, cut] = final((a + 1) * channels + h * 128) + cv[a]
    pull = jnp.sum(d_apart, axis=0) - final(width)
    for a in range(3):
        forces_ref[a : a + 1, :] = row_of(pull[:, a : a + 1])


def settle(*refs):
    count = len(refs) // 2
    sems = refs[-1]
    made = [
        pltpu.make_async_copy(refs[n], refs[count + n], sems.at[n]) for n in range(count)
    ]
    for m in made:
        m.start()
    for m in made:
        m.wait()


def shards(sizes):
    def run(
        places,
        scalars,
        vectors,
        species,
        bound_rows,
        bound_count,
        neighbour_ids,
        neighbour_count,
        radial_first,
        radial_second,
        radial_third,
        energy_table,
        vector_gains,
    ):
        atoms, channels = scalars.shape
        slots = neighbour_ids.shape[0]
        edges = slots * atoms
        packed = 4 * channels + 128
        vmem = pl.BlockSpec(memory_space=pltpu.VMEM)
        hbm = pl.BlockSpec(memory_space=pl.ANY)
        f32 = jnp.float32
        operands = (
            bound_count,
            places.T,
            scalars,
            vectors.transpose(1, 0, 2),
            species.reshape(1, -1),
            bound_rows.reshape(1, -1),
            neighbour_ids.T,
            neighbour_count.reshape(1, -1),
            radial_first,
            radial_second,
            radial_third,
            energy_table,
            vector_gains.reshape(1, -1),
        )
        landing = [
            pltpu.VMEM(x.shape, x.dtype) for n, x in enumerate(operands) if n not in (0, 2, 3)
        ]
        out_shape = (
            jax.ShapeDtypeStruct((1, atoms), f32),
            jax.ShapeDtypeStruct((3, atoms), f32),
            jax.ShapeDtypeStruct((atoms, channels), f32),
            jax.ShapeDtypeStruct((3, atoms, channels), f32),
        )
        results = pl.pallas_call(
            functools.partial(kernel, sizes),
            out_shape=out_shape,
            in_specs=[pl.BlockSpec(memory_space=pltpu.SMEM)] + [hbm] * 12,
            out_specs=(vmem,) * 4,
            scratch_shapes=landing
            + [
                pltpu.SemaphoreType.DMA((14,)),
                pltpu.VMEM((RAW + 1, atoms, packed), f32),
                pltpu.VMEM((RAW + 1, atoms, packed), f32),
                pltpu.VMEM((18, atoms, packed), f32),
                pltpu.VMEM((3, atoms, packed), f32),
                pltpu.VMEM((5, atoms, packed), f32),
                pltpu.VMEM((edges, 8 * (RAW + 1)), f32),
                pltpu.VMEM((8 * (RAW + 1), edges), f32),
                pltpu.VMEM((slots, atoms, 4 * channels), f32),
                pltpu.VMEM((slots, atoms, 6 * channels), f32),
                pltpu.VMEM((3, slots, atoms, 128), f32),
                pltpu.VMEM((3, slots, atoms, 128), f32),
                pltpu.VMEM((edges, 4 * channels), jnp.bfloat16),
                pltpu.VMEM((edges, 6 * channels), jnp.bfloat16),
                pltpu.SemaphoreType.DMA((12,)),
                pltpu.SemaphoreType.DMA((12,)),
                pltpu.SemaphoreType.DMA((12,)),
                pltpu.SemaphoreType.DMA((12,)),
            ],
            compiler_params=pltpu.CompilerParams(
                collective_id=0, has_side_effects=True, vmem_limit_bytes=56 * 1024 * 1024
            ),
        )(*operands)
        energies, forces, grad_scalars, grad_vectors = pl.pallas_call(
            settle,
            out_shape=out_shape,
            in_specs=[hbm] * 4,
            out_specs=(hbm,) * 4,
            scratch_shapes=[pltpu.SemaphoreType.DMA((4,))],
            compiler_params=pltpu.CompilerParams(vmem_limit_bytes=56 * 1024 * 1024),
        )(*results)
        return energies.reshape(-1), forces.T, grad_scalars, grad_vectors.transpose(1, 0, 2)

    return run


def solution(mesh):
    spread = ("gx", "gy", "gz")
    in_specs = (
        P(spread, None),
        P(spread, None),
        P(spread, None, None),
        P(spread),
        P(spread),
        P(spread),
        P(None, spread),
        P(spread),
        P(),
        P(),
        P(),
        P(),
        P(),
    )
    out_specs = (P(spread), P(spread, None), P(spread, None), P(spread, None, None))
    sizes = tuple(mesh.shape[axis] for axis in spread)
    return jax.shard_map(
        shards(sizes), mesh=mesh, in_specs=in_specs, out_specs=out_specs, check_vma=False
    )
```

```python
import functools

import jax
import jax.numpy as jnp
from jax import lax
from jax.experimental import pallas as pl
from jax.experimental.pallas import tpu as pltpu
from jax.sharding import PartitionSpec as P

SOFTENING = 0.25
SHARPNESS = 2.0
FIRST_CENTRE = 0.5
SPACING = 0.4
EDGE = 1.0

MESH = pl.DeviceIdType.MESH
HIGHEST = lax.Precision.HIGHEST
NT = (((1,), (1,)), ((), ()))

OWN, NEAR, FAR = 9, 12, 15
SELF = 10
RAW = 27


def sigmoid(x):
    return 1.0 / (1.0 + jnp.exp(-x))


def column(row):
    n = row.shape[1]
    eye = lax.broadcasted_iota(jnp.int32, (n, n), 0) == lax.broadcasted_iota(jnp.int32, (n, n), 1)
    return jnp.sum(jnp.where(eye, jnp.broadcast_to(row, (n, n)), 0.0), axis=1, keepdims=True)


def row_of(col):
    n = col.shape[0]
    eye = lax.broadcasted_iota(jnp.int32, (n, n), 0) == lax.broadcasted_iota(jnp.int32, (n, n), 1)
    return jnp.sum(jnp.where(eye, jnp.broadcast_to(col, (n, n)), 0.0), axis=0, keepdims=True)


def kernel(
    sizes,
    count_ref,
    places_hbm,
    scalars_hbm,
    vectors_hbm,
    species_hbm,
    bound_hbm,
    ids_hbm,
    ncount_hbm,
    first_hbm,
    second_hbm,
    third_hbm,
    energy_table_hbm,
    gains_hbm,
    energy_ref,
    forces_ref,
    gscal_ref,
    gvec_ref,
    places_ref,
    species_ref,
    bound_ref,
    ids_ref,
    ncount_ref,
    first_ref,
    second_ref,
    third_ref,
    energy_table_ref,
    gains_ref,
    load_sem,
    table,
    grads,
    from_z,
    from_x,
    from_w,
    from_y,
    hot,
    hot_t,
    far,
    weights,
    units,
    turn,
    edge_grads,
    weight_grads,
    send_sem,
    recv_sem,
    back_send,
    back_recv,
    ready,
):
    nx, ny, nz = sizes
    atoms, channels = scalars_hbm.shape
    slots = ids_ref.shape[1]
    edges = slots * atoms
    width = 4 * channels
    gx, gy, gz = lax.axis_index("gx"), lax.axis_index("gy"), lax.axis_index("gz")
    odd = lax.rem(gx, 2)
    sign = 1 - 2 * odd
    near = gx + sign
    ahead = lax.rem(gx + 2 * sign + nx, nx)
    behind = lax.rem(gx - 2 * sign + nx, nx)
    up, down = lax.rem(gy + 1, ny), lax.rem(gy + ny - 1, ny)
    right, left = lax.rem(gz + 1, nz), lax.rem(gz + nz - 1, nz)

    first, last = gx == 0, gx == nx - 1
    three = ((0, down), (1, gy), (2, up))
    barrier = pltpu.get_barrier_semaphore()

    def hello(partner):
        pl.semaphore_signal(barrier, inc=1, device_id=partner, device_id_type=MESH)

    partners = [
        (near, down, gz),
        (near, gy, gz),
        (near, up, gz),
        (gx, down, gz),
        (gx, up, gz),
        (gx, gy, left),
        (gx, gy, right),
    ]
    for partner in partners:
        hello(partner)
    for other in (ahead, behind):

        @pl.when(other > gx)
        def _(other=other):
            hello((other, gy, gz))

    @pl.when(first)
    def _():
        for n, place in three:
            hello((nx - 1, place, gz))

    loads_first = [
        (scalars_hbm, table.at[RAW, :, pl.ds(0, channels)]),
        (vectors_hbm.at[0], table.at[RAW, :, pl.ds(channels, channels)]),
        (vectors_hbm.at[1], table.at[RAW, :, pl.ds(2 * channels, channels)]),
        (vectors_hbm.at[2], table.at[RAW, :, pl.ds(3 * channels, channels)]),
        (places_hbm, places_ref),
        (bound_hbm, bound_ref),
    ]
    loads_later = [
        (ids_hbm, ids_ref),
        (first_hbm, first_ref),
        (second_hbm, second_ref),
        (third_hbm, third_ref),
        (ncount_hbm, ncount_ref),
        (species_hbm, species_ref),
        (energy_table_hbm, energy_table_ref),
        (gains_hbm, gains_ref),
    ]
    incoming = []
    for n, (source, target) in enumerate(loads_first + loads_later):
        made = pltpu.make_async_copy(source, target, load_sem.at[n])
        made.start()
        incoming.append(made)

    for made in incoming[: len(loads_first)]:
        made.wait()
    lane = lax.broadcasted_iota(jnp.int32, (atoms, 128), 1)
    sub = lax.broadcasted_iota(jnp.int32, (atoms, 1), 0)
    own_places = jnp.zeros((atoms, 128), jnp.float32)
    for a in range(3):
        own_places = jnp.where(lane == a, column(places_ref[a : a + 1, :]), own_places)
    table[RAW, :, width:] = own_places
    bound = column(bound_ref[...].astype(jnp.float32))
    alive = sub < count_ref[0]
    picks = [(bound == float(i)) & alive for i in range(atoms)]
    for c in range(0, width + 128, 128):
        block = table[RAW, :, c : c + 128]
        packet = jnp.zeros((atoms, 128), jnp.float32)
        for i in range(atoms):
            packet = jnp.where(picks[i], block[i : i + 1, :], packet)
        table[SELF, :, c : c + 128] = packet

    place_z, top = lax.div(gx, 2), nx // 2 - 1
    earlier = lax.div(place_z + top - 1, top) + lax.div(place_z, top)
    pl.semaphore_wait(barrier, len(partners) + earlier + 3 * lax.div(gx, nx - 1))

    def plan(index, source, target, partner, sems=(send_sem, recv_sem), landed=None):
        return pltpu.make_async_remote_copy(
            src_ref=source,
            dst_ref=target,
            send_sem=sems[0].at[index],
            recv_sem=sems[1].at[index if landed is None else landed],
            device_id=partner,
            device_id_type=MESH,
        )

    def copy(*args):
        made = plan(*args)
        made.start()
        return made

    def blocks(ref, start, count=3):
        return ref.at[pl.ds(start, count)]

    direct = [
        plan(12 + n, blocks(table, SELF, 1), blocks(table, FAR + 2 - n, 1), (0, place, gz), landed=5)
        for n, place in three
    ]

    @pl.when(last)
    def _():
        for made in direct:
            made.start()

    sends = []
    to_near = [
        copy(2 + n, blocks(table, SELF, 1), blocks(table, NEAR + n, 1), (near, place, gz))
        for n, place in ((0, up), (1, gy), (2, down))
    ]
    to_side = [
        copy(0, blocks(table, SELF, 1), blocks(table, OWN, 1), (gx, up, gz)),
        copy(1, blocks(table, SELF, 1), blocks(table, OWN + 2, 1), (gx, down, gz)),
    ]

    @pl.when(ahead < gx)
    def _():
        pl.semaphore_signal(ready.at[1], inc=1, device_id=(ahead, gy, gz), device_id_type=MESH)

    @pl.when(behind < gx)
    def _():
        pl.semaphore_signal(ready.at[0], inc=1, device_id=(behind, gy, gz), device_id_type=MESH)

    for made in incoming[len(loads_first) :]:
        made.wait()

    ids = ids_ref[...]
    ghost = jnp.maximum(ids - atoms, 0)
    t = lax.shift_right_logical(ghost, 3)
    one = lambda test: jnp.where(test, 1, 0)
    ox = one(t >= 9) + one(t >= 18) - 1
    rest = t - 9 * (ox + 1)
    oy = one(rest >= 3) + one(rest >= 6) - 1
    oz = rest - 3 * (oy + 1) - 1
    group = jnp.where(ox == 0, 0, jnp.where(ox == sign, 1, 2))
    mapped = 8 * (9 * (oz + 1) + 3 * group + (oy + 1)) + (ghost & 7)
    mapped = jnp.where(ids < atoms, 8 * RAW + ids, mapped)
    rows = 8 * (RAW + 1)
    row_iota = lax.broadcasted_iota(jnp.int32, (atoms, rows), 1)
    hot_f32 = jnp.concatenate(
        [jnp.where(mapped[:, k : k + 1] == row_iota, 1.0, 0.0) for k in range(slots)], axis=0
    )
    hot[...] = hot_f32
    hot_t[...] = hot_f32.T

    for made in to_side:
        made.wait()
    sends.append(copy(6, blocks(table, OWN), blocks(table, 0), (gx, gy, right)))
    sends.append(copy(7, blocks(table, OWN), blocks(table, 18), (gx, gy, left)))
    for made in to_near:
        made.wait()
    ahead_copy = plan(5, blocks(table, NEAR), blocks(table, FAR), (ahead, gy, gz))

    @pl.when(ahead > gx)
    def _():
        pl.semaphore_wait(ready.at[0], 1)

    @pl.when(gx != nx - 2)
    def _():
        ahead_copy.start()

    sends.append(copy(8, blocks(table, NEAR), blocks(table, 3), (gx, gy, right)))
    sends.append(copy(9, blocks(table, NEAR), blocks(table, 21), (gx, gy, left)))
    ahead_copy.wait_recv()
    sends.append(copy(10, blocks(table, FAR), blocks(table, 6), (gx, gy, right)))
    sends.append(copy(11, blocks(table, FAR), blocks(table, 24), (gx, gy, left)))
    for made in sends:
        made.wait()

    @pl.when(gx != nx - 2)
    def _():
        ahead_copy.wait_send()

    @pl.when(last)
    def _():
        for made in direct:
            made.wait_send()


    fsign = sign.astype(jnp.float32)
    unit = [jnp.where(lane == a, EDGE, 0.0) for a in range(3)]
    moved = []
    for z in (-1.0, 0.0, 1.0):
        for g in (0.0, fsign, -fsign):
            for y in (-1.0, 0.0, 1.0):
                moved.append(unit[0] * g + unit[1] * y + unit[2] * z)
    moved.append(jnp.zeros((atoms, 128), jnp.float32))
    positions = jnp.concatenate(
        [table[n, :, width:] + moved[n] for n in range(RAW + 1)], axis=0
    )
    picked = jnp.dot(hot[...], positions, precision=HIGHEST, preferred_element_type=jnp.float32)
    apart = picked.reshape(slots, atoms, 128) - own_places[None]
    distance = jnp.sqrt(jnp.sum(apart * apart, axis=2, keepdims=True) + SOFTENING)
    inverse = 1.0 / distance
    for a in range(3):
        units[a] = jnp.broadcast_to(apart[:, :, a : a + 1] * inverse, (slots, atoms, 128))
    distance = distance.reshape(edges, 1)
    gaussians = first_ref.shape[0]
    centres = FIRST_CENTRE + SPACING * lax.broadcasted_iota(
        jnp.int32, (edges, gaussians), 1
    ).astype(jnp.float32)
    gap = distance - centres
    gauss = jnp.exp(-SHARPNESS * gap * gap)
    pre_one = jnp.dot(
        gauss.astype(jnp.bfloat16), first_ref[...], preferred_element_type=jnp.float32
    )
    gate_one = sigmoid(pre_one)
    hidden_one = (pre_one * gate_one).astype(jnp.bfloat16)
    pre_two = jnp.dot(hidden_one, second_ref[...], preferred_element_type=jnp.float32)
    gate_two = sigmoid(pre_two)
    ncount = column(ncount_ref[...].astype(jnp.float32))
    listed = jnp.concatenate(
        [jnp.where(ncount > float(k), 1.0, 0.0) for k in range(slots)], axis=0
    )
    hidden_two = (pre_two * gate_two * listed).astype(jnp.bfloat16)
    weights[...] = jnp.dot(
        hidden_two, third_ref[...], preferred_element_type=jnp.float32
    ).reshape(slots, atoms, 6 * channels)

    features = table[:, :, 0:width].reshape(rows, width).astype(jnp.bfloat16)
    far[...] = jnp.dot(
        hot[...].astype(jnp.bfloat16), features, preferred_element_type=jnp.float32
    ).reshape(slots, atoms, width)

    step = 2
    scale = slots ** (-0.5)
    quarter = channels ** (-0.25)
    species = column(species_ref[...].astype(jnp.float32))
    energy = jnp.zeros((atoms, 1), jnp.float32)
    cotans = []
    halves = channels // 128

    def loads(ks, h):
        w = [weights[ks, :, n * channels + h * 128 : n * channels + h * 128 + 128] for n in range(6)]
        s = far[ks, :, h * 128 : h * 128 + 128]
        v = [
            far[ks, :, (a + 1) * channels + h * 128 : (a + 1) * channels + h * 128 + 128]
            for a in range(3)
        ]
        u = [units[a, ks] for a in range(3)]
        return w, s, v, u

    def cross(x, y):
        return [
            x[1] * y[2] - x[2] * y[1],
            x[2] * y[0] - x[0] * y[2],
            x[0] * y[1] - x[1] * y[0],
        ]

    def dot3(x, y):
        return x[0] * y[0] + x[1] * y[1] + x[2] * y[2]

    for h in range(halves):
        cut = slice(h * 128, h * 128 + 128)

        def forward(n, carry, h=h):
            ks = pl.ds(n * step, step)
            w, s, v, u = loads(ks, h)
            q = dot3(u, v)
            turned = cross(v, u)
            along = w[2] * s + w[5] * q
            straight = w[3] - w[5] * (1.0 / 3.0)
            out = [carry[0] + jnp.sum(w[0] * s + w[1] * q, axis=0)]
            for a in range(3):
                out.append(
                    carry[1 + a]
                    + jnp.sum(along * u[a] + straight * v[a] + w[4] * turned[a], axis=0)
                )
            return tuple(out)

        zero = jnp.zeros((atoms, 128), jnp.float32)
        sums = lax.fori_loop(0, slots // step, forward, (zero,) * 4)
        s_out = table[RAW, :, cut] + scale * sums[0]
        v_out = [table[RAW, :, (a + 1) * channels + h * 128 : (a + 1) * channels + h * 128 + 128] + scale * sums[1 + a] for a in range(3)]
        coeff = jnp.zeros((atoms, 128), jnp.float32)
        for z in range(energy_table_ref.shape[0]):
            coeff = jnp.where(species == float(z), energy_table_ref[z : z + 1, cut], coeff)
        gains = gains_ref[:, cut]
        gate = sigmoid(s_out)
        part = coeff * (s_out * gate) + gains * dot3(v_out, v_out)
        energy = energy + jnp.sum(part, axis=1, keepdims=True)
        cs = quarter * coeff * (gate * (1.0 + s_out * (1.0 - gate)))
        cv = [(2.0 * quarter) * gains * v for v in v_out]
        cotans.append((cs, cv))
    energy_ref[...] = row_of(energy * quarter)

    for h in range(halves):
        cs, cv = cotans[h]
        gs = (scale * cs)[None]
        gv = [(scale * c)[None] for c in cv]

        def backward(n, carry, h=h, gs=gs, gv=gv):
            ks = pl.ds(n * step, step)
            row = pl.ds(pl.multiple_of(n * step * atoms, step * atoms), step * atoms)
            w, s, v, u = loads(ks, h)
            q = dot3(u, v)
            turned = cross(v, u)
            p = dot3(gv, u)
            same = dot3(gv, v)

            def put(ref, block, value):
                ref[row, block * channels + h * 128 : block * channels + h * 128 + 128] = (
                    value.reshape(step * atoms, 128).astype(jnp.bfloat16)
                )

            put(weight_grads, 0, gs * s)
            put(weight_grads, 1, gs * q)
            put(weight_grads, 2, s * p)
            put(weight_grads, 3, same)
            put(weight_grads, 4, dot3(gv, turned))
            put(weight_grads, 5, p * q - same * (1.0 / 3.0))
            dq = w[1] * gs + w[5] * p
            straight = w[3] - w[5] * (1.0 / 3.0)
            put(edge_grads, 0, w[0] * gs + w[2] * p)
            back = cross(u, gv)
            along = w[2] * s + w[5] * q
            spun = cross(gv, v)
            for a in range(3):
                put(edge_grads, 1 + a, dq * u[a] + straight * gv[a] + w[4] * back[a])
                piece = dq * v[a] + along * gv[a] + w[4] * spun[a]
                if h == 0:
                    turn[a, ks] = piece
                else:
                    turn[a, ks] += piece
            return carry

        lax.fori_loop(0, slots // step, backward, 0)

    summed = jnp.dot(
        hot_t[...].astype(jnp.bfloat16), edge_grads[...], preferred_element_type=jnp.float32
    )
    grads[:, :, 0:width] = summed.reshape(RAW + 1, atoms, width)

    d_two = lax.dot_general(
        weight_grads[...], third_ref[...], NT, preferred_element_type=jnp.float32
    )
    d_two = d_two * listed * (gate_two * (1.0 + pre_two * (1.0 - gate_two)))
    d_one = lax.dot_general(
        d_two.astype(jnp.bfloat16), second_ref[...], NT, preferred_element_type=jnp.float32
    )
    d_one = d_one * (gate_one * (1.0 + pre_one * (1.0 - gate_one)))
    d_gauss = lax.dot_general(
        d_one.astype(jnp.bfloat16), first_ref[...], NT, preferred_element_type=jnp.float32
    )
    d_distance = jnp.sum(
        d_gauss * gauss * gap * (-2.0 * SHARPNESS), axis=1, keepdims=True
    ).reshape(slots, atoms, 1)
    d_unit = [jnp.sum(turn[a], axis=2, keepdims=True) for a in range(3)]
    u = [units[a, :, :, 0:1] for a in range(3)]
    radial = d_distance - dot3(d_unit, u) * inverse
    lanes = lax.broadcasted_iota(jnp.int32, (slots, atoms, 128), 2)
    d_apart = jnp.zeros((slots, atoms, 128), jnp.float32)
    for a in range(3):
        d_apart = jnp.where(lanes == a, d_unit[a] * inverse + radial * u[a], d_apart)
    pulled = jnp.dot(
        hot_t[...],
        d_apart.reshape(edges, 128),
        precision=HIGHEST,
        preferred_element_type=jnp.float32,
    )
    grads[:, :, width:] = pulled.reshape(RAW + 1, atoms, 128)

    back = (back_send, back_recv)
    returns = []
    for g in (2, 1, 0):
        returns.append(
            (
                copy(6 + 2 * g, blocks(grads, 3 * g), blocks(from_z, 3 * g), (gx, gy, left), back),
                copy(
                    7 + 2 * g,
                    blocks(grads, 18 + 3 * g),
                    blocks(from_z, 9 + 3 * g),
                    (gx, gy, right),
                    back,
                ),
            )
        )
    pending = []

    def fold(g):
        for made in returns[2 - g]:
            made.wait()
        total = grads[OWN + 3 * g : OWN + 3 * g + 3]
        return total + from_z[3 * g : 3 * g + 3] + from_z[9 + 3 * g : 12 + 3 * g]

    grads[FAR : FAR + 3] = fold(2)
    far_copy = plan(5, blocks(grads, FAR), blocks(from_x, 0), (behind, gy, gz), back)
    direct_back = [
        plan(12 + n, blocks(grads, FAR + n, 1), blocks(from_w, 2 - n, 1), (0, place, gz), back, 14 - n)
        for n, place in three
    ]

    @pl.when(behind > gx)
    def _():
        pl.semaphore_wait(ready.at[1], 1)

    @pl.when(gx != nx - 1)
    def _():
        far_copy.start()

    @pl.when(last)
    def _():
        for made in direct_back:
            made.start()

    grads[NEAR : NEAR + 3] = fold(1)

    @pl.when(gx != 1)
    def _():
        far_copy.wait_recv()
        grads[NEAR : NEAR + 3] += from_x[...]

    for n, place in ((0, down), (1, gy), (2, up)):
        pending.append(
            copy(
                2 + n,
                blocks(grads, NEAR + n, 1),
                blocks(from_y, 4 - n, 1),
                (near, place, gz),
                back,
            )
        )
    grads[OWN : OWN + 3] = fold(0)
    pending.append(copy(0, blocks(grads, OWN, 1), blocks(from_y, 0, 1), (gx, down, gz), back))
    pending.append(copy(1, blocks(grads, OWN + 2, 1), blocks(from_y, 1, 1), (gx, up, gz), back))
    for made in pending:
        made.wait()

    @pl.when(first)
    def _():
        for made in direct_back:
            made.wait_recv()
        grads[SELF] += from_w[0] + from_w[1] + from_w[2]

    @pl.when(gx != nx - 1)
    def _():
        far_copy.wait_send()

    @pl.when(last)
    def _():
        for made in direct_back:
            made.wait_send()


    def final(c):
        cut = slice(c, c + 128)
        total = grads[SELF, :, cut]
        for n in range(5):
            total = total + from_y[n, :, cut]
        total = jnp.where(alive, total, 0.0)
        back_home = grads[RAW, :, cut]
        for b in range(atoms):
            back_home = back_home + jnp.where(homes[b], total[b : b + 1, :], 0.0)
        return back_home

    homes = [bound_ref[:, b : b + 1] == sub for b in range(atoms)]
    for h in range(halves):
        cs, cv = cotans[h]
        cut = slice(h * 128, h * 128 + 128)
        gscal_ref[:, cut] = final(h * 128) + cs
        for a in range(3):
            gvec_ref[a, :, cut] = final((a + 1) * channels + h * 128) + cv[a]
    pull = jnp.sum(d_apart, axis=0) - final(width)
    for a in range(3):
        forces_ref[a : a + 1, :] = row_of(pull[:, a : a + 1])


def settle(*refs):
    count = len(refs) // 2
    sems = refs[-1]
    made = [
        pltpu.make_async_copy(refs[n], refs[count + n], sems.at[n]) for n in range(count)
    ]
    for m in made:
        m.start()
    for m in made:
        m.wait()


def shards(sizes):
    def run(
        places,
        scalars,
        vectors,
        species,
        bound_rows,
        bound_count,
        neighbour_ids,
        neighbour_count,
        radial_first,
        radial_second,
        radial_third,
        energy_table,
        vector_gains,
    ):
        atoms, channels = scalars.shape
        slots = neighbour_ids.shape[0]
        edges = slots * atoms
        packed = 4 * channels + 128
        vmem = pl.BlockSpec(memory_space=pltpu.VMEM)
        hbm = pl.BlockSpec(memory_space=pl.ANY)
        f32 = jnp.float32
        operands = (
            bound_count,
            places.T,
            scalars,
            vectors.transpose(1, 0, 2),
            species.reshape(1, -1),
            bound_rows.reshape(1, -1),
            neighbour_ids.T,
            neighbour_count.reshape(1, -1),
            radial_first,
            radial_second,
            radial_third,
            energy_table,
            vector_gains.reshape(1, -1),
        )
        landing = [
            pltpu.VMEM(x.shape, x.dtype) for n, x in enumerate(operands) if n not in (0, 2, 3)
        ]
        out_shape = (
            jax.ShapeDtypeStruct((1, atoms), f32),
            jax.ShapeDtypeStruct((3, atoms), f32),
            jax.ShapeDtypeStruct((atoms, channels), f32),
            jax.ShapeDtypeStruct((3, atoms, channels), f32),
        )
        results = pl.pallas_call(
            functools.partial(kernel, sizes),
            out_shape=out_shape,
            in_specs=[pl.BlockSpec(memory_space=pltpu.SMEM)] + [hbm] * 12,
            out_specs=(vmem,) * 4,
            scratch_shapes=landing
            + [
                pltpu.SemaphoreType.DMA((14,)),
                pltpu.VMEM((RAW + 1, atoms, packed), f32),
                pltpu.VMEM((RAW + 1, atoms, packed), f32),
                pltpu.VMEM((18, atoms, packed), f32),
                pltpu.VMEM((3, atoms, packed), f32),
                pltpu.VMEM((3, atoms, packed), f32),
                pltpu.VMEM((5, atoms, packed), f32),
                pltpu.VMEM((edges, 8 * (RAW + 1)), f32),
                pltpu.VMEM((8 * (RAW + 1), edges), f32),
                pltpu.VMEM((slots, atoms, 4 * channels), f32),
                pltpu.VMEM((slots, atoms, 6 * channels), f32),
                pltpu.VMEM((3, slots, atoms, 128), f32),
                pltpu.VMEM((3, slots, atoms, 128), f32),
                pltpu.VMEM((edges, 4 * channels), jnp.bfloat16),
                pltpu.VMEM((edges, 6 * channels), jnp.bfloat16),
                pltpu.SemaphoreType.DMA((15,)),
                pltpu.SemaphoreType.DMA((15,)),
                pltpu.SemaphoreType.DMA((15,)),
                pltpu.SemaphoreType.DMA((15,)),
                pltpu.SemaphoreType.REGULAR((2,)),
            ],
            compiler_params=pltpu.CompilerParams(
                collective_id=0, has_side_effects=True, vmem_limit_bytes=56 * 1024 * 1024
            ),
        )(*operands)
        energies, forces, grad_scalars, grad_vectors = pl.pallas_call(
            settle,
            out_shape=out_shape,
            in_specs=[hbm] * 4,
            out_specs=(hbm,) * 4,
            scratch_shapes=[pltpu.SemaphoreType.DMA((4,))],
            compiler_params=pltpu.CompilerParams(vmem_limit_bytes=56 * 1024 * 1024),
        )(*results)
        return energies.reshape(-1), forces.T, grad_scalars, grad_vectors.transpose(1, 0, 2)

    return run


def solution(mesh):
    spread = ("gx", "gy", "gz")
    in_specs = (
        P(spread, None),
        P(spread, None),
        P(spread, None, None),
        P(spread),
        P(spread),
        P(spread),
        P(None, spread),
        P(spread),
        P(),
        P(),
        P(),
        P(),
        P(),
    )
    out_specs = (P(spread), P(spread, None), P(spread, None), P(spread, None, None))
    sizes = tuple(mesh.shape[axis] for axis in spread)
    return jax.shard_map(
        shards(sizes), mesh=mesh, in_specs=in_specs, out_specs=out_specs, check_vma=False
    )
```

```python
import functools

import jax
import jax.numpy as jnp
from jax import lax
from jax.experimental import pallas as pl
from jax.experimental.pallas import tpu as pltpu
from jax.sharding import PartitionSpec as P

SOFTENING = 0.25
SHARPNESS = 2.0
FIRST_CENTRE = 0.5
SPACING = 0.4
EDGE = 1.0

MESH = pl.DeviceIdType.MESH
HIGHEST = lax.Precision.HIGHEST
NT = (((1,), (1,)), ((), ()))

OWN, NEAR, FAR = 9, 12, 15
SELF = 10
RAW = 27


def sigmoid(x):
    return 1.0 / (1.0 + jnp.exp(-x))


def column(row):
    n = row.shape[1]
    eye = lax.broadcasted_iota(jnp.int32, (n, n), 0) == lax.broadcasted_iota(jnp.int32, (n, n), 1)
    return jnp.sum(jnp.where(eye, jnp.broadcast_to(row, (n, n)), 0.0), axis=1, keepdims=True)


def row_of(col):
    n = col.shape[0]
    eye = lax.broadcasted_iota(jnp.int32, (n, n), 0) == lax.broadcasted_iota(jnp.int32, (n, n), 1)
    return jnp.sum(jnp.where(eye, jnp.broadcast_to(col, (n, n)), 0.0), axis=0, keepdims=True)


def kernel(
    sizes,
    count_ref,
    places_hbm,
    scalars_hbm,
    vectors_hbm,
    species_hbm,
    bound_hbm,
    ids_hbm,
    ncount_hbm,
    first_hbm,
    second_hbm,
    third_hbm,
    energy_table_hbm,
    gains_hbm,
    energy_ref,
    forces_ref,
    gscal_ref,
    gvec_ref,
    places_ref,
    species_ref,
    bound_ref,
    ids_ref,
    ncount_ref,
    first_ref,
    second_ref,
    third_ref,
    energy_table_ref,
    gains_ref,
    load_sem,
    table,
    grads,
    from_z,
    from_x,
    from_w,
    from_y,
    place_table,
    place_grads,
    place_z,
    place_x,
    place_w,
    place_y,
    hot,
    hot_t,
    far,
    weights,
    units,
    turn,
    edge_grads,
    weight_grads,
    send_sem,
    recv_sem,
    back_send,
    back_recv,
    ready,
):
    nx, ny, nz = sizes
    atoms, channels = scalars_hbm.shape
    slots = ids_ref.shape[1]
    edges = slots * atoms
    width = 4 * channels
    gx, gy, gz = lax.axis_index("gx"), lax.axis_index("gy"), lax.axis_index("gz")
    odd = lax.rem(gx, 2)
    sign = 1 - 2 * odd
    near = gx + sign
    ahead = lax.rem(gx + 2 * sign + nx, nx)
    behind = lax.rem(gx - 2 * sign + nx, nx)
    up, down = lax.rem(gy + 1, ny), lax.rem(gy + ny - 1, ny)
    right, left = lax.rem(gz + 1, nz), lax.rem(gz + nz - 1, nz)

    first, last = gx == 0, gx == nx - 1
    three = ((0, down), (1, gy), (2, up))
    barrier = pltpu.get_barrier_semaphore()

    def hello(partner):
        pl.semaphore_signal(barrier, inc=1, device_id=partner, device_id_type=MESH)

    partners = [
        (near, down, gz),
        (near, gy, gz),
        (near, up, gz),
        (gx, down, gz),
        (gx, up, gz),
        (gx, gy, left),
        (gx, gy, right),
    ]
    for partner in partners:
        hello(partner)
    for other in (ahead, behind):

        @pl.when(other > gx)
        def _(other=other):
            hello((other, gy, gz))

    @pl.when(first)
    def _():
        for n, place in three:
            hello((nx - 1, place, gz))

    loads_first = [
        (scalars_hbm, table.at[RAW, :, pl.ds(0, channels)]),
        (vectors_hbm.at[0], table.at[RAW, :, pl.ds(channels, channels)]),
        (vectors_hbm.at[1], table.at[RAW, :, pl.ds(2 * channels, channels)]),
        (vectors_hbm.at[2], table.at[RAW, :, pl.ds(3 * channels, channels)]),
        (places_hbm, places_ref),
        (bound_hbm, bound_ref),
    ]
    loads_later = [
        (ids_hbm, ids_ref),
        (first_hbm, first_ref),
        (second_hbm, second_ref),
        (third_hbm, third_ref),
        (ncount_hbm, ncount_ref),
        (species_hbm, species_ref),
        (energy_table_hbm, energy_table_ref),
        (gains_hbm, gains_ref),
    ]
    incoming = []
    for n, (source, target) in enumerate(loads_first + loads_later):
        made = pltpu.make_async_copy(source, target, load_sem.at[n])
        made.start()
        incoming.append(made)

    for made in incoming[: len(loads_first)]:
        made.wait()
    lane = lax.broadcasted_iota(jnp.int32, (atoms, 128), 1)
    sub = lax.broadcasted_iota(jnp.int32, (atoms, 1), 0)
    own_places = jnp.zeros((atoms, 128), jnp.float32)
    for a in range(3):
        own_places = jnp.where(lane == a, column(places_ref[a : a + 1, :]), own_places)
    place_table[RAW] = own_places
    bound = column(bound_ref[...].astype(jnp.float32))
    alive = sub < count_ref[0]
    picks = [(bound == float(i)) & alive for i in range(atoms)]


    def packed(block):
        packet = jnp.zeros((atoms, 128), jnp.float32)
        for i in range(atoms):
            packet = jnp.where(picks[i], block[i : i + 1, :], packet)
        return packet

    place_table[SELF] = packed(own_places)
    for c in range(0, width, 128):
        table[SELF, :, c : c + 128] = packed(table[RAW, :, c : c + 128])

    level, top = lax.div(gx, 2), nx // 2 - 1
    earlier = lax.div(level + top - 1, top) + lax.div(level, top)
    pl.semaphore_wait(barrier, len(partners) + earlier + 3 * lax.div(gx, nx - 1))

    features = (0, table, grads, from_z, from_x, from_w, from_y)
    positions = (16, place_table, place_grads, place_z, place_x, place_w, place_y)

    def plan(kind, index, source, target, partner, sems=(send_sem, recv_sem), landed=None):
        (source_ref, start, count), (target_ref, place) = source, target
        landed = index if landed is None else landed
        return pltpu.make_async_remote_copy(
            src_ref=kind[source_ref].at[pl.ds(start, count)],
            dst_ref=kind[target_ref].at[pl.ds(place, count)],
            send_sem=sems[0].at[kind[0] + index],
            recv_sem=sems[1].at[kind[0] + landed],
            device_id=partner,
            device_id_type=MESH,
        )

    def copy(*args):
        made = plan(*args)
        made.start()
        return made

    direct = {
        kind[0]: [
            plan(kind, 12 + n, (1, SELF, 1), (1, FAR + 2 - n), (0, place, gz), landed=5)
            for n, place in three
        ]
        for kind in (positions, features)
    }

    @pl.when(last)
    def _():
        for made in direct[16] + direct[0]:
            made.start()

    sends = {0: [], 16: []}
    to_near, to_side = {}, {}
    for kind in (positions, features):
        to_near[kind[0]] = [
            copy(kind, 2 + n, (1, SELF, 1), (1, NEAR + n), (near, place, gz))
            for n, place in ((0, up), (1, gy), (2, down))
        ]
        to_side[kind[0]] = [
            copy(kind, 0, (1, SELF, 1), (1, OWN), (gx, up, gz)),
            copy(kind, 1, (1, SELF, 1), (1, OWN + 2), (gx, down, gz)),
        ]

    @pl.when(ahead < gx)
    def _():
        pl.semaphore_signal(ready.at[1], inc=1, device_id=(ahead, gy, gz), device_id_type=MESH)

    @pl.when(behind < gx)
    def _():
        pl.semaphore_signal(ready.at[0], inc=1, device_id=(behind, gy, gz), device_id_type=MESH)

    for made in incoming[len(loads_first) :]:
        made.wait()

    ids = ids_ref[...]
    ghost = jnp.maximum(ids - atoms, 0)
    t = lax.shift_right_logical(ghost, 3)
    one = lambda test: jnp.where(test, 1, 0)
    ox = one(t >= 9) + one(t >= 18) - 1
    rest = t - 9 * (ox + 1)
    oy = one(rest >= 3) + one(rest >= 6) - 1
    oz = rest - 3 * (oy + 1) - 1
    group = jnp.where(ox == 0, 0, jnp.where(ox == sign, 1, 2))
    mapped = 8 * (9 * (oz + 1) + 3 * group + (oy + 1)) + (ghost & 7)
    mapped = jnp.where(ids < atoms, 8 * RAW + ids, mapped)
    rows = 8 * (RAW + 1)
    row_iota = lax.broadcasted_iota(jnp.int32, (atoms, rows), 1)
    hot_f32 = jnp.concatenate(
        [jnp.where(mapped[:, k : k + 1] == row_iota, 1.0, 0.0) for k in range(slots)], axis=0
    )
    hot[...] = hot_f32
    hot_t[...] = hot_f32.T

    def along_z(kind, g):
        sends[kind[0]] += [
            copy(kind, 6 + 2 * g, (1, OWN + 3 * g, 3), (1, 3 * g), (gx, gy, right)),
            copy(kind, 7 + 2 * g, (1, OWN + 3 * g, 3), (1, 18 + 3 * g), (gx, gy, left)),
        ]

    for kind in (positions, features):
        for made in to_side[kind[0]]:
            made.wait()
        along_z(kind, 0)

    @pl.when(ahead > gx)
    def _():
        pl.semaphore_wait(ready.at[0], 1)

    ahead_copy = {}
    for kind in (positions, features):
        for made in to_near[kind[0]]:
            made.wait()
        ahead_copy[kind[0]] = plan(kind, 5, (1, NEAR, 3), (1, FAR), (ahead, gy, gz))

        @pl.when(gx != nx - 2)
        def _(made=ahead_copy[kind[0]]):
            made.start()

        along_z(kind, 1)
    for kind in (positions, features):
        ahead_copy[kind[0]].wait_recv()
        along_z(kind, 2)
    for made in sends[16]:
        made.wait()

    fsign = sign.astype(jnp.float32)
    unit = [jnp.where(lane == a, EDGE, 0.0) for a in range(3)]
    moved = []
    for z in (-1.0, 0.0, 1.0):
        for g in (0.0, fsign, -fsign):
            for y in (-1.0, 0.0, 1.0):
                moved.append(unit[0] * g + unit[1] * y + unit[2] * z)
    moved.append(jnp.zeros((atoms, 128), jnp.float32))
    spots = jnp.concatenate(
        [place_table[n] + moved[n] for n in range(RAW + 1)], axis=0
    )
    picked = jnp.dot(hot[...], spots, precision=HIGHEST, preferred_element_type=jnp.float32)
    apart = picked.reshape(slots, atoms, 128) - own_places[None]
    distance = jnp.sqrt(jnp.sum(apart * apart, axis=2, keepdims=True) + SOFTENING)
    inverse = 1.0 / distance
    for a in range(3):
        units[a] = jnp.broadcast_to(apart[:, :, a : a + 1] * inverse, (slots, atoms, 128))
    distance = distance.reshape(edges, 1)
    gaussians = first_ref.shape[0]
    centres = FIRST_CENTRE + SPACING * lax.broadcasted_iota(
        jnp.int32, (edges, gaussians), 1
    ).astype(jnp.float32)
    gap = distance - centres
    gauss = jnp.exp(-SHARPNESS * gap * gap)
    pre_one = jnp.dot(
        gauss.astype(jnp.bfloat16), first_ref[...], preferred_element_type=jnp.float32
    )
    gate_one = sigmoid(pre_one)
    hidden_one = (pre_one * gate_one).astype(jnp.bfloat16)
    pre_two = jnp.dot(hidden_one, second_ref[...], preferred_element_type=jnp.float32)
    gate_two = sigmoid(pre_two)
    ncount = column(ncount_ref[...].astype(jnp.float32))
    listed = jnp.concatenate(
        [jnp.where(ncount > float(k), 1.0, 0.0) for k in range(slots)], axis=0
    )
    hidden_two = (pre_two * gate_two * listed).astype(jnp.bfloat16)
    weights[...] = jnp.dot(
        hidden_two, third_ref[...], preferred_element_type=jnp.float32
    ).reshape(slots, atoms, 6 * channels)

    for made in sends[0]:
        made.wait()

    @pl.when(gx != nx - 2)
    def _():
        for kind in (positions, features):
            ahead_copy[kind[0]].wait_send()

    @pl.when(last)
    def _():
        for made in direct[16] + direct[0]:
            made.wait_send()

    table_rows = table[...].reshape(rows, width).astype(jnp.bfloat16)
    far[...] = jnp.dot(
        hot[...].astype(jnp.bfloat16), table_rows, preferred_element_type=jnp.float32
    ).reshape(slots, atoms, width)

    step = 2
    scale = slots ** (-0.5)
    quarter = channels ** (-0.25)
    species = column(species_ref[...].astype(jnp.float32))
    energy = jnp.zeros((atoms, 1), jnp.float32)
    cotans = []
    halves = channels // 128

    def loads(ks, h):
        w = [weights[ks, :, n * channels + h * 128 : n * channels + h * 128 + 128] for n in range(6)]
        s = far[ks, :, h * 128 : h * 128 + 128]
        v = [
            far[ks, :, (a + 1) * channels + h * 128 : (a + 1) * channels + h * 128 + 128]
            for a in range(3)
        ]
        u = [units[a, ks] for a in range(3)]
        return w, s, v, u

    def cross(x, y):
        return [
            x[1] * y[2] - x[2] * y[1],
            x[2] * y[0] - x[0] * y[2],
            x[0] * y[1] - x[1] * y[0],
        ]

    def dot3(x, y):
        return x[0] * y[0] + x[1] * y[1] + x[2] * y[2]

    for h in range(halves):
        cut = slice(h * 128, h * 128 + 128)

        def forward(n, carry, h=h):
            ks = pl.ds(n * step, step)
            w, s, v, u = loads(ks, h)
            q = dot3(u, v)
            turned = cross(v, u)
            along = w[2] * s + w[5] * q
            straight = w[3] - w[5] * (1.0 / 3.0)
            out = [carry[0] + jnp.sum(w[0] * s + w[1] * q, axis=0)]
            for a in range(3):
                out.append(
                    carry[1 + a]
                    + jnp.sum(along * u[a] + straight * v[a] + w[4] * turned[a], axis=0)
                )
            return tuple(out)

        zero = jnp.zeros((atoms, 128), jnp.float32)
        sums = lax.fori_loop(0, slots // step, forward, (zero,) * 4)
        s_out = table[RAW, :, cut] + scale * sums[0]
        v_out = [table[RAW, :, (a + 1) * channels + h * 128 : (a + 1) * channels + h * 128 + 128] + scale * sums[1 + a] for a in range(3)]
        coeff = jnp.zeros((atoms, 128), jnp.float32)
        for z in range(energy_table_ref.shape[0]):
            coeff = jnp.where(species == float(z), energy_table_ref[z : z + 1, cut], coeff)
        gains = gains_ref[:, cut]
        gate = sigmoid(s_out)
        part = coeff * (s_out * gate) + gains * dot3(v_out, v_out)
        energy = energy + jnp.sum(part, axis=1, keepdims=True)
        cs = quarter * coeff * (gate * (1.0 + s_out * (1.0 - gate)))
        cv = [(2.0 * quarter) * gains * v for v in v_out]
        cotans.append((cs, cv))
    energy_ref[...] = row_of(energy * quarter)

    for h in range(halves):
        cs, cv = cotans[h]
        gs = (scale * cs)[None]
        gv = [(scale * c)[None] for c in cv]

        def backward(n, carry, h=h, gs=gs, gv=gv):
            ks = pl.ds(n * step, step)
            row = pl.ds(pl.multiple_of(n * step * atoms, step * atoms), step * atoms)
            w, s, v, u = loads(ks, h)
            q = dot3(u, v)
            turned = cross(v, u)
            p = dot3(gv, u)
            same = dot3(gv, v)

            def put(ref, block, value):
                ref[row, block * channels + h * 128 : block * channels + h * 128 + 128] = (
                    value.reshape(step * atoms, 128).astype(jnp.bfloat16)
                )

            put(weight_grads, 0, gs * s)
            put(weight_grads, 1, gs * q)
            put(weight_grads, 2, s * p)
            put(weight_grads, 3, same)
            put(weight_grads, 4, dot3(gv, turned))
            put(weight_grads, 5, p * q - same * (1.0 / 3.0))
            dq = w[1] * gs + w[5] * p
            straight = w[3] - w[5] * (1.0 / 3.0)
            put(edge_grads, 0, w[0] * gs + w[2] * p)
            back = cross(u, gv)
            along = w[2] * s + w[5] * q
            spun = cross(gv, v)
            for a in range(3):
                put(edge_grads, 1 + a, dq * u[a] + straight * gv[a] + w[4] * back[a])
                piece = dq * v[a] + along * gv[a] + w[4] * spun[a]
                if h == 0:
                    turn[a, ks] = piece
                else:
                    turn[a, ks] += piece
            return carry

        lax.fori_loop(0, slots // step, backward, 0)

    summed = jnp.dot(
        hot_t[...].astype(jnp.bfloat16), edge_grads[...], preferred_element_type=jnp.float32
    )
    grads[...] = summed.reshape(RAW + 1, atoms, width)

    back = (back_send, back_recv)

    def return_z(kind):
        return [
            [
                copy(kind, 6 + 2 * g, (2, 3 * g, 3), (3, 3 * g), (gx, gy, left), back),
                copy(kind, 7 + 2 * g, (2, 18 + 3 * g, 3), (3, 9 + 3 * g), (gx, gy, right), back),
            ]
            for g in (2, 1, 0)
        ]

    returns = {0: return_z(features)}

    d_two = lax.dot_general(
        weight_grads[...], third_ref[...], NT, preferred_element_type=jnp.float32
    )
    d_two = d_two * listed * (gate_two * (1.0 + pre_two * (1.0 - gate_two)))
    d_one = lax.dot_general(
        d_two.astype(jnp.bfloat16), second_ref[...], NT, preferred_element_type=jnp.float32
    )
    d_one = d_one * (gate_one * (1.0 + pre_one * (1.0 - gate_one)))
    d_gauss = lax.dot_general(
        d_one.astype(jnp.bfloat16), first_ref[...], NT, preferred_element_type=jnp.float32
    )
    d_distance = jnp.sum(
        d_gauss * gauss * gap * (-2.0 * SHARPNESS), axis=1, keepdims=True
    ).reshape(slots, atoms, 1)
    d_unit = [jnp.sum(turn[a], axis=2, keepdims=True) for a in range(3)]
    u = [units[a, :, :, 0:1] for a in range(3)]
    radial = d_distance - dot3(d_unit, u) * inverse
    lanes = lax.broadcasted_iota(jnp.int32, (slots, atoms, 128), 2)
    d_apart = jnp.zeros((slots, atoms, 128), jnp.float32)
    for a in range(3):
        d_apart = jnp.where(lanes == a, d_unit[a] * inverse + radial * u[a], d_apart)
    pulled = jnp.dot(
        hot_t[...],
        d_apart.reshape(edges, 128),
        precision=HIGHEST,
        preferred_element_type=jnp.float32,
    )
    place_grads[...] = pulled.reshape(RAW + 1, atoms, 128)
    returns[16] = return_z(positions)

    pending = []

    def fold(kind, g):
        for made in returns[kind[0]][2 - g]:
            made.wait()
        span, came = pl.ds(OWN + 3 * g, 3), kind[3]
        kind[2][span] += came[3 * g : 3 * g + 3] + came[9 + 3 * g : 12 + 3 * g]

    @pl.when(behind > gx)
    def _():
        pl.semaphore_wait(ready.at[1], 1)

    far_copy, direct_back = {}, {}
    for kind in (features, positions):
        fold(kind, 2)
        far_copy[kind[0]] = plan(kind, 5, (2, FAR, 3), (4, 0), (behind, gy, gz), back)
        direct_back[kind[0]] = [
            plan(kind, 12 + n, (2, FAR + n, 1), (5, 2 - n), (0, place, gz), back, 14 - n)
            for n, place in three
        ]

        @pl.when(gx != nx - 1)
        def _(made=far_copy[kind[0]]):
            made.start()

        @pl.when(last)
        def _(several=direct_back[kind[0]]):
            for made in several:
                made.start()

    for kind in (features, positions):
        fold(kind, 0)
        pending.append(copy(kind, 0, (2, OWN, 1), (6, 0), (gx, down, gz), back))
        pending.append(copy(kind, 1, (2, OWN + 2, 1), (6, 1), (gx, up, gz), back))
        fold(kind, 1)
    for kind in (features, positions):
        @pl.when(gx != 1)
        def _(kind=kind):
            far_copy[kind[0]].wait_recv()
            kind[2][NEAR : NEAR + 3] += kind[4][...]

        for n, place in ((0, down), (1, gy), (2, up)):
            pending.append(copy(kind, 2 + n, (2, NEAR + n, 1), (6, 4 - n), (near, place, gz), back))
    for made in pending:
        made.wait()

    @pl.when(first)
    def _():
        for kind in (features, positions):
            for made in direct_back[kind[0]]:
                made.wait_recv()
            kind[2][SELF] += kind[5][0] + kind[5][1] + kind[5][2]

    @pl.when(gx != nx - 1)
    def _():
        for kind in (features, positions):
            far_copy[kind[0]].wait_send()

    @pl.when(last)
    def _():
        for made in direct_back[0] + direct_back[16]:
            made.wait_send()

    def final(kind, c):
        cut = slice(c, c + 128)
        total = kind[2][SELF, :, cut]
        for n in range(5):
            total = total + kind[6][n, :, cut]
        total = jnp.where(alive, total, 0.0)
        back_home = kind[2][RAW, :, cut]
        for b in range(atoms):
            back_home = back_home + jnp.where(homes[b], total[b : b + 1, :], 0.0)
        return back_home

    homes = [bound_ref[:, b : b + 1] == sub for b in range(atoms)]
    for h in range(halves):
        cs, cv = cotans[h]
        cut = slice(h * 128, h * 128 + 128)
        gscal_ref[:, cut] = final(features, h * 128) + cs
        for a in range(3):
            gvec_ref[a, :, cut] = final(features, (a + 1) * channels + h * 128) + cv[a]
    pull = jnp.sum(d_apart, axis=0) - final(positions, 0)
    for a in range(3):
        forces_ref[a : a + 1, :] = row_of(pull[:, a : a + 1])


def settle(*refs):
    for source, target in zip(refs[:4], refs[4:]):
        target[...] = source[...]


def shards(sizes):
    def run(
        places,
        scalars,
        vectors,
        species,
        bound_rows,
        bound_count,
        neighbour_ids,
        neighbour_count,
        radial_first,
        radial_second,
        radial_third,
        energy_table,
        vector_gains,
    ):
        atoms, channels = scalars.shape
        slots = neighbour_ids.shape[0]
        edges = slots * atoms
        packed = 4 * channels
        vmem = pl.BlockSpec(memory_space=pltpu.VMEM)
        hbm = pl.BlockSpec(memory_space=pl.ANY)
        f32 = jnp.float32
        operands = (
            bound_count,
            places.T,
            scalars,
            vectors.transpose(1, 0, 2),
            species.reshape(1, -1),
            bound_rows.reshape(1, -1),
            neighbour_ids.T,
            neighbour_count.reshape(1, -1),
            radial_first,
            radial_second,
            radial_third,
            energy_table,
            vector_gains.reshape(1, -1),
        )
        landing = [
            pltpu.VMEM(x.shape, x.dtype) for n, x in enumerate(operands) if n not in (0, 2, 3)
        ]
        out_shape = (
            jax.ShapeDtypeStruct((1, atoms), f32),
            jax.ShapeDtypeStruct((3, atoms), f32),
            jax.ShapeDtypeStruct((atoms, channels), f32),
            jax.ShapeDtypeStruct((3, atoms, channels), f32),
        )
        results = pl.pallas_call(
            functools.partial(kernel, sizes),
            out_shape=out_shape,
            in_specs=[pl.BlockSpec(memory_space=pltpu.SMEM)] + [hbm] * 12,
            out_specs=(vmem,) * 4,
            scratch_shapes=landing
            + [
                pltpu.SemaphoreType.DMA((14,)),
            ]
            + [
                pltpu.VMEM((count, atoms, row), f32)
                for row in (packed, 128)
                for count in (RAW + 1, RAW + 1, 18, 3, 3, 5)
            ]
            + [
                pltpu.VMEM((edges, 8 * (RAW + 1)), f32),
                pltpu.VMEM((8 * (RAW + 1), edges), f32),
                pltpu.VMEM((slots, atoms, 4 * channels), f32),
                pltpu.VMEM((slots, atoms, 6 * channels), f32),
                pltpu.VMEM((3, slots, atoms, 128), f32),
                pltpu.VMEM((3, slots, atoms, 128), f32),
                pltpu.VMEM((edges, 4 * channels), jnp.bfloat16),
                pltpu.VMEM((edges, 6 * channels), jnp.bfloat16),
                pltpu.SemaphoreType.DMA((31,)),
                pltpu.SemaphoreType.DMA((31,)),
                pltpu.SemaphoreType.DMA((31,)),
                pltpu.SemaphoreType.DMA((31,)),
                pltpu.SemaphoreType.REGULAR((2,)),
            ],
            compiler_params=pltpu.CompilerParams(
                collective_id=0, has_side_effects=True, vmem_limit_bytes=56 * 1024 * 1024
            ),
        )(*operands)
        energies, forces, grad_scalars, grad_vectors = pl.pallas_call(
            settle,
            out_shape=out_shape,
            in_specs=[vmem] * 4,
            out_specs=(vmem,) * 4,
            compiler_params=pltpu.CompilerParams(vmem_limit_bytes=56 * 1024 * 1024),
        )(*results)
        return energies.reshape(-1), forces.T, grad_scalars, grad_vectors.transpose(1, 0, 2)

    return run


def solution(mesh):
    spread = ("gx", "gy", "gz")
    in_specs = (
        P(spread, None),
        P(spread, None),
        P(spread, None, None),
        P(spread),
        P(spread),
        P(spread),
        P(None, spread),
        P(spread),
        P(),
        P(),
        P(),
        P(),
        P(),
    )
    out_specs = (P(spread), P(spread, None), P(spread, None), P(spread, None, None))
    sizes = tuple(mesh.shape[axis] for axis in spread)
    return jax.shard_map(
        shards(sizes), mesh=mesh, in_specs=in_specs, out_specs=out_specs, check_vma=False
    )
```

```python
import functools

import jax
import jax.numpy as jnp
from jax import lax
from jax.experimental import pallas as pl
from jax.experimental.pallas import tpu as pltpu
from jax.sharding import PartitionSpec as P

SOFTENING = 0.25
SHARPNESS = 2.0
FIRST_CENTRE = 0.5
SPACING = 0.4
EDGE = 1.0

MESH = pl.DeviceIdType.MESH
HIGHEST = lax.Precision.HIGHEST
NT = (((1,), (1,)), ((), ()))

OWN, NEAR, FAR = 9, 12, 15
SELF = 10
RAW = 27


def sigmoid(x):
    return 1.0 / (1.0 + jnp.exp(-x))


def column(row):
    n = row.shape[1]
    eye = lax.broadcasted_iota(jnp.int32, (n, n), 0) == lax.broadcasted_iota(jnp.int32, (n, n), 1)
    return jnp.sum(jnp.where(eye, jnp.broadcast_to(row, (n, n)), 0.0), axis=1, keepdims=True)


def row_of(col):
    n = col.shape[0]
    eye = lax.broadcasted_iota(jnp.int32, (n, n), 0) == lax.broadcasted_iota(jnp.int32, (n, n), 1)
    return jnp.sum(jnp.where(eye, jnp.broadcast_to(col, (n, n)), 0.0), axis=0, keepdims=True)


def kernel(
    sizes,
    count_ref,
    places_hbm,
    scalars_hbm,
    vectors_hbm,
    species_hbm,
    bound_hbm,
    ids_hbm,
    ncount_hbm,
    first_hbm,
    second_hbm,
    third_hbm,
    energy_table_hbm,
    gains_hbm,
    energy_ref,
    forces_ref,
    gscal_ref,
    gvec_ref,
    places_ref,
    species_ref,
    bound_ref,
    ids_ref,
    ncount_ref,
    first_ref,
    second_ref,
    third_ref,
    energy_table_ref,
    gains_ref,
    load_sem,
    table,
    grads,
    from_z,
    from_x,
    from_w,
    from_y,
    place_table,
    place_grads,
    place_z,
    place_x,
    place_w,
    place_y,
    hot,
    hot_t,
    far,
    weights,
    units,
    turn,
    edge_grads,
    weight_grads,
    send_sem,
    recv_sem,
    back_send,
    back_recv,
    ready,
):
    nx, ny, nz = sizes
    atoms, channels = scalars_hbm.shape
    slots = ids_ref.shape[1]
    edges = slots * atoms
    width = 4 * channels
    gx, gy, gz = lax.axis_index("gx"), lax.axis_index("gy"), lax.axis_index("gz")
    odd = lax.rem(gx, 2)
    sign = 1 - 2 * odd
    near = gx + sign
    ahead = lax.rem(gx + 2 * sign + nx, nx)
    behind = lax.rem(gx - 2 * sign + nx, nx)
    up, down = lax.rem(gy + 1, ny), lax.rem(gy + ny - 1, ny)
    right, left = lax.rem(gz + 1, nz), lax.rem(gz + nz - 1, nz)

    first, last = gx == 0, gx == nx - 1
    three = ((0, down), (1, gy), (2, up))
    barrier = pltpu.get_barrier_semaphore()

    def hello(partner):
        pl.semaphore_signal(barrier, inc=1, device_id=partner, device_id_type=MESH)

    partners = [
        (near, down, gz),
        (near, gy, gz),
        (near, up, gz),
        (gx, down, gz),
        (gx, up, gz),
        (gx, gy, left),
        (gx, gy, right),
    ]
    for partner in partners:
        hello(partner)
    for other in (ahead, behind):

        @pl.when(other > gx)
        def _(other=other):
            hello((other, gy, gz))

    @pl.when(first)
    def _():
        for n, place in three:
            hello((nx - 1, place, gz))

    loads_first = [
        (scalars_hbm, table.at[RAW, :, pl.ds(0, channels)]),
        (vectors_hbm.at[0], table.at[RAW, :, pl.ds(channels, channels)]),
        (vectors_hbm.at[1], table.at[RAW, :, pl.ds(2 * channels, channels)]),
        (vectors_hbm.at[2], table.at[RAW, :, pl.ds(3 * channels, channels)]),
        (places_hbm, places_ref),
        (bound_hbm, bound_ref),
    ]
    loads_later = [
        (ids_hbm, ids_ref),
        (first_hbm, first_ref),
        (second_hbm, second_ref),
        (third_hbm, third_ref),
        (ncount_hbm, ncount_ref),
        (species_hbm, species_ref),
        (energy_table_hbm, energy_table_ref),
        (gains_hbm, gains_ref),
    ]
    incoming = []
    for n, (source, target) in enumerate(loads_first + loads_later):
        made = pltpu.make_async_copy(source, target, load_sem.at[n])
        made.start()
        incoming.append(made)

    for made in incoming[: len(loads_first)]:
        made.wait()
    lane = lax.broadcasted_iota(jnp.int32, (atoms, 128), 1)
    sub = lax.broadcasted_iota(jnp.int32, (atoms, 1), 0)
    own_places = jnp.zeros((atoms, 128), jnp.float32)
    for a in range(3):
        own_places = jnp.where(lane == a, column(places_ref[a : a + 1, :]), own_places)
    place_table[RAW] = own_places
    bound = column(bound_ref[...].astype(jnp.float32))
    alive = sub < count_ref[0]
    picks = [(bound == float(i)) & alive for i in range(atoms)]


    def packed(block):
        packet = jnp.zeros((atoms, 128), jnp.float32)
        for i in range(atoms):
            packet = jnp.where(picks[i], block[i : i + 1, :], packet)
        return packet

    place_table[SELF] = packed(own_places)
    for c in range(0, width, 128):
        table[SELF, :, c : c + 128] = packed(table[RAW, :, c : c + 128])

    level, top = lax.div(gx, 2), nx // 2 - 1
    earlier = lax.div(level + top - 1, top) + lax.div(level, top)
    pl.semaphore_wait(barrier, len(partners) + earlier + 3 * lax.div(gx, nx - 1))

    features = (0, table, grads, from_z, from_x, from_w, from_y)
    positions = (16, place_table, place_grads, place_z, place_x, place_w, place_y)

    def plan(kind, index, source, target, partner, sems=(send_sem, recv_sem), landed=None):
        (source_ref, start, count), (target_ref, place) = source, target
        landed = index if landed is None else landed
        return pltpu.make_async_remote_copy(
            src_ref=kind[source_ref].at[pl.ds(start, count)],
            dst_ref=kind[target_ref].at[pl.ds(place, count)],
            send_sem=sems[0].at[kind[0] + index],
            recv_sem=sems[1].at[kind[0] + landed],
            device_id=partner,
            device_id_type=MESH,
        )

    def copy(*args):
        made = plan(*args)
        made.start()
        return made

    direct = {
        kind[0]: [
            plan(kind, 12 + n, (1, SELF, 1), (1, FAR + 2 - n), (0, place, gz), landed=5)
            for n, place in three
        ]
        for kind in (positions, features)
    }

    @pl.when(last)
    def _():
        for made in direct[16] + direct[0]:
            made.start()

    sends = {0: [], 16: []}
    to_near, to_side = {}, {}
    for kind in (positions, features):
        to_near[kind[0]] = [
            copy(kind, 2 + n, (1, SELF, 1), (1, NEAR + n), (near, place, gz))
            for n, place in ((0, up), (1, gy), (2, down))
        ]
        to_side[kind[0]] = [
            copy(kind, 0, (1, SELF, 1), (1, OWN), (gx, up, gz)),
            copy(kind, 1, (1, SELF, 1), (1, OWN + 2), (gx, down, gz)),
        ]

    @pl.when(ahead < gx)
    def _():
        pl.semaphore_signal(ready.at[1], inc=1, device_id=(ahead, gy, gz), device_id_type=MESH)

    @pl.when(behind < gx)
    def _():
        pl.semaphore_signal(ready.at[0], inc=1, device_id=(behind, gy, gz), device_id_type=MESH)

    for made in incoming[len(loads_first) :]:
        made.wait()

    ids = ids_ref[...]
    ghost = jnp.maximum(ids - atoms, 0)
    t = lax.shift_right_logical(ghost, 3)
    one = lambda test: jnp.where(test, 1, 0)
    ox = one(t >= 9) + one(t >= 18) - 1
    rest = t - 9 * (ox + 1)
    oy = one(rest >= 3) + one(rest >= 6) - 1
    oz = rest - 3 * (oy + 1) - 1
    group = jnp.where(ox == 0, 0, jnp.where(ox == sign, 1, 2))
    mapped = 8 * (9 * (oz + 1) + 3 * group + (oy + 1)) + (ghost & 7)
    mapped = jnp.where(ids < atoms, 8 * RAW + ids, mapped)
    rows = 8 * (RAW + 1)
    row_iota = lax.broadcasted_iota(jnp.int32, (atoms, rows), 1)
    hot_f32 = jnp.concatenate(
        [jnp.where(mapped[:, k : k + 1] == row_iota, 1.0, 0.0) for k in range(slots)], axis=0
    )
    hot[...] = hot_f32
    hot_t[...] = hot_f32.T

    def along_z(kind, g):
        sends[kind[0]] += [
            copy(kind, 6 + 2 * g, (1, OWN + 3 * g, 3), (1, 3 * g), (gx, gy, right)),
            copy(kind, 7 + 2 * g, (1, OWN + 3 * g, 3), (1, 18 + 3 * g), (gx, gy, left)),
        ]

    for kind in (positions, features):
        for made in to_side[kind[0]]:
            made.wait()
        along_z(kind, 0)

    @pl.when(ahead > gx)
    def _():
        pl.semaphore_wait(ready.at[0], 1)

    ahead_copy = {}
    for kind in (positions, features):
        for made in to_near[kind[0]]:
            made.wait()
        ahead_copy[kind[0]] = plan(kind, 5, (1, NEAR, 3), (1, FAR), (ahead, gy, gz))

        @pl.when(gx != nx - 2)
        def _(made=ahead_copy[kind[0]]):
            made.start()

        along_z(kind, 1)
    for kind in (positions, features):
        ahead_copy[kind[0]].wait_recv()
        along_z(kind, 2)
    for made in sends[16]:
        made.wait()

    fsign = sign.astype(jnp.float32)
    unit = [jnp.where(lane == a, EDGE, 0.0) for a in range(3)]
    moved = []
    for z in (-1.0, 0.0, 1.0):
        for g in (0.0, fsign, -fsign):
            for y in (-1.0, 0.0, 1.0):
                moved.append(unit[0] * g + unit[1] * y + unit[2] * z)
    moved.append(jnp.zeros((atoms, 128), jnp.float32))
    spots = jnp.concatenate(
        [place_table[n] + moved[n] for n in range(RAW + 1)], axis=0
    )
    picked = jnp.dot(hot[...], spots, precision=HIGHEST, preferred_element_type=jnp.float32)
    apart = picked.reshape(slots, atoms, 128) - own_places[None]
    distance = jnp.sqrt(jnp.sum(apart * apart, axis=2, keepdims=True) + SOFTENING)
    inverse = 1.0 / distance
    for a in range(3):
        units[a] = jnp.broadcast_to(apart[:, :, a : a + 1] * inverse, (slots, atoms, 128))
    distance = distance.reshape(edges, 1)
    gaussians = first_ref.shape[0]
    centres = FIRST_CENTRE + SPACING * lax.broadcasted_iota(
        jnp.int32, (edges, gaussians), 1
    ).astype(jnp.float32)
    gap = distance - centres
    gauss = jnp.exp(-SHARPNESS * gap * gap)
    pre_one = jnp.dot(
        gauss.astype(jnp.bfloat16), first_ref[...], preferred_element_type=jnp.float32
    )
    gate_one = sigmoid(pre_one)
    hidden_one = (pre_one * gate_one).astype(jnp.bfloat16)
    pre_two = jnp.dot(hidden_one, second_ref[...], preferred_element_type=jnp.float32)
    gate_two = sigmoid(pre_two)
    ncount = column(ncount_ref[...].astype(jnp.float32))
    listed = jnp.concatenate(
        [jnp.where(ncount > float(k), 1.0, 0.0) for k in range(slots)], axis=0
    )
    hidden_two = (pre_two * gate_two * listed).astype(jnp.bfloat16)
    weights[...] = jnp.dot(
        hidden_two, third_ref[...], preferred_element_type=jnp.float32
    ).reshape(slots, atoms, 6 * channels)

    for made in sends[0]:
        made.wait()

    @pl.when(gx != nx - 2)
    def _():
        for kind in (positions, features):
            ahead_copy[kind[0]].wait_send()

    @pl.when(last)
    def _():
        for made in direct[16] + direct[0]:
            made.wait_send()

    table_rows = table[...].reshape(rows, width).astype(jnp.bfloat16)
    far[...] = jnp.dot(
        hot[...].astype(jnp.bfloat16), table_rows, preferred_element_type=jnp.float32
    ).reshape(slots, atoms, width)

    step = 2
    scale = slots ** (-0.5)
    quarter = channels ** (-0.25)
    species = column(species_ref[...].astype(jnp.float32))
    energy = jnp.zeros((atoms, 1), jnp.float32)
    cotans = []
    halves = channels // 128

    def loads(ks, h):
        w = [weights[ks, :, n * channels + h * 128 : n * channels + h * 128 + 128] for n in range(6)]
        s = far[ks, :, h * 128 : h * 128 + 128]
        v = [
            far[ks, :, (a + 1) * channels + h * 128 : (a + 1) * channels + h * 128 + 128]
            for a in range(3)
        ]
        u = [units[a, ks] for a in range(3)]
        return w, s, v, u

    def cross(x, y):
        return [
            x[1] * y[2] - x[2] * y[1],
            x[2] * y[0] - x[0] * y[2],
            x[0] * y[1] - x[1] * y[0],
        ]

    def dot3(x, y):
        return x[0] * y[0] + x[1] * y[1] + x[2] * y[2]

    for h in range(halves):
        cut = slice(h * 128, h * 128 + 128)

        def forward(n, carry, h=h):
            ks = pl.ds(n * step, step)
            w, s, v, u = loads(ks, h)
            q = dot3(u, v)
            turned = cross(v, u)
            along = w[2] * s + w[5] * q
            straight = w[3] - w[5] * (1.0 / 3.0)
            out = [carry[0] + jnp.sum(w[0] * s + w[1] * q, axis=0)]
            for a in range(3):
                out.append(
                    carry[1 + a]
                    + jnp.sum(along * u[a] + straight * v[a] + w[4] * turned[a], axis=0)
                )
            return tuple(out)

        zero = jnp.zeros((atoms, 128), jnp.float32)
        sums = lax.fori_loop(0, slots // step, forward, (zero,) * 4)
        s_out = table[RAW, :, cut] + scale * sums[0]
        v_out = [table[RAW, :, (a + 1) * channels + h * 128 : (a + 1) * channels + h * 128 + 128] + scale * sums[1 + a] for a in range(3)]
        coeff = jnp.zeros((atoms, 128), jnp.float32)
        for z in range(energy_table_ref.shape[0]):
            coeff = jnp.where(species == float(z), energy_table_ref[z : z + 1, cut], coeff)
        gains = gains_ref[:, cut]
        gate = sigmoid(s_out)
        part = coeff * (s_out * gate) + gains * dot3(v_out, v_out)
        energy = energy + jnp.sum(part, axis=1, keepdims=True)
        cs = quarter * coeff * (gate * (1.0 + s_out * (1.0 - gate)))
        cv = [(2.0 * quarter) * gains * v for v in v_out]
        cotans.append((cs, cv))
    energy_ref[...] = row_of(energy * quarter)

    for h in range(halves):
        cs, cv = cotans[h]
        gs = (scale * cs)[None]
        gv = [(scale * c)[None] for c in cv]

        def backward(n, carry, h=h, gs=gs, gv=gv):
            ks = pl.ds(n * step, step)
            row = pl.ds(pl.multiple_of(n * step * atoms, step * atoms), step * atoms)
            w, s, v, u = loads(ks, h)
            q = dot3(u, v)
            turned = cross(v, u)
            p = dot3(gv, u)
            same = dot3(gv, v)

            def put(ref, block, value):
                ref[row, block * channels + h * 128 : block * channels + h * 128 + 128] = (
                    value.reshape(step * atoms, 128).astype(jnp.bfloat16)
                )

            put(weight_grads, 0, gs * s)
            put(weight_grads, 1, gs * q)
            put(weight_grads, 2, s * p)
            put(weight_grads, 3, same)
            put(weight_grads, 4, dot3(gv, turned))
            put(weight_grads, 5, p * q - same * (1.0 / 3.0))
            dq = w[1] * gs + w[5] * p
            straight = w[3] - w[5] * (1.0 / 3.0)
            put(edge_grads, 0, w[0] * gs + w[2] * p)
            back = cross(u, gv)
            along = w[2] * s + w[5] * q
            spun = cross(gv, v)
            for a in range(3):
                put(edge_grads, 1 + a, dq * u[a] + straight * gv[a] + w[4] * back[a])
                piece = dq * v[a] + along * gv[a] + w[4] * spun[a]
                if h == 0:
                    turn[a, ks] = piece
                else:
                    turn[a, ks] += piece
            return carry

        lax.fori_loop(0, slots // step, backward, 0)

    summed = jnp.dot(
        hot_t[...].astype(jnp.bfloat16), edge_grads[...], preferred_element_type=jnp.float32
    )
    grads[...] = summed.reshape(RAW + 1, atoms, width)

    back = (back_send, back_recv)

    def return_z(kind):
        return [
            [
                copy(kind, 6 + 2 * g, (2, 3 * g, 3), (3, 3 * g), (gx, gy, left), back),
                copy(kind, 7 + 2 * g, (2, 18 + 3 * g, 3), (3, 9 + 3 * g), (gx, gy, right), back),
            ]
            for g in (2, 1, 0)
        ]

    returns = {0: return_z(features)}

    d_two = lax.dot_general(
        weight_grads[...], third_ref[...], NT, preferred_element_type=jnp.float32
    )
    d_two = d_two * listed * (gate_two * (1.0 + pre_two * (1.0 - gate_two)))
    d_one = lax.dot_general(
        d_two.astype(jnp.bfloat16), second_ref[...], NT, preferred_element_type=jnp.float32
    )
    d_one = d_one * (gate_one * (1.0 + pre_one * (1.0 - gate_one)))
    d_gauss = lax.dot_general(
        d_one.astype(jnp.bfloat16), first_ref[...], NT, preferred_element_type=jnp.float32
    )
    d_distance = jnp.sum(
        d_gauss * gauss * gap * (-2.0 * SHARPNESS), axis=1, keepdims=True
    ).reshape(slots, atoms, 1)
    d_unit = [jnp.sum(turn[a], axis=2, keepdims=True) for a in range(3)]
    u = [units[a, :, :, 0:1] for a in range(3)]
    radial = d_distance - dot3(d_unit, u) * inverse
    lanes = lax.broadcasted_iota(jnp.int32, (slots, atoms, 128), 2)
    d_apart = jnp.zeros((slots, atoms, 128), jnp.float32)
    for a in range(3):
        d_apart = jnp.where(lanes == a, d_unit[a] * inverse + radial * u[a], d_apart)
    pulled = jnp.dot(
        hot_t[...],
        d_apart.reshape(edges, 128),
        precision=HIGHEST,
        preferred_element_type=jnp.float32,
    )
    place_grads[...] = pulled.reshape(RAW + 1, atoms, 128)
    returns[16] = return_z(positions)

    pending = []

    def fold(kind, g):
        for made in returns[kind[0]][2 - g]:
            made.wait()
        span, came = pl.ds(OWN + 3 * g, 3), kind[3]
        kind[2][span] += came[3 * g : 3 * g + 3] + came[9 + 3 * g : 12 + 3 * g]

    @pl.when(behind > gx)
    def _():
        pl.semaphore_wait(ready.at[1], 1)

    far_copy, direct_back = {}, {}
    for kind in (features, positions):
        fold(kind, 2)
        far_copy[kind[0]] = plan(kind, 5, (2, FAR, 3), (4, 0), (behind, gy, gz), back)
        direct_back[kind[0]] = [
            plan(kind, 12 + n, (2, FAR + n, 1), (5, 2 - n), (0, place, gz), back, 14 - n)
            for n, place in three
        ]

        @pl.when(gx != nx - 1)
        def _(made=far_copy[kind[0]]):
            made.start()

        @pl.when(last)
        def _(several=direct_back[kind[0]]):
            for made in several:
                made.start()

    for kind in (features, positions):
        fold(kind, 0)
        pending.append(copy(kind, 0, (2, OWN, 1), (6, 0), (gx, down, gz), back))
        pending.append(copy(kind, 1, (2, OWN + 2, 1), (6, 1), (gx, up, gz), back))
        fold(kind, 1)
    for kind in (features, positions):
        @pl.when(gx != 1)
        def _(kind=kind):
            far_copy[kind[0]].wait_recv()
            kind[2][NEAR : NEAR + 3] += kind[4][...]

        for n, place in ((0, down), (1, gy), (2, up)):
            pending.append(copy(kind, 2 + n, (2, NEAR + n, 1), (6, 4 - n), (near, place, gz), back))
    for made in pending:
        made.wait()

    @pl.when(first)
    def _():
        for kind in (features, positions):
            for made in direct_back[kind[0]]:
                made.wait_recv()
            kind[2][SELF] += kind[5][0] + kind[5][1] + kind[5][2]

    @pl.when(gx != nx - 1)
    def _():
        for kind in (features, positions):
            far_copy[kind[0]].wait_send()

    @pl.when(last)
    def _():
        for made in direct_back[0] + direct_back[16]:
            made.wait_send()

    def final(kind, c):
        cut = slice(c, c + 128)
        total = kind[2][SELF, :, cut]
        for n in range(5):
            total = total + kind[6][n, :, cut]
        total = jnp.where(alive, total, 0.0)
        back_home = kind[2][RAW, :, cut]
        for b in range(atoms):
            back_home = back_home + jnp.where(homes[b], total[b : b + 1, :], 0.0)
        return back_home

    homes = [bound_ref[:, b : b + 1] == sub for b in range(atoms)]
    for h in range(halves):
        cs, cv = cotans[h]
        cut = slice(h * 128, h * 128 + 128)
        gscal_ref[:, cut] = final(features, h * 128) + cs
        for a in range(3):
            gvec_ref[a, :, cut] = final(features, (a + 1) * channels + h * 128) + cv[a]
    pull = jnp.sum(d_apart, axis=0) - final(positions, 0)
    for a in range(3):
        forces_ref[a : a + 1, :] = row_of(pull[:, a : a + 1])


def settle(*refs):
    for source, target in zip(refs[:4], refs[4:]):
        target[...] = source[...]


def shards(sizes):
    def run(
        places,
        scalars,
        vectors,
        species,
        bound_rows,
        bound_count,
        neighbour_ids,
        neighbour_count,
        radial_first,
        radial_second,
        radial_third,
        energy_table,
        vector_gains,
    ):
        atoms, channels = scalars.shape
        slots = neighbour_ids.shape[0]
        edges = slots * atoms
        packed = 4 * channels
        vmem = pl.BlockSpec(memory_space=pltpu.VMEM)
        hbm = pl.BlockSpec(memory_space=pl.ANY)
        f32 = jnp.float32
        operands = (
            bound_count,
            places.T,
            scalars,
            vectors.transpose(1, 0, 2),
            species.reshape(1, -1),
            bound_rows.reshape(1, -1),
            neighbour_ids.T,
            neighbour_count.reshape(1, -1),
            radial_first,
            radial_second,
            radial_third,
            energy_table,
            vector_gains.reshape(1, -1),
        )
        landing = [
            pltpu.VMEM(x.shape, x.dtype) for n, x in enumerate(operands) if n not in (0, 2, 3)
        ]
        out_shape = (
            jax.ShapeDtypeStruct((1, atoms), f32),
            jax.ShapeDtypeStruct((3, atoms), f32),
            jax.ShapeDtypeStruct((atoms, channels), f32),
            jax.ShapeDtypeStruct((3, atoms, channels), f32),
        )
        results = pl.pallas_call(
            functools.partial(kernel, sizes),
            out_shape=tuple(pltpu.VMEM(x.shape, x.dtype) for x in out_shape),
            in_specs=[pl.BlockSpec(memory_space=pltpu.SMEM)] + [hbm] * 12,
            out_specs=(vmem,) * 4,
            scratch_shapes=landing
            + [
                pltpu.SemaphoreType.DMA((14,)),
            ]
            + [
                pltpu.VMEM((count, atoms, row), f32)
                for row in (packed, 128)
                for count in (RAW + 1, RAW + 1, 18, 3, 3, 5)
            ]
            + [
                pltpu.VMEM((edges, 8 * (RAW + 1)), f32),
                pltpu.VMEM((8 * (RAW + 1), edges), f32),
                pltpu.VMEM((slots, atoms, 4 * channels), f32),
                pltpu.VMEM((slots, atoms, 6 * channels), f32),
                pltpu.VMEM((3, slots, atoms, 128), f32),
                pltpu.VMEM((3, slots, atoms, 128), f32),
                pltpu.VMEM((edges, 4 * channels), jnp.bfloat16),
                pltpu.VMEM((edges, 6 * channels), jnp.bfloat16),
                pltpu.SemaphoreType.DMA((31,)),
                pltpu.SemaphoreType.DMA((31,)),
                pltpu.SemaphoreType.DMA((31,)),
                pltpu.SemaphoreType.DMA((31,)),
                pltpu.SemaphoreType.REGULAR((2,)),
            ],
            compiler_params=pltpu.CompilerParams(
                collective_id=0, has_side_effects=True, vmem_limit_bytes=56 * 1024 * 1024
            ),
        )(*operands)
        energies, forces, grad_scalars, grad_vectors = pl.pallas_call(
            settle,
            out_shape=out_shape,
            in_specs=[vmem] * 4,
            out_specs=(vmem,) * 4,
            compiler_params=pltpu.CompilerParams(vmem_limit_bytes=1024 * 1024),
        )(*results)
        return energies.reshape(-1), forces.T, grad_scalars, grad_vectors.transpose(1, 0, 2)

    return run


def solution(mesh):
    spread = ("gx", "gy", "gz")
    in_specs = (
        P(spread, None),
        P(spread, None),
        P(spread, None, None),
        P(spread),
        P(spread),
        P(spread),
        P(None, spread),
        P(spread),
        P(),
        P(),
        P(),
        P(),
        P(),
    )
    out_specs = (P(spread), P(spread, None), P(spread, None), P(spread, None, None))
    sizes = tuple(mesh.shape[axis] for axis in spread)
    return jax.shard_map(
        shards(sizes), mesh=mesh, in_specs=in_specs, out_specs=out_specs, check_vma=False
    )
```

```python
import functools

import jax
import jax.numpy as jnp
from jax import lax
from jax.experimental import pallas as pl
from jax.experimental.pallas import tpu as pltpu
from jax.sharding import PartitionSpec as P

SOFTENING = 0.25
SHARPNESS = 2.0
FIRST_CENTRE = 0.5
SPACING = 0.4
EDGE = 1.0

MESH = pl.DeviceIdType.MESH
HIGHEST = lax.Precision.HIGHEST
NT = (((1,), (1,)), ((), ()))

OWN, NEAR, FAR = 9, 12, 15
SELF = 10
RAW = 27


def sigmoid(x):
    return 1.0 / (1.0 + jnp.exp(-x))


def column(row):
    n = row.shape[1]
    eye = lax.broadcasted_iota(jnp.int32, (n, n), 0) == lax.broadcasted_iota(jnp.int32, (n, n), 1)
    return jnp.sum(jnp.where(eye, jnp.broadcast_to(row, (n, n)), 0.0), axis=1, keepdims=True)


def row_of(col):
    n = col.shape[0]
    eye = lax.broadcasted_iota(jnp.int32, (n, n), 0) == lax.broadcasted_iota(jnp.int32, (n, n), 1)
    return jnp.sum(jnp.where(eye, jnp.broadcast_to(col, (n, n)), 0.0), axis=0, keepdims=True)


def kernel(
    sizes,
    count_ref,
    places_hbm,
    scalars_hbm,
    vectors_hbm,
    species_hbm,
    bound_hbm,
    ids_hbm,
    ncount_hbm,
    first_hbm,
    second_hbm,
    third_hbm,
    energy_table_hbm,
    gains_hbm,
    energy_ref,
    forces_ref,
    gscal_ref,
    gvec_ref,
    places_ref,
    species_ref,
    bound_ref,
    ids_ref,
    ncount_ref,
    first_ref,
    second_ref,
    third_ref,
    energy_table_ref,
    gains_ref,
    load_sem,
    table,
    grads,
    from_z,
    from_x,
    from_w,
    from_y,
    place_table,
    place_grads,
    place_z,
    place_x,
    place_w,
    place_y,
    hot,
    hot_t,
    far,
    weights,
    units,
    turn,
    edge_grads,
    weight_grads,
    send_sem,
    recv_sem,
    back_send,
    back_recv,
    ready,
):
    nx, ny, nz = sizes
    atoms, channels = scalars_hbm.shape
    slots = ids_ref.shape[1]
    edges = slots * atoms
    width = 4 * channels
    gx, gy, gz = lax.axis_index("gx"), lax.axis_index("gy"), lax.axis_index("gz")
    odd = lax.rem(gx, 2)
    sign = 1 - 2 * odd
    near = gx + sign
    ahead = lax.rem(gx + 2 * sign + nx, nx)
    behind = lax.rem(gx - 2 * sign + nx, nx)
    up, down = lax.rem(gy + 1, ny), lax.rem(gy + ny - 1, ny)
    right, left = lax.rem(gz + 1, nz), lax.rem(gz + nz - 1, nz)

    first, last = gx == 0, gx == nx - 1
    three = ((0, down), (1, gy), (2, up))
    barrier = pltpu.get_barrier_semaphore()

    def hello(partner):
        pl.semaphore_signal(barrier, inc=1, device_id=partner, device_id_type=MESH)

    near_partners = [(near, down, gz), (near, gy, gz), (near, up, gz)]
    partners = [
        (gx, down, gz),
        (gx, up, gz),
        (gx, gy, left),
        (gx, gy, right),
    ]
    for partner in partners:
        hello(partner)

    @pl.when(gx != nx - 2)
    def _():
        for partner in near_partners:
            hello(partner)

    for other in (ahead, behind):

        @pl.when(other > gx)
        def _(other=other):
            hello((other, gy, gz))

    @pl.when(first)
    def _():
        for n, place in three:
            hello((nx - 1, place, gz))

    loads_first = [
        (scalars_hbm, table.at[RAW, :, pl.ds(0, channels)]),
        (vectors_hbm.at[0], table.at[RAW, :, pl.ds(channels, channels)]),
        (vectors_hbm.at[1], table.at[RAW, :, pl.ds(2 * channels, channels)]),
        (vectors_hbm.at[2], table.at[RAW, :, pl.ds(3 * channels, channels)]),
        (places_hbm, places_ref),
        (bound_hbm, bound_ref),
    ]
    loads_later = [
        (ids_hbm, ids_ref),
        (first_hbm, first_ref),
        (second_hbm, second_ref),
        (third_hbm, third_ref),
        (ncount_hbm, ncount_ref),
        (species_hbm, species_ref),
        (energy_table_hbm, energy_table_ref),
        (gains_hbm, gains_ref),
    ]
    incoming = []
    for n, (source, target) in enumerate(loads_first + loads_later):
        made = pltpu.make_async_copy(source, target, load_sem.at[n])
        made.start()
        incoming.append(made)

    for made in incoming[: len(loads_first)]:
        made.wait()
    lane = lax.broadcasted_iota(jnp.int32, (atoms, 128), 1)
    sub = lax.broadcasted_iota(jnp.int32, (atoms, 1), 0)
    own_places = jnp.zeros((atoms, 128), jnp.float32)
    for a in range(3):
        own_places = jnp.where(lane == a, column(places_ref[a : a + 1, :]), own_places)
    place_table[RAW] = own_places
    bound = column(bound_ref[...].astype(jnp.float32))
    alive = sub < count_ref[0]
    picks = [(bound == float(i)) & alive for i in range(atoms)]


    def packed(block):
        packet = jnp.zeros((atoms, 128), jnp.float32)
        for i in range(atoms):
            packet = jnp.where(picks[i], block[i : i + 1, :], packet)
        return packet

    place_table[SELF] = packed(own_places)
    for c in range(0, width, 128):
        table[SELF, :, c : c + 128] = packed(table[RAW, :, c : c + 128])

    level, top = lax.div(gx, 2), nx // 2 - 1
    earlier = lax.div(level + top - 1, top) + lax.div(level, top)
    pl.semaphore_wait(barrier, len(partners) + 3 + earlier)

    @pl.when(gx == nx - 2)
    def _():
        for partner in near_partners:
            pl.semaphore_signal(ready.at[2], inc=1, device_id=partner, device_id_type=MESH)


    features = (0, table, grads, from_z, from_x, from_w, from_y)
    positions = (16, place_table, place_grads, place_z, place_x, place_w, place_y)

    def plan(kind, index, source, target, partner, sems=(send_sem, recv_sem), landed=None):
        (source_ref, start, count), (target_ref, place) = source, target
        landed = index if landed is None else landed
        return pltpu.make_async_remote_copy(
            src_ref=kind[source_ref].at[pl.ds(start, count)],
            dst_ref=kind[target_ref].at[pl.ds(place, count)],
            send_sem=sems[0].at[kind[0] + index],
            recv_sem=sems[1].at[kind[0] + landed],
            device_id=partner,
            device_id_type=MESH,
        )

    def copy(*args):
        made = plan(*args)
        made.start()
        return made

    direct = {
        kind[0]: [
            plan(kind, 12 + n, (1, SELF, 1), (1, FAR + 2 - n), (0, place, gz), landed=5)
            for n, place in three
        ]
        for kind in (positions, features)
    }

    @pl.when(last)
    def _():
        for made in direct[16] + direct[0]:
            made.start()

    sends = {0: [], 16: []}
    to_near, to_side = {}, {}
    for kind in (positions, features):
        to_side[kind[0]] = [
            copy(kind, 0, (1, SELF, 1), (1, OWN), (gx, up, gz)),
            copy(kind, 1, (1, SELF, 1), (1, OWN + 2), (gx, down, gz)),
        ]

    @pl.when(last)
    def _():
        pl.semaphore_wait(ready.at[2], 3)

    for kind in (positions, features):
        to_near[kind[0]] = [
            copy(kind, 2 + n, (1, SELF, 1), (1, NEAR + n), (near, place, gz))
            for n, place in ((0, up), (1, gy), (2, down))
        ]

    @pl.when(ahead < gx)
    def _():
        pl.semaphore_signal(ready.at[1], inc=1, device_id=(ahead, gy, gz), device_id_type=MESH)

    @pl.when(behind < gx)
    def _():
        pl.semaphore_signal(ready.at[0], inc=1, device_id=(behind, gy, gz), device_id_type=MESH)

    for made in incoming[len(loads_first) :]:
        made.wait()

    ids = ids_ref[...]
    ghost = jnp.maximum(ids - atoms, 0)
    t = lax.shift_right_logical(ghost, 3)
    one = lambda test: jnp.where(test, 1, 0)
    ox = one(t >= 9) + one(t >= 18) - 1
    rest = t - 9 * (ox + 1)
    oy = one(rest >= 3) + one(rest >= 6) - 1
    oz = rest - 3 * (oy + 1) - 1
    group = jnp.where(ox == 0, 0, jnp.where(ox == sign, 1, 2))
    mapped = 8 * (9 * (oz + 1) + 3 * group + (oy + 1)) + (ghost & 7)
    mapped = jnp.where(ids < atoms, 8 * RAW + ids, mapped)
    rows = 8 * (RAW + 1)
    row_iota = lax.broadcasted_iota(jnp.int32, (atoms, rows), 1)
    hot_f32 = jnp.concatenate(
        [jnp.where(mapped[:, k : k + 1] == row_iota, 1.0, 0.0) for k in range(slots)], axis=0
    )
    hot[...] = hot_f32
    hot_t[...] = hot_f32.T

    def along_z(kind, g):
        sends[kind[0]] += [
            copy(kind, 6 + 2 * g, (1, OWN + 3 * g, 3), (1, 3 * g), (gx, gy, right)),
            copy(kind, 7 + 2 * g, (1, OWN + 3 * g, 3), (1, 18 + 3 * g), (gx, gy, left)),
        ]

    for kind in (positions, features):
        for made in to_side[kind[0]]:
            made.wait()
        along_z(kind, 0)

    @pl.when(ahead > gx)
    def _():
        pl.semaphore_wait(ready.at[0], 1)

    ahead_copy = {}
    for kind in (positions, features):
        for made in to_near[kind[0]]:
            made.wait()
        ahead_copy[kind[0]] = plan(kind, 5, (1, NEAR, 3), (1, FAR), (ahead, gy, gz))

        @pl.when(gx != nx - 2)
        def _(made=ahead_copy[kind[0]]):
            made.start()

        along_z(kind, 1)
    for kind in (positions, features):
        ahead_copy[kind[0]].wait_recv()
        along_z(kind, 2)
    for made in sends[16]:
        made.wait()

    fsign = sign.astype(jnp.float32)
    unit = [jnp.where(lane == a, EDGE, 0.0) for a in range(3)]
    moved = []
    for z in (-1.0, 0.0, 1.0):
        for g in (0.0, fsign, -fsign):
            for y in (-1.0, 0.0, 1.0):
                moved.append(unit[0] * g + unit[1] * y + unit[2] * z)
    moved.append(jnp.zeros((atoms, 128), jnp.float32))
    spots = jnp.concatenate(
        [place_table[n] + moved[n] for n in range(RAW + 1)], axis=0
    )
    picked = jnp.dot(hot[...], spots, precision=HIGHEST, preferred_element_type=jnp.float32)
    apart = picked.reshape(slots, atoms, 128) - own_places[None]
    distance = jnp.sqrt(jnp.sum(apart * apart, axis=2, keepdims=True) + SOFTENING)
    inverse = 1.0 / distance
    for a in range(3):
        units[a] = jnp.broadcast_to(apart[:, :, a : a + 1] * inverse, (slots, atoms, 128))
    distance = distance.reshape(edges, 1)
    gaussians = first_ref.shape[0]
    centres = FIRST_CENTRE + SPACING * lax.broadcasted_iota(
        jnp.int32, (edges, gaussians), 1
    ).astype(jnp.float32)
    gap = distance - centres
    gauss = jnp.exp(-SHARPNESS * gap * gap)
    pre_one = jnp.dot(
        gauss.astype(jnp.bfloat16), first_ref[...], preferred_element_type=jnp.float32
    )
    gate_one = sigmoid(pre_one)
    hidden_one = (pre_one * gate_one).astype(jnp.bfloat16)
    pre_two = jnp.dot(hidden_one, second_ref[...], preferred_element_type=jnp.float32)
    gate_two = sigmoid(pre_two)
    ncount = column(ncount_ref[...].astype(jnp.float32))
    listed = jnp.concatenate(
        [jnp.where(ncount > float(k), 1.0, 0.0) for k in range(slots)], axis=0
    )
    hidden_two = (pre_two * gate_two * listed).astype(jnp.bfloat16)
    weights[...] = jnp.dot(
        hidden_two, third_ref[...], preferred_element_type=jnp.float32
    ).reshape(slots, atoms, 6 * channels)

    for made in sends[0]:
        made.wait()

    @pl.when(gx != nx - 2)
    def _():
        for kind in (positions, features):
            ahead_copy[kind[0]].wait_send()

    @pl.when(last)
    def _():
        for made in direct[16] + direct[0]:
            made.wait_send()

    table_rows = table[...].reshape(rows, width).astype(jnp.bfloat16)
    far[...] = jnp.dot(
        hot[...].astype(jnp.bfloat16), table_rows, preferred_element_type=jnp.float32
    ).reshape(slots, atoms, width)

    step = 2
    scale = slots ** (-0.5)
    quarter = channels ** (-0.25)
    species = column(species_ref[...].astype(jnp.float32))
    energy = jnp.zeros((atoms, 1), jnp.float32)
    cotans = []
    halves = channels // 128

    def loads(ks, h):
        w = [weights[ks, :, n * channels + h * 128 : n * channels + h * 128 + 128] for n in range(6)]
        s = far[ks, :, h * 128 : h * 128 + 128]
        v = [
            far[ks, :, (a + 1) * channels + h * 128 : (a + 1) * channels + h * 128 + 128]
            for a in range(3)
        ]
        u = [units[a, ks] for a in range(3)]
        return w, s, v, u

    def cross(x, y):
        return [
            x[1] * y[2] - x[2] * y[1],
            x[2] * y[0] - x[0] * y[2],
            x[0] * y[1] - x[1] * y[0],
        ]

    def dot3(x, y):
        return x[0] * y[0] + x[1] * y[1] + x[2] * y[2]

    for h in range(halves):
        cut = slice(h * 128, h * 128 + 128)

        def forward(n, carry, h=h):
            ks = pl.ds(n * step, step)
            w, s, v, u = loads(ks, h)
            q = dot3(u, v)
            turned = cross(v, u)
            along = w[2] * s + w[5] * q
            straight = w[3] - w[5] * (1.0 / 3.0)
            out = [carry[0] + jnp.sum(w[0] * s + w[1] * q, axis=0)]
            for a in range(3):
                out.append(
                    carry[1 + a]
                    + jnp.sum(along * u[a] + straight * v[a] + w[4] * turned[a], axis=0)
                )
            return tuple(out)

        zero = jnp.zeros((atoms, 128), jnp.float32)
        sums = lax.fori_loop(0, slots // step, forward, (zero,) * 4)
        s_out = table[RAW, :, cut] + scale * sums[0]
        v_out = [table[RAW, :, (a + 1) * channels + h * 128 : (a + 1) * channels + h * 128 + 128] + scale * sums[1 + a] for a in range(3)]
        coeff = jnp.zeros((atoms, 128), jnp.float32)
        for z in range(energy_table_ref.shape[0]):
            coeff = jnp.where(species == float(z), energy_table_ref[z : z + 1, cut], coeff)
        gains = gains_ref[:, cut]
        gate = sigmoid(s_out)
        part = coeff * (s_out * gate) + gains * dot3(v_out, v_out)
        energy = energy + jnp.sum(part, axis=1, keepdims=True)
        cs = quarter * coeff * (gate * (1.0 + s_out * (1.0 - gate)))
        cv = [(2.0 * quarter) * gains * v for v in v_out]
        cotans.append((cs, cv))
    energy_ref[...] = row_of(energy * quarter)

    for h in range(halves):
        cs, cv = cotans[h]
        gs = (scale * cs)[None]
        gv = [(scale * c)[None] for c in cv]

        def backward(n, carry, h=h, gs=gs, gv=gv):
            ks = pl.ds(n * step, step)
            row = pl.ds(pl.multiple_of(n * step * atoms, step * atoms), step * atoms)
            w, s, v, u = loads(ks, h)
            q = dot3(u, v)
            turned = cross(v, u)
            p = dot3(gv, u)
            same = dot3(gv, v)

            def put(ref, block, value):
                ref[row, block * channels + h * 128 : block * channels + h * 128 + 128] = (
                    value.reshape(step * atoms, 128).astype(jnp.bfloat16)
                )

            put(weight_grads, 0, gs * s)
            put(weight_grads, 1, gs * q)
            put(weight_grads, 2, s * p)
            put(weight_grads, 3, same)
            put(weight_grads, 4, dot3(gv, turned))
            put(weight_grads, 5, p * q - same * (1.0 / 3.0))
            dq = w[1] * gs + w[5] * p
            straight = w[3] - w[5] * (1.0 / 3.0)
            put(edge_grads, 0, w[0] * gs + w[2] * p)
            back = cross(u, gv)
            along = w[2] * s + w[5] * q
            spun = cross(gv, v)
            for a in range(3):
                put(edge_grads, 1 + a, dq * u[a] + straight * gv[a] + w[4] * back[a])
                piece = dq * v[a] + along * gv[a] + w[4] * spun[a]
                if h == 0:
                    turn[a, ks] = piece
                else:
                    turn[a, ks] += piece
            return carry

        lax.fori_loop(0, slots // step, backward, 0)

    summed = jnp.dot(
        hot_t[...].astype(jnp.bfloat16), edge_grads[...], preferred_element_type=jnp.float32
    )
    grads[...] = summed.reshape(RAW + 1, atoms, width)

    back = (back_send, back_recv)

    def return_z(kind):
        return [
            [
                copy(kind, 6 + 2 * g, (2, 3 * g, 3), (3, 3 * g), (gx, gy, left), back),
                copy(kind, 7 + 2 * g, (2, 18 + 3 * g, 3), (3, 9 + 3 * g), (gx, gy, right), back),
            ]
            for g in (2, 1, 0)
        ]

    returns = {0: return_z(features)}

    d_two = lax.dot_general(
        weight_grads[...], third_ref[...], NT, preferred_element_type=jnp.float32
    )
    d_two = d_two * listed * (gate_two * (1.0 + pre_two * (1.0 - gate_two)))
    d_one = lax.dot_general(
        d_two.astype(jnp.bfloat16), second_ref[...], NT, preferred_element_type=jnp.float32
    )
    d_one = d_one * (gate_one * (1.0 + pre_one * (1.0 - gate_one)))
    d_gauss = lax.dot_general(
        d_one.astype(jnp.bfloat16), first_ref[...], NT, preferred_element_type=jnp.float32
    )
    d_distance = jnp.sum(
        d_gauss * gauss * gap * (-2.0 * SHARPNESS), axis=1, keepdims=True
    ).reshape(slots, atoms, 1)
    d_unit = [jnp.sum(turn[a], axis=2, keepdims=True) for a in range(3)]
    u = [units[a, :, :, 0:1] for a in range(3)]
    radial = d_distance - dot3(d_unit, u) * inverse
    lanes = lax.broadcasted_iota(jnp.int32, (slots, atoms, 128), 2)
    d_apart = jnp.zeros((slots, atoms, 128), jnp.float32)
    for a in range(3):
        d_apart = jnp.where(lanes == a, d_unit[a] * inverse + radial * u[a], d_apart)
    pulled = jnp.dot(
        hot_t[...],
        d_apart.reshape(edges, 128),
        precision=HIGHEST,
        preferred_element_type=jnp.float32,
    )
    place_grads[...] = pulled.reshape(RAW + 1, atoms, 128)
    returns[16] = return_z(positions)

    pending = []

    def fold(kind, g):
        for made in returns[kind[0]][2 - g]:
            made.wait()
        span, came = pl.ds(OWN + 3 * g, 3), kind[3]
        kind[2][span] += came[3 * g : 3 * g + 3] + came[9 + 3 * g : 12 + 3 * g]

    @pl.when(behind > gx)
    def _():
        pl.semaphore_wait(ready.at[1], 1)

    far_copy, direct_back = {}, {}
    for kind in (features, positions):
        fold(kind, 2)
        far_copy[kind[0]] = plan(kind, 5, (2, FAR, 3), (4, 0), (behind, gy, gz), back)
        direct_back[kind[0]] = [
            plan(kind, 12 + n, (2, FAR + n, 1), (5, 2 - n), (0, place, gz), back, 14 - n)
            for n, place in three
        ]

        @pl.when(gx != nx - 1)
        def _(made=far_copy[kind[0]]):
            made.start()

        @pl.when(last)
        def _(several=direct_back[kind[0]]):
            for made in several:
                made.start()

    for kind in (features, positions):
        fold(kind, 0)
        pending.append(copy(kind, 0, (2, OWN, 1), (6, 0), (gx, down, gz), back))
        pending.append(copy(kind, 1, (2, OWN + 2, 1), (6, 1), (gx, up, gz), back))
        fold(kind, 1)
    for kind in (features, positions):
        @pl.when(gx != 1)
        def _(kind=kind):
            far_copy[kind[0]].wait_recv()
            kind[2][NEAR : NEAR + 3] += kind[4][...]

        for n, place in ((0, down), (1, gy), (2, up)):
            pending.append(copy(kind, 2 + n, (2, NEAR + n, 1), (6, 4 - n), (near, place, gz), back))
    for made in pending:
        made.wait()

    @pl.when(first)
    def _():
        for kind in (features, positions):
            for made in direct_back[kind[0]]:
                made.wait_recv()
            kind[2][SELF] += kind[5][0] + kind[5][1] + kind[5][2]

    @pl.when(gx != nx - 1)
    def _():
        for kind in (features, positions):
            far_copy[kind[0]].wait_send()

    @pl.when(last)
    def _():
        for made in direct_back[0] + direct_back[16]:
            made.wait_send()

    def final(kind, c):
        cut = slice(c, c + 128)
        total = kind[2][SELF, :, cut]
        for n in range(5):
            total = total + kind[6][n, :, cut]
        total = jnp.where(alive, total, 0.0)
        back_home = kind[2][RAW, :, cut]
        for b in range(atoms):
            back_home = back_home + jnp.where(homes[b], total[b : b + 1, :], 0.0)
        return back_home

    homes = [bound_ref[:, b : b + 1] == sub for b in range(atoms)]
    for h in range(halves):
        cs, cv = cotans[h]
        cut = slice(h * 128, h * 128 + 128)
        gscal_ref[:, cut] = final(features, h * 128) + cs
        for a in range(3):
            gvec_ref[a, :, cut] = final(features, (a + 1) * channels + h * 128) + cv[a]
    pull = jnp.sum(d_apart, axis=0) - final(positions, 0)
    for a in range(3):
        forces_ref[a : a + 1, :] = row_of(pull[:, a : a + 1])


def settle(*refs):
    for source, target in zip(refs[:4], refs[4:]):
        target[...] = source[...]


def shards(sizes):
    def run(
        places,
        scalars,
        vectors,
        species,
        bound_rows,
        bound_count,
        neighbour_ids,
        neighbour_count,
        radial_first,
        radial_second,
        radial_third,
        energy_table,
        vector_gains,
    ):
        atoms, channels = scalars.shape
        slots = neighbour_ids.shape[0]
        edges = slots * atoms
        packed = 4 * channels
        vmem = pl.BlockSpec(memory_space=pltpu.VMEM)
        hbm = pl.BlockSpec(memory_space=pl.ANY)
        f32 = jnp.float32
        operands = (
            bound_count,
            places.T,
            scalars,
            vectors.transpose(1, 0, 2),
            species.reshape(1, -1),
            bound_rows.reshape(1, -1),
            neighbour_ids.T,
            neighbour_count.reshape(1, -1),
            radial_first,
            radial_second,
            radial_third,
            energy_table,
            vector_gains.reshape(1, -1),
        )
        landing = [
            pltpu.VMEM(x.shape, x.dtype) for n, x in enumerate(operands) if n not in (0, 2, 3)
        ]
        out_shape = (
            jax.ShapeDtypeStruct((1, atoms), f32),
            jax.ShapeDtypeStruct((3, atoms), f32),
            jax.ShapeDtypeStruct((atoms, channels), f32),
            jax.ShapeDtypeStruct((3, atoms, channels), f32),
        )
        results = pl.pallas_call(
            functools.partial(kernel, sizes),
            out_shape=tuple(pltpu.VMEM(x.shape, x.dtype) for x in out_shape),
            in_specs=[pl.BlockSpec(memory_space=pltpu.SMEM)] + [hbm] * 12,
            out_specs=(vmem,) * 4,
            scratch_shapes=landing
            + [
                pltpu.SemaphoreType.DMA((14,)),
            ]
            + [
                pltpu.VMEM((count, atoms, row), f32)
                for row in (packed, 128)
                for count in (RAW + 1, RAW + 1, 18, 3, 3, 5)
            ]
            + [
                pltpu.VMEM((edges, 8 * (RAW + 1)), f32),
                pltpu.VMEM((8 * (RAW + 1), edges), f32),
                pltpu.VMEM((slots, atoms, 4 * channels), f32),
                pltpu.VMEM((slots, atoms, 6 * channels), f32),
                pltpu.VMEM((3, slots, atoms, 128), f32),
                pltpu.VMEM((3, slots, atoms, 128), f32),
                pltpu.VMEM((edges, 4 * channels), jnp.bfloat16),
                pltpu.VMEM((edges, 6 * channels), jnp.bfloat16),
                pltpu.SemaphoreType.DMA((31,)),
                pltpu.SemaphoreType.DMA((31,)),
                pltpu.SemaphoreType.DMA((31,)),
                pltpu.SemaphoreType.DMA((31,)),
                pltpu.SemaphoreType.REGULAR((3,)),
            ],
            compiler_params=pltpu.CompilerParams(
                collective_id=0, has_side_effects=True, vmem_limit_bytes=56 * 1024 * 1024
            ),
        )(*operands)
        energies, forces, grad_scalars, grad_vectors = pl.pallas_call(
            settle,
            out_shape=out_shape,
            in_specs=[vmem] * 4,
            out_specs=(vmem,) * 4,
            compiler_params=pltpu.CompilerParams(vmem_limit_bytes=1024 * 1024),
        )(*results)
        return energies.reshape(-1), forces.T, grad_scalars, grad_vectors.transpose(1, 0, 2)

    return run


def solution(mesh):
    spread = ("gx", "gy", "gz")
    in_specs = (
        P(spread, None),
        P(spread, None),
        P(spread, None, None),
        P(spread),
        P(spread),
        P(spread),
        P(None, spread),
        P(spread),
        P(),
        P(),
        P(),
        P(),
        P(),
    )
    out_specs = (P(spread), P(spread, None), P(spread, None), P(spread, None, None))
    sizes = tuple(mesh.shape[axis] for axis in spread)
    return jax.shard_map(
        shards(sizes), mesh=mesh, in_specs=in_specs, out_specs=out_specs, check_vma=False
    )
```

```python
import functools

import jax
import jax.numpy as jnp
from jax import lax
from jax.experimental import pallas as pl
from jax.experimental.pallas import tpu as pltpu
from jax.sharding import PartitionSpec as P

SOFTENING = 0.25
SHARPNESS = 2.0
FIRST_CENTRE = 0.5
SPACING = 0.4
EDGE = 1.0

MESH = pl.DeviceIdType.MESH
HIGHEST = lax.Precision.HIGHEST
NT = (((1,), (1,)), ((), ()))

OWN, NEAR, FAR = 9, 12, 15
SELF = 10
RAW = 27


def sigmoid(x):
    return 1.0 / (1.0 + jnp.exp(-x))


def column(row):
    n = row.shape[1]
    eye = lax.broadcasted_iota(jnp.int32, (n, n), 0) == lax.broadcasted_iota(jnp.int32, (n, n), 1)
    return jnp.sum(jnp.where(eye, jnp.broadcast_to(row, (n, n)), 0.0), axis=1, keepdims=True)


def row_of(col):
    n = col.shape[0]
    eye = lax.broadcasted_iota(jnp.int32, (n, n), 0) == lax.broadcasted_iota(jnp.int32, (n, n), 1)
    return jnp.sum(jnp.where(eye, jnp.broadcast_to(col, (n, n)), 0.0), axis=0, keepdims=True)


def kernel(
    sizes,
    count_ref,
    places_hbm,
    scalars_hbm,
    vectors_hbm,
    species_hbm,
    bound_hbm,
    ids_hbm,
    ncount_hbm,
    first_hbm,
    second_hbm,
    third_hbm,
    energy_table_hbm,
    gains_hbm,
    energy_ref,
    forces_ref,
    gscal_ref,
    gvec_ref,
    places_ref,
    species_ref,
    bound_ref,
    ids_ref,
    ncount_ref,
    first_ref,
    second_ref,
    third_ref,
    energy_table_ref,
    gains_ref,
    load_sem,
    table,
    grads,
    from_z,
    from_x,
    from_w,
    from_y,
    place_table,
    place_grads,
    place_z,
    place_x,
    place_w,
    place_y,
    hot,
    hot_t,
    far,
    weights,
    units,
    turn,
    edge_grads,
    weight_grads,
    send_sem,
    recv_sem,
    back_send,
    back_recv,
    ready,
):
    nx, ny, nz = sizes
    atoms, channels = scalars_hbm.shape
    slots = ids_ref.shape[1]
    edges = slots * atoms
    width = 4 * channels
    gx, gy, gz = lax.axis_index("gx"), lax.axis_index("gy"), lax.axis_index("gz")
    odd = lax.rem(gx, 2)
    sign = 1 - 2 * odd
    near = gx + sign
    ahead = lax.rem(gx + 2 * sign + nx, nx)
    behind = lax.rem(gx - 2 * sign + nx, nx)
    up, down = lax.rem(gy + 1, ny), lax.rem(gy + ny - 1, ny)
    right, left = lax.rem(gz + 1, nz), lax.rem(gz + nz - 1, nz)

    first, last = gx == 0, gx == nx - 1
    three = ((1, gy), (0, down), (2, up))
    barrier = pltpu.get_barrier_semaphore()

    def hello(partner):
        pl.semaphore_signal(barrier, inc=1, device_id=partner, device_id_type=MESH)

    near_partners = [(near, down, gz), (near, gy, gz), (near, up, gz)]
    partners = [
        (gx, down, gz),
        (gx, up, gz),
        (gx, gy, left),
        (gx, gy, right),
    ]
    for partner in partners:
        hello(partner)

    @pl.when(gx != nx - 2)
    def _():
        for partner in near_partners:
            hello(partner)

    for other in (ahead, behind):

        @pl.when(other > gx)
        def _(other=other):
            hello((other, gy, gz))

    @pl.when(first)
    def _():
        for n, place in three:
            hello((nx - 1, place, gz))

    loads_first = [
        (scalars_hbm, table.at[RAW, :, pl.ds(0, channels)]),
        (vectors_hbm.at[0], table.at[RAW, :, pl.ds(channels, channels)]),
        (vectors_hbm.at[1], table.at[RAW, :, pl.ds(2 * channels, channels)]),
        (vectors_hbm.at[2], table.at[RAW, :, pl.ds(3 * channels, channels)]),
        (places_hbm, places_ref),
        (bound_hbm, bound_ref),
    ]
    loads_later = [
        (ids_hbm, ids_ref),
        (first_hbm, first_ref),
        (second_hbm, second_ref),
        (third_hbm, third_ref),
        (ncount_hbm, ncount_ref),
        (species_hbm, species_ref),
        (energy_table_hbm, energy_table_ref),
        (gains_hbm, gains_ref),
    ]
    incoming = []
    for n, (source, target) in enumerate(loads_first + loads_later):
        made = pltpu.make_async_copy(source, target, load_sem.at[n])
        made.start()
        incoming.append(made)

    for made in incoming[: len(loads_first)]:
        made.wait()
    lane = lax.broadcasted_iota(jnp.int32, (atoms, 128), 1)
    sub = lax.broadcasted_iota(jnp.int32, (atoms, 1), 0)
    own_places = jnp.zeros((atoms, 128), jnp.float32)
    for a in range(3):
        own_places = jnp.where(lane == a, column(places_ref[a : a + 1, :]), own_places)
    place_table[RAW] = own_places
    bound = column(bound_ref[...].astype(jnp.float32))
    alive = sub < count_ref[0]
    picks = [(bound == float(i)) & alive for i in range(atoms)]


    def packed(block):
        packet = jnp.zeros((atoms, 128), jnp.float32)
        for i in range(atoms):
            packet = jnp.where(picks[i], block[i : i + 1, :], packet)
        return packet

    place_table[SELF] = packed(own_places)
    for c in range(0, width, 128):
        table[SELF, :, c : c + 128] = packed(table[RAW, :, c : c + 128])

    level, top = lax.div(gx, 2), nx // 2 - 1
    earlier = lax.div(level + top - 1, top) + lax.div(level, top)
    pl.semaphore_wait(barrier, len(partners) + 3 + earlier)

    @pl.when(gx == nx - 2)
    def _():
        for partner in near_partners:
            pl.semaphore_signal(ready.at[2], inc=1, device_id=partner, device_id_type=MESH)


    features = (0, table, grads, from_z, from_x, from_w, from_y)
    positions = (16, place_table, place_grads, place_z, place_x, place_w, place_y)

    def plan(kind, index, source, target, partner, sems=(send_sem, recv_sem), landed=None):
        (source_ref, start, count), (target_ref, place) = source, target
        landed = index if landed is None else landed
        return pltpu.make_async_remote_copy(
            src_ref=kind[source_ref].at[pl.ds(start, count)],
            dst_ref=kind[target_ref].at[pl.ds(place, count)],
            send_sem=sems[0].at[kind[0] + index],
            recv_sem=sems[1].at[kind[0] + landed],
            device_id=partner,
            device_id_type=MESH,
        )

    def copy(*args):
        made = plan(*args)
        made.start()
        return made

    direct = {
        kind[0]: [
            plan(kind, 12 + n, (1, SELF, 1), (1, FAR + 2 - n), (0, place, gz), landed=5)
            for n, place in three
        ]
        for kind in (positions, features)
    }

    @pl.when(last)
    def _():
        for made in direct[16] + direct[0]:
            made.start()

    sends = {0: [], 16: []}
    to_near, to_side = {}, {}
    for kind in (positions, features):
        to_side[kind[0]] = [
            copy(kind, 0, (1, SELF, 1), (1, OWN), (gx, up, gz)),
            copy(kind, 1, (1, SELF, 1), (1, OWN + 2), (gx, down, gz)),
        ]

    @pl.when(last)
    def _():
        pl.semaphore_wait(ready.at[2], 3)

    for kind in (positions, features):
        to_near[kind[0]] = [
            copy(kind, 2 + n, (1, SELF, 1), (1, NEAR + n), (near, place, gz))
            for n, place in ((0, up), (1, gy), (2, down))
        ]

    @pl.when(ahead < gx)
    def _():
        pl.semaphore_signal(ready.at[1], inc=1, device_id=(ahead, gy, gz), device_id_type=MESH)

    @pl.when(behind < gx)
    def _():
        pl.semaphore_signal(ready.at[0], inc=1, device_id=(behind, gy, gz), device_id_type=MESH)

    for made in incoming[len(loads_first) :]:
        made.wait()

    ids = ids_ref[...]
    ghost = jnp.maximum(ids - atoms, 0)
    t = lax.shift_right_logical(ghost, 3)
    one = lambda test: jnp.where(test, 1, 0)
    ox = one(t >= 9) + one(t >= 18) - 1
    rest = t - 9 * (ox + 1)
    oy = one(rest >= 3) + one(rest >= 6) - 1
    oz = rest - 3 * (oy + 1) - 1
    group = jnp.where(ox == 0, 0, jnp.where(ox == sign, 1, 2))
    mapped = 8 * (9 * (oz + 1) + 3 * group + (oy + 1)) + (ghost & 7)
    mapped = jnp.where(ids < atoms, 8 * RAW + ids, mapped)
    rows = 8 * (RAW + 1)
    row_iota = lax.broadcasted_iota(jnp.int32, (atoms, rows), 1)
    hot_f32 = jnp.concatenate(
        [jnp.where(mapped[:, k : k + 1] == row_iota, 1.0, 0.0) for k in range(slots)], axis=0
    )
    hot[...] = hot_f32
    hot_t[...] = hot_f32.T

    def along_z(kind, g):
        sends[kind[0]] += [
            copy(kind, 6 + 2 * g, (1, OWN + 3 * g, 3), (1, 3 * g), (gx, gy, right)),
            copy(kind, 7 + 2 * g, (1, OWN + 3 * g, 3), (1, 18 + 3 * g), (gx, gy, left)),
        ]

    for kind in (positions, features):
        for made in to_side[kind[0]]:
            made.wait()
        along_z(kind, 0)

    @pl.when(ahead > gx)
    def _():
        pl.semaphore_wait(ready.at[0], 1)

    ahead_copy = {}
    for kind in (positions, features):
        for made in to_near[kind[0]]:
            made.wait()
        ahead_copy[kind[0]] = plan(kind, 5, (1, NEAR, 3), (1, FAR), (ahead, gy, gz))

        @pl.when(gx != nx - 2)
        def _(made=ahead_copy[kind[0]]):
            made.start()

        along_z(kind, 1)
    for kind in (positions, features):
        ahead_copy[kind[0]].wait_recv()
        along_z(kind, 2)
    for made in sends[16]:
        made.wait()

    fsign = sign.astype(jnp.float32)
    unit = [jnp.where(lane == a, EDGE, 0.0) for a in range(3)]
    moved = []
    for z in (-1.0, 0.0, 1.0):
        for g in (0.0, fsign, -fsign):
            for y in (-1.0, 0.0, 1.0):
                moved.append(unit[0] * g + unit[1] * y + unit[2] * z)
    moved.append(jnp.zeros((atoms, 128), jnp.float32))
    spots = jnp.concatenate(
        [place_table[n] + moved[n] for n in range(RAW + 1)], axis=0
    )
    picked = jnp.dot(hot[...], spots, precision=HIGHEST, preferred_element_type=jnp.float32)
    apart = picked.reshape(slots, atoms, 128) - own_places[None]
    distance = jnp.sqrt(jnp.sum(apart * apart, axis=2, keepdims=True) + SOFTENING)
    inverse = 1.0 / distance
    for a in range(3):
        units[a] = jnp.broadcast_to(apart[:, :, a : a + 1] * inverse, (slots, atoms, 128))
    distance = distance.reshape(edges, 1)
    gaussians = first_ref.shape[0]
    centres = FIRST_CENTRE + SPACING * lax.broadcasted_iota(
        jnp.int32, (edges, gaussians), 1
    ).astype(jnp.float32)
    gap = distance - centres
    gauss = jnp.exp(-SHARPNESS * gap * gap)
    pre_one = jnp.dot(
        gauss.astype(jnp.bfloat16), first_ref[...], preferred_element_type=jnp.float32
    )
    gate_one = sigmoid(pre_one)
    hidden_one = (pre_one * gate_one).astype(jnp.bfloat16)
    pre_two = jnp.dot(hidden_one, second_ref[...], preferred_element_type=jnp.float32)
    gate_two = sigmoid(pre_two)
    ncount = column(ncount_ref[...].astype(jnp.float32))
    listed = jnp.concatenate(
        [jnp.where(ncount > float(k), 1.0, 0.0) for k in range(slots)], axis=0
    )
    hidden_two = (pre_two * gate_two * listed).astype(jnp.bfloat16)
    weights[...] = jnp.dot(
        hidden_two, third_ref[...], preferred_element_type=jnp.float32
    ).reshape(slots, atoms, 6 * channels)

    for made in sends[0]:
        made.wait()

    @pl.when(gx != nx - 2)
    def _():
        for kind in (positions, features):
            ahead_copy[kind[0]].wait_send()

    @pl.when(last)
    def _():
        for made in direct[16] + direct[0]:
            made.wait_send()

    table_rows = table[...].reshape(rows, width).astype(jnp.bfloat16)
    far[...] = jnp.dot(
        hot[...].astype(jnp.bfloat16), table_rows, preferred_element_type=jnp.float32
    ).reshape(slots, atoms, width)

    step = 2
    scale = slots ** (-0.5)
    quarter = channels ** (-0.25)
    species = column(species_ref[...].astype(jnp.float32))
    energy = jnp.zeros((atoms, 1), jnp.float32)
    cotans = []
    halves = channels // 128

    def loads(ks, h):
        w = [weights[ks, :, n * channels + h * 128 : n * channels + h * 128 + 128] for n in range(6)]
        s = far[ks, :, h * 128 : h * 128 + 128]
        v = [
            far[ks, :, (a + 1) * channels + h * 128 : (a + 1) * channels + h * 128 + 128]
            for a in range(3)
        ]
        u = [units[a, ks] for a in range(3)]
        return w, s, v, u

    def cross(x, y):
        return [
            x[1] * y[2] - x[2] * y[1],
            x[2] * y[0] - x[0] * y[2],
            x[0] * y[1] - x[1] * y[0],
        ]

    def dot3(x, y):
        return x[0] * y[0] + x[1] * y[1] + x[2] * y[2]

    for h in range(halves):
        cut = slice(h * 128, h * 128 + 128)

        def forward(n, carry, h=h):
            ks = pl.ds(n * step, step)
            w, s, v, u = loads(ks, h)
            q = dot3(u, v)
            turned = cross(v, u)
            along = w[2] * s + w[5] * q
            straight = w[3] - w[5] * (1.0 / 3.0)
            out = [carry[0] + jnp.sum(w[0] * s + w[1] * q, axis=0)]
            for a in range(3):
                out.append(
                    carry[1 + a]
                    + jnp.sum(along * u[a] + straight * v[a] + w[4] * turned[a], axis=0)
                )
            return tuple(out)

        zero = jnp.zeros((atoms, 128), jnp.float32)
        sums = lax.fori_loop(0, slots // step, forward, (zero,) * 4)
        s_out = table[RAW, :, cut] + scale * sums[0]
        v_out = [table[RAW, :, (a + 1) * channels + h * 128 : (a + 1) * channels + h * 128 + 128] + scale * sums[1 + a] for a in range(3)]
        coeff = jnp.zeros((atoms, 128), jnp.float32)
        for z in range(energy_table_ref.shape[0]):
            coeff = jnp.where(species == float(z), energy_table_ref[z : z + 1, cut], coeff)
        gains = gains_ref[:, cut]
        gate = sigmoid(s_out)
        part = coeff * (s_out * gate) + gains * dot3(v_out, v_out)
        energy = energy + jnp.sum(part, axis=1, keepdims=True)
        cs = quarter * coeff * (gate * (1.0 + s_out * (1.0 - gate)))
        cv = [(2.0 * quarter) * gains * v for v in v_out]
        cotans.append((cs, cv))
    energy_ref[...] = row_of(energy * quarter)

    for h in range(halves):
        cs, cv = cotans[h]
        gs = (scale * cs)[None]
        gv = [(scale * c)[None] for c in cv]

        def backward(n, carry, h=h, gs=gs, gv=gv):
            ks = pl.ds(n * step, step)
            row = pl.ds(pl.multiple_of(n * step * atoms, step * atoms), step * atoms)
            w, s, v, u = loads(ks, h)
            q = dot3(u, v)
            turned = cross(v, u)
            p = dot3(gv, u)
            same = dot3(gv, v)

            def put(ref, block, value):
                ref[row, block * channels + h * 128 : block * channels + h * 128 + 128] = (
                    value.reshape(step * atoms, 128).astype(jnp.bfloat16)
                )

            put(weight_grads, 0, gs * s)
            put(weight_grads, 1, gs * q)
            put(weight_grads, 2, s * p)
            put(weight_grads, 3, same)
            put(weight_grads, 4, dot3(gv, turned))
            put(weight_grads, 5, p * q - same * (1.0 / 3.0))
            dq = w[1] * gs + w[5] * p
            straight = w[3] - w[5] * (1.0 / 3.0)
            put(edge_grads, 0, w[0] * gs + w[2] * p)
            back = cross(u, gv)
            along = w[2] * s + w[5] * q
            spun = cross(gv, v)
            for a in range(3):
                put(edge_grads, 1 + a, dq * u[a] + straight * gv[a] + w[4] * back[a])
                piece = dq * v[a] + along * gv[a] + w[4] * spun[a]
                if h == 0:
                    turn[a, ks] = piece
                else:
                    turn[a, ks] += piece
            return carry

        lax.fori_loop(0, slots // step, backward, 0)

    summed = jnp.dot(
        hot_t[...].astype(jnp.bfloat16), edge_grads[...], preferred_element_type=jnp.float32
    )
    grads[...] = summed.reshape(RAW + 1, atoms, width)

    back = (back_send, back_recv)

    def return_z(kind):
        return [
            [
                copy(kind, 6 + 2 * g, (2, 3 * g, 3), (3, 3 * g), (gx, gy, left), back),
                copy(kind, 7 + 2 * g, (2, 18 + 3 * g, 3), (3, 9 + 3 * g), (gx, gy, right), back),
            ]
            for g in (2, 1, 0)
        ]

    returns = {0: return_z(features)}

    d_two = lax.dot_general(
        weight_grads[...], third_ref[...], NT, preferred_element_type=jnp.float32
    )
    d_two = d_two * listed * (gate_two * (1.0 + pre_two * (1.0 - gate_two)))
    d_one = lax.dot_general(
        d_two.astype(jnp.bfloat16), second_ref[...], NT, preferred_element_type=jnp.float32
    )
    d_one = d_one * (gate_one * (1.0 + pre_one * (1.0 - gate_one)))
    d_gauss = lax.dot_general(
        d_one.astype(jnp.bfloat16), first_ref[...], NT, preferred_element_type=jnp.float32
    )
    d_distance = jnp.sum(
        d_gauss * gauss * gap * (-2.0 * SHARPNESS), axis=1, keepdims=True
    ).reshape(slots, atoms, 1)
    d_unit = [jnp.sum(turn[a], axis=2, keepdims=True) for a in range(3)]
    u = [units[a, :, :, 0:1] for a in range(3)]
    radial = d_distance - dot3(d_unit, u) * inverse
    lanes = lax.broadcasted_iota(jnp.int32, (slots, atoms, 128), 2)
    d_apart = jnp.zeros((slots, atoms, 128), jnp.float32)
    for a in range(3):
        d_apart = jnp.where(lanes == a, d_unit[a] * inverse + radial * u[a], d_apart)
    pulled = jnp.dot(
        hot_t[...],
        d_apart.reshape(edges, 128),
        precision=HIGHEST,
        preferred_element_type=jnp.float32,
    )
    place_grads[...] = pulled.reshape(RAW + 1, atoms, 128)
    returns[16] = return_z(positions)

    pending = []

    def fold(kind, g):
        for made in returns[kind[0]][2 - g]:
            made.wait()
        span, came = pl.ds(OWN + 3 * g, 3), kind[3]
        kind[2][span] += came[3 * g : 3 * g + 3] + came[9 + 3 * g : 12 + 3 * g]

    @pl.when(behind > gx)
    def _():
        pl.semaphore_wait(ready.at[1], 1)

    far_copy, direct_back = {}, {}
    for kind in (features, positions):
        fold(kind, 2)
        far_copy[kind[0]] = plan(kind, 5, (2, FAR, 3), (4, 0), (behind, gy, gz), back)
        direct_back[kind[0]] = [
            plan(kind, 12 + n, (2, FAR + n, 1), (5, 2 - n), (0, place, gz), back, 14 - n)
            for n, place in three
        ]

        @pl.when(gx != nx - 1)
        def _(made=far_copy[kind[0]]):
            made.start()

        @pl.when(last)
        def _(several=direct_back[kind[0]]):
            for made in several:
                made.start()

    for kind in (features, positions):
        fold(kind, 0)
        pending.append(copy(kind, 0, (2, OWN, 1), (6, 0), (gx, down, gz), back))
        pending.append(copy(kind, 1, (2, OWN + 2, 1), (6, 1), (gx, up, gz), back))
        fold(kind, 1)
    for kind in (features, positions):
        @pl.when(gx != 1)
        def _(kind=kind):
            far_copy[kind[0]].wait_recv()
            kind[2][NEAR : NEAR + 3] += kind[4][...]

        for n, place in ((0, down), (1, gy), (2, up)):
            pending.append(copy(kind, 2 + n, (2, NEAR + n, 1), (6, 4 - n), (near, place, gz), back))
    for made in pending:
        made.wait_recv()

    @pl.when(first)
    def _():
        for kind in (features, positions):
            for made in direct_back[kind[0]]:
                made.wait_recv()
            kind[2][SELF] += kind[5][0] + kind[5][1] + kind[5][2]

    def final(kind, c):
        cut = slice(c, c + 128)
        total = kind[2][SELF, :, cut]
        for n in range(5):
            total = total + kind[6][n, :, cut]
        total = jnp.where(alive, total, 0.0)
        back_home = kind[2][RAW, :, cut]
        for b in range(atoms):
            back_home = back_home + jnp.where(homes[b], total[b : b + 1, :], 0.0)
        return back_home

    homes = [bound_ref[:, b : b + 1] == sub for b in range(atoms)]
    for h in range(halves):
        cs, cv = cotans[h]
        cut = slice(h * 128, h * 128 + 128)
        gscal_ref[:, cut] = final(features, h * 128) + cs
        for a in range(3):
            gvec_ref[a, :, cut] = final(features, (a + 1) * channels + h * 128) + cv[a]
    pull = jnp.sum(d_apart, axis=0) - final(positions, 0)
    for a in range(3):
        forces_ref[a : a + 1, :] = row_of(pull[:, a : a + 1])

    for made in pending:
        made.wait_send()

    @pl.when(gx != nx - 1)
    def _():
        for kind in (features, positions):
            far_copy[kind[0]].wait_send()

    @pl.when(last)
    def _():
        for made in direct_back[0] + direct_back[16]:
            made.wait_send()


def settle(*refs):
    for source, target in zip(refs[:4], refs[4:]):
        target[...] = source[...]


def shards(sizes):
    def run(
        places,
        scalars,
        vectors,
        species,
        bound_rows,
        bound_count,
        neighbour_ids,
        neighbour_count,
        radial_first,
        radial_second,
        radial_third,
        energy_table,
        vector_gains,
    ):
        atoms, channels = scalars.shape
        slots = neighbour_ids.shape[0]
        edges = slots * atoms
        packed = 4 * channels
        vmem = pl.BlockSpec(memory_space=pltpu.VMEM)
        hbm = pl.BlockSpec(memory_space=pl.ANY)
        f32 = jnp.float32
        operands = (
            bound_count,
            places.T,
            scalars,
            vectors.transpose(1, 0, 2),
            species.reshape(1, -1),
            bound_rows.reshape(1, -1),
            neighbour_ids.T,
            neighbour_count.reshape(1, -1),
            radial_first,
            radial_second,
            radial_third,
            energy_table,
            vector_gains.reshape(1, -1),
        )
        landing = [
            pltpu.VMEM(x.shape, x.dtype) for n, x in enumerate(operands) if n not in (0, 2, 3)
        ]
        out_shape = (
            jax.ShapeDtypeStruct((1, atoms), f32),
            jax.ShapeDtypeStruct((3, atoms), f32),
            jax.ShapeDtypeStruct((atoms, channels), f32),
            jax.ShapeDtypeStruct((3, atoms, channels), f32),
        )
        results = pl.pallas_call(
            functools.partial(kernel, sizes),
            out_shape=tuple(pltpu.VMEM(x.shape, x.dtype) for x in out_shape),
            in_specs=[pl.BlockSpec(memory_space=pltpu.SMEM)] + [hbm] * 12,
            out_specs=(vmem,) * 4,
            scratch_shapes=landing
            + [
                pltpu.SemaphoreType.DMA((14,)),
            ]
            + [
                pltpu.VMEM((count, atoms, row), f32)
                for row in (packed, 128)
                for count in (RAW + 1, RAW + 1, 18, 3, 3, 5)
            ]
            + [
                pltpu.VMEM((edges, 8 * (RAW + 1)), f32),
                pltpu.VMEM((8 * (RAW + 1), edges), f32),
                pltpu.VMEM((slots, atoms, 4 * channels), f32),
                pltpu.VMEM((slots, atoms, 6 * channels), f32),
                pltpu.VMEM((3, slots, atoms, 128), f32),
                pltpu.VMEM((3, slots, atoms, 128), f32),
                pltpu.VMEM((edges, 4 * channels), jnp.bfloat16),
                pltpu.VMEM((edges, 6 * channels), jnp.bfloat16),
                pltpu.SemaphoreType.DMA((31,)),
                pltpu.SemaphoreType.DMA((31,)),
                pltpu.SemaphoreType.DMA((31,)),
                pltpu.SemaphoreType.DMA((31,)),
                pltpu.SemaphoreType.REGULAR((3,)),
            ],
            compiler_params=pltpu.CompilerParams(
                collective_id=0, has_side_effects=True, vmem_limit_bytes=56 * 1024 * 1024
            ),
        )(*operands)
        energies, forces, grad_scalars, grad_vectors = pl.pallas_call(
            settle,
            out_shape=out_shape,
            in_specs=[vmem] * 4,
            out_specs=(vmem,) * 4,
            compiler_params=pltpu.CompilerParams(vmem_limit_bytes=1024 * 1024),
        )(*results)
        return energies.reshape(-1), forces.T, grad_scalars, grad_vectors.transpose(1, 0, 2)

    return run


def solution(mesh):
    spread = ("gx", "gy", "gz")
    in_specs = (
        P(spread, None),
        P(spread, None),
        P(spread, None, None),
        P(spread),
        P(spread),
        P(spread),
        P(None, spread),
        P(spread),
        P(),
        P(),
        P(),
        P(),
        P(),
    )
    out_specs = (P(spread), P(spread, None), P(spread, None), P(spread, None, None))
    sizes = tuple(mesh.shape[axis] for axis in spread)
    return jax.shard_map(
        shards(sizes), mesh=mesh, in_specs=in_specs, out_specs=out_specs, check_vma=False
    )
```

```python
import functools

import jax
import jax.numpy as jnp
from jax import lax
from jax.experimental import pallas as pl
from jax.experimental.pallas import tpu as pltpu
from jax.sharding import PartitionSpec as P

SOFTENING = 0.25
SHARPNESS = 2.0
FIRST_CENTRE = 0.5
SPACING = 0.4
EDGE = 1.0

MESH = pl.DeviceIdType.MESH
HIGHEST = lax.Precision.HIGHEST
NT = (((1,), (1,)), ((), ()))

OWN, NEAR, FAR = 9, 12, 15
SELF = 10
RAW = 27


def sigmoid(x):
    return 1.0 / (1.0 + jnp.exp(-x))


def column(row):
    n = row.shape[1]
    eye = lax.broadcasted_iota(jnp.int32, (n, n), 0) == lax.broadcasted_iota(jnp.int32, (n, n), 1)
    return jnp.sum(jnp.where(eye, jnp.broadcast_to(row, (n, n)), 0.0), axis=1, keepdims=True)


def row_of(col):
    n = col.shape[0]
    eye = lax.broadcasted_iota(jnp.int32, (n, n), 0) == lax.broadcasted_iota(jnp.int32, (n, n), 1)
    return jnp.sum(jnp.where(eye, jnp.broadcast_to(col, (n, n)), 0.0), axis=0, keepdims=True)


def kernel(
    sizes,
    count_ref,
    places_hbm,
    scalars_hbm,
    vectors_hbm,
    species_hbm,
    bound_hbm,
    ids_hbm,
    ncount_hbm,
    first_hbm,
    second_hbm,
    third_hbm,
    energy_table_hbm,
    gains_hbm,
    energy_ref,
    forces_ref,
    gscal_ref,
    gvec_ref,
    places_ref,
    species_ref,
    bound_ref,
    ids_ref,
    ncount_ref,
    first_ref,
    second_ref,
    third_ref,
    energy_table_ref,
    gains_ref,
    load_sem,
    table,
    grads,
    from_z,
    from_x,
    from_w,
    from_y,
    place_table,
    place_grads,
    place_z,
    place_x,
    place_w,
    place_y,
    hot,
    hot_t,
    far,
    weights,
    units,
    turn,
    edge_grads,
    weight_grads,
    send_sem,
    recv_sem,
    back_send,
    back_recv,
    ready,
):
    nx, ny, nz = sizes
    atoms, channels = scalars_hbm.shape
    slots = ids_ref.shape[1]
    edges = slots * atoms
    width = 4 * channels
    gx, gy, gz = lax.axis_index("gx"), lax.axis_index("gy"), lax.axis_index("gz")
    odd = lax.rem(gx, 2)
    sign = 1 - 2 * odd
    near = gx + sign
    ahead = lax.rem(gx + 2 * sign + nx, nx)
    behind = lax.rem(gx - 2 * sign + nx, nx)
    up, down = lax.rem(gy + 1, ny), lax.rem(gy + ny - 1, ny)
    right, left = lax.rem(gz + 1, nz), lax.rem(gz + nz - 1, nz)

    first, last = gx == 0, gx == nx - 1
    three = ((1, gy), (0, down), (2, up))
    barrier = pltpu.get_barrier_semaphore()

    def hello(partner):
        pl.semaphore_signal(barrier, inc=1, device_id=partner, device_id_type=MESH)

    near_partners = [(near, down, gz), (near, gy, gz), (near, up, gz)]
    partners = [
        (gx, down, gz),
        (gx, up, gz),
        (gx, gy, left),
        (gx, gy, right),
    ]
    for partner in partners:
        hello(partner)

    @pl.when(gx != nx - 2)
    def _():
        for partner in near_partners:
            hello(partner)

    for other in (ahead, behind):

        @pl.when(other > gx)
        def _(other=other):
            hello((other, gy, gz))

    @pl.when(first)
    def _():
        for n, place in three:
            hello((nx - 1, place, gz))

    loads_first = [
        (scalars_hbm, table.at[RAW, :, pl.ds(0, channels)]),
        (vectors_hbm.at[0], table.at[RAW, :, pl.ds(channels, channels)]),
        (vectors_hbm.at[1], table.at[RAW, :, pl.ds(2 * channels, channels)]),
        (vectors_hbm.at[2], table.at[RAW, :, pl.ds(3 * channels, channels)]),
        (places_hbm, places_ref),
        (bound_hbm, bound_ref),
    ]
    loads_later = [
        (ids_hbm, ids_ref),
        (first_hbm, first_ref),
        (second_hbm, second_ref),
        (third_hbm, third_ref),
        (ncount_hbm, ncount_ref),
        (species_hbm, species_ref),
        (energy_table_hbm, energy_table_ref),
        (gains_hbm, gains_ref),
    ]
    incoming = []
    for n, (source, target) in enumerate(loads_first + loads_later):
        made = pltpu.make_async_copy(source, target, load_sem.at[n])
        made.start()
        incoming.append(made)

    for made in incoming[: len(loads_first)]:
        made.wait()
    lane = lax.broadcasted_iota(jnp.int32, (atoms, 128), 1)
    sub = lax.broadcasted_iota(jnp.int32, (atoms, 1), 0)
    own_places = jnp.zeros((atoms, 128), jnp.float32)
    for a in range(3):
        own_places = jnp.where(lane == a, column(places_ref[a : a + 1, :]), own_places)
    place_table[RAW] = own_places
    bound = column(bound_ref[...].astype(jnp.float32))
    alive = sub < count_ref[0]
    picks = [(bound == float(i)) & alive for i in range(atoms)]


    def packed(block):
        packet = jnp.zeros((atoms, 128), jnp.float32)
        for i in range(atoms):
            packet = jnp.where(picks[i], block[i : i + 1, :], packet)
        return packet

    place_table[SELF] = packed(own_places)
    for c in range(0, width, 128):
        table[SELF, :, c : c + 128] = packed(table[RAW, :, c : c + 128])

    level, top = lax.div(gx, 2), nx // 2 - 1
    earlier = lax.div(level + top - 1, top) + lax.div(level, top)
    pl.semaphore_wait(barrier, len(partners) + 3 + earlier)

    @pl.when(gx == nx - 2)
    def _():
        for partner in near_partners:
            pl.semaphore_signal(ready.at[2], inc=1, device_id=partner, device_id_type=MESH)


    features = (0, table, grads, from_z, from_x, from_w, from_y)
    positions = (16, place_table, place_grads, place_z, place_x, place_w, place_y)

    def plan(kind, index, source, target, partner, sems=(send_sem, recv_sem), landed=None):
        (source_ref, start, count), (target_ref, place) = source, target
        landed = index if landed is None else landed
        return pltpu.make_async_remote_copy(
            src_ref=kind[source_ref].at[pl.ds(start, count)],
            dst_ref=kind[target_ref].at[pl.ds(place, count)],
            send_sem=sems[0].at[kind[0] + index],
            recv_sem=sems[1].at[kind[0] + landed],
            device_id=partner,
            device_id_type=MESH,
        )

    def copy(*args):
        made = plan(*args)
        made.start()
        return made

    direct = {
        kind[0]: [
            plan(kind, 12 + n, (1, SELF, 1), (1, FAR + 2 - n), (0, place, gz), landed=5)
            for n, place in three
        ]
        for kind in (positions, features)
    }

    @pl.when(last)
    def _():
        for made in direct[16] + direct[0]:
            made.start()

    sends = {0: [], 16: []}
    to_near, to_side = {}, {}
    for kind in (positions, features):
        to_side[kind[0]] = [
            copy(kind, 0, (1, SELF, 1), (1, OWN), (gx, up, gz)),
            copy(kind, 1, (1, SELF, 1), (1, OWN + 2), (gx, down, gz)),
        ]

    @pl.when(last)
    def _():
        pl.semaphore_wait(ready.at[2], 3)

    for kind in (positions, features):
        to_near[kind[0]] = [
            copy(kind, 2 + n, (1, SELF, 1), (1, NEAR + n), (near, place, gz))
            for n, place in ((0, up), (1, gy), (2, down))
        ]

    @pl.when(ahead < gx)
    def _():
        pl.semaphore_signal(ready.at[1], inc=1, device_id=(ahead, gy, gz), device_id_type=MESH)

    @pl.when(behind < gx)
    def _():
        pl.semaphore_signal(ready.at[0], inc=1, device_id=(behind, gy, gz), device_id_type=MESH)

    for made in incoming[len(loads_first) :]:
        made.wait()

    ids = ids_ref[...]
    ghost = jnp.maximum(ids - atoms, 0)
    t = lax.shift_right_logical(ghost, 3)
    one = lambda test: jnp.where(test, 1, 0)
    ox = one(t >= 9) + one(t >= 18) - 1
    rest = t - 9 * (ox + 1)
    oy = one(rest >= 3) + one(rest >= 6) - 1
    oz = rest - 3 * (oy + 1) - 1
    group = jnp.where(ox == 0, 0, jnp.where(ox == sign, 1, 2))
    mapped = 8 * (9 * (oz + 1) + 3 * group + (oy + 1)) + (ghost & 7)
    mapped = jnp.where(ids < atoms, 8 * RAW + ids, mapped)
    rows = 8 * (RAW + 1)
    row_iota = lax.broadcasted_iota(jnp.int32, (atoms, rows), 1)
    hot_f32 = jnp.concatenate(
        [jnp.where(mapped[:, k : k + 1] == row_iota, 1.0, 0.0) for k in range(slots)], axis=0
    )
    hot[...] = hot_f32
    hot_t[...] = hot_f32.T

    def along_z(kind, g):
        if kind is positions:
            if g == 2:
                sends[kind[0]] += [
                    copy(kind, 10, (1, OWN, 9), (1, 0), (gx, gy, right)),
                    copy(kind, 11, (1, OWN, 9), (1, 18), (gx, gy, left)),
                ]
            return
        sends[kind[0]] += [
            copy(kind, 6 + 2 * g, (1, OWN + 3 * g, 3), (1, 3 * g), (gx, gy, right)),
            copy(kind, 7 + 2 * g, (1, OWN + 3 * g, 3), (1, 18 + 3 * g), (gx, gy, left)),
        ]

    for kind in (positions, features):
        for made in to_side[kind[0]]:
            made.wait()
        along_z(kind, 0)

    @pl.when(ahead > gx)
    def _():
        pl.semaphore_wait(ready.at[0], 1)

    ahead_copy = {}
    for kind in (positions, features):
        for made in to_near[kind[0]]:
            made.wait()
        ahead_copy[kind[0]] = plan(kind, 5, (1, NEAR, 3), (1, FAR), (ahead, gy, gz))

        @pl.when(gx != nx - 2)
        def _(made=ahead_copy[kind[0]]):
            made.start()

        along_z(kind, 1)
    for kind in (positions, features):
        ahead_copy[kind[0]].wait_recv()
        along_z(kind, 2)
    for made in sends[16]:
        made.wait()

    fsign = sign.astype(jnp.float32)
    unit = [jnp.where(lane == a, EDGE, 0.0) for a in range(3)]
    moved = []
    for z in (-1.0, 0.0, 1.0):
        for g in (0.0, fsign, -fsign):
            for y in (-1.0, 0.0, 1.0):
                moved.append(unit[0] * g + unit[1] * y + unit[2] * z)
    moved.append(jnp.zeros((atoms, 128), jnp.float32))
    spots = jnp.concatenate(
        [place_table[n] + moved[n] for n in range(RAW + 1)], axis=0
    )
    picked = jnp.dot(hot[...], spots, precision=HIGHEST, preferred_element_type=jnp.float32)
    apart = picked.reshape(slots, atoms, 128) - own_places[None]
    distance = jnp.sqrt(jnp.sum(apart * apart, axis=2, keepdims=True) + SOFTENING)
    inverse = 1.0 / distance
    for a in range(3):
        units[a] = jnp.broadcast_to(apart[:, :, a : a + 1] * inverse, (slots, atoms, 128))
    distance = distance.reshape(edges, 1)
    gaussians = first_ref.shape[0]
    centres = FIRST_CENTRE + SPACING * lax.broadcasted_iota(
        jnp.int32, (edges, gaussians), 1
    ).astype(jnp.float32)
    gap = distance - centres
    gauss = jnp.exp(-SHARPNESS * gap * gap)
    pre_one = jnp.dot(
        gauss.astype(jnp.bfloat16), first_ref[...], preferred_element_type=jnp.float32
    )
    gate_one = sigmoid(pre_one)
    hidden_one = (pre_one * gate_one).astype(jnp.bfloat16)
    pre_two = jnp.dot(hidden_one, second_ref[...], preferred_element_type=jnp.float32)
    gate_two = sigmoid(pre_two)
    ncount = column(ncount_ref[...].astype(jnp.float32))
    listed = jnp.concatenate(
        [jnp.where(ncount > float(k), 1.0, 0.0) for k in range(slots)], axis=0
    )
    hidden_two = (pre_two * gate_two * listed).astype(jnp.bfloat16)
    weights[...] = jnp.dot(
        hidden_two, third_ref[...], preferred_element_type=jnp.float32
    ).reshape(slots, atoms, 6 * channels)

    for made in sends[0]:
        made.wait()

    @pl.when(gx != nx - 2)
    def _():
        for kind in (positions, features):
            ahead_copy[kind[0]].wait_send()

    @pl.when(last)
    def _():
        for made in direct[16] + direct[0]:
            made.wait_send()

    table_rows = table[...].reshape(rows, width).astype(jnp.bfloat16)
    far[...] = jnp.dot(
        hot[...].astype(jnp.bfloat16), table_rows, preferred_element_type=jnp.float32
    ).reshape(slots, atoms, width)

    step = 2
    scale = slots ** (-0.5)
    quarter = channels ** (-0.25)
    species = column(species_ref[...].astype(jnp.float32))
    energy = jnp.zeros((atoms, 1), jnp.float32)
    cotans = []
    halves = channels // 128

    def loads(ks, h):
        w = [weights[ks, :, n * channels + h * 128 : n * channels + h * 128 + 128] for n in range(6)]
        s = far[ks, :, h * 128 : h * 128 + 128]
        v = [
            far[ks, :, (a + 1) * channels + h * 128 : (a + 1) * channels + h * 128 + 128]
            for a in range(3)
        ]
        u = [units[a, ks] for a in range(3)]
        return w, s, v, u

    def cross(x, y):
        return [
            x[1] * y[2] - x[2] * y[1],
            x[2] * y[0] - x[0] * y[2],
            x[0] * y[1] - x[1] * y[0],
        ]

    def dot3(x, y):
        return x[0] * y[0] + x[1] * y[1] + x[2] * y[2]

    for h in range(halves):
        cut = slice(h * 128, h * 128 + 128)

        def forward(n, carry, h=h):
            ks = pl.ds(n * step, step)
            w, s, v, u = loads(ks, h)
            q = dot3(u, v)
            turned = cross(v, u)
            along = w[2] * s + w[5] * q
            straight = w[3] - w[5] * (1.0 / 3.0)
            out = [carry[0] + jnp.sum(w[0] * s + w[1] * q, axis=0)]
            for a in range(3):
                out.append(
                    carry[1 + a]
                    + jnp.sum(along * u[a] + straight * v[a] + w[4] * turned[a], axis=0)
                )
            return tuple(out)

        zero = jnp.zeros((atoms, 128), jnp.float32)
        sums = lax.fori_loop(0, slots // step, forward, (zero,) * 4)
        s_out = table[RAW, :, cut] + scale * sums[0]
        v_out = [table[RAW, :, (a + 1) * channels + h * 128 : (a + 1) * channels + h * 128 + 128] + scale * sums[1 + a] for a in range(3)]
        coeff = jnp.zeros((atoms, 128), jnp.float32)
        for z in range(energy_table_ref.shape[0]):
            coeff = jnp.where(species == float(z), energy_table_ref[z : z + 1, cut], coeff)
        gains = gains_ref[:, cut]
        gate = sigmoid(s_out)
        part = coeff * (s_out * gate) + gains * dot3(v_out, v_out)
        energy = energy + jnp.sum(part, axis=1, keepdims=True)
        cs = quarter * coeff * (gate * (1.0 + s_out * (1.0 - gate)))
        cv = [(2.0 * quarter) * gains * v for v in v_out]
        cotans.append((cs, cv))
    energy_ref[...] = row_of(energy * quarter)

    for h in range(halves):
        cs, cv = cotans[h]
        gs = (scale * cs)[None]
        gv = [(scale * c)[None] for c in cv]

        def backward(n, carry, h=h, gs=gs, gv=gv):
            ks = pl.ds(n * step, step)
            row = pl.ds(pl.multiple_of(n * step * atoms, step * atoms), step * atoms)
            w, s, v, u = loads(ks, h)
            q = dot3(u, v)
            turned = cross(v, u)
            p = dot3(gv, u)
            same = dot3(gv, v)

            def put(ref, block, value):
                ref[row, block * channels + h * 128 : block * channels + h * 128 + 128] = (
                    value.reshape(step * atoms, 128).astype(jnp.bfloat16)
                )

            put(weight_grads, 0, gs * s)
            put(weight_grads, 1, gs * q)
            put(weight_grads, 2, s * p)
            put(weight_grads, 3, same)
            put(weight_grads, 4, dot3(gv, turned))
            put(weight_grads, 5, p * q - same * (1.0 / 3.0))
            dq = w[1] * gs + w[5] * p
            straight = w[3] - w[5] * (1.0 / 3.0)
            put(edge_grads, 0, w[0] * gs + w[2] * p)
            back = cross(u, gv)
            along = w[2] * s + w[5] * q
            spun = cross(gv, v)
            for a in range(3):
                put(edge_grads, 1 + a, dq * u[a] + straight * gv[a] + w[4] * back[a])
                piece = dq * v[a] + along * gv[a] + w[4] * spun[a]
                if h == 0:
                    turn[a, ks] = piece
                else:
                    turn[a, ks] += piece
            return carry

        lax.fori_loop(0, slots // step, backward, 0)

    summed = jnp.dot(
        hot_t[...].astype(jnp.bfloat16), edge_grads[...], preferred_element_type=jnp.float32
    )
    grads[...] = summed.reshape(RAW + 1, atoms, width)

    back = (back_send, back_recv)

    def return_z(kind):
        return [
            [
                copy(kind, 6 + 2 * g, (2, 3 * g, 3), (3, 3 * g), (gx, gy, left), back),
                copy(kind, 7 + 2 * g, (2, 18 + 3 * g, 3), (3, 9 + 3 * g), (gx, gy, right), back),
            ]
            for g in (2, 1, 0)
        ]

    returns = {0: return_z(features)}

    d_two = lax.dot_general(
        weight_grads[...], third_ref[...], NT, preferred_element_type=jnp.float32
    )
    d_two = d_two * listed * (gate_two * (1.0 + pre_two * (1.0 - gate_two)))
    d_one = lax.dot_general(
        d_two.astype(jnp.bfloat16), second_ref[...], NT, preferred_element_type=jnp.float32
    )
    d_one = d_one * (gate_one * (1.0 + pre_one * (1.0 - gate_one)))
    d_gauss = lax.dot_general(
        d_one.astype(jnp.bfloat16), first_ref[...], NT, preferred_element_type=jnp.float32
    )
    d_distance = jnp.sum(
        d_gauss * gauss * gap * (-2.0 * SHARPNESS), axis=1, keepdims=True
    ).reshape(slots, atoms, 1)
    d_unit = [jnp.sum(turn[a], axis=2, keepdims=True) for a in range(3)]
    u = [units[a, :, :, 0:1] for a in range(3)]
    radial = d_distance - dot3(d_unit, u) * inverse
    lanes = lax.broadcasted_iota(jnp.int32, (slots, atoms, 128), 2)
    d_apart = jnp.zeros((slots, atoms, 128), jnp.float32)
    for a in range(3):
        d_apart = jnp.where(lanes == a, d_unit[a] * inverse + radial * u[a], d_apart)
    pulled = jnp.dot(
        hot_t[...],
        d_apart.reshape(edges, 128),
        precision=HIGHEST,
        preferred_element_type=jnp.float32,
    )
    place_grads[...] = pulled.reshape(RAW + 1, atoms, 128)
    returns[16] = return_z(positions)

    pending = []

    def fold(kind, g):
        for made in returns[kind[0]][2 - g]:
            made.wait()
        span, came = pl.ds(OWN + 3 * g, 3), kind[3]
        kind[2][span] += came[3 * g : 3 * g + 3] + came[9 + 3 * g : 12 + 3 * g]

    @pl.when(behind > gx)
    def _():
        pl.semaphore_wait(ready.at[1], 1)

    far_copy, direct_back = {}, {}
    for kind in (features, positions):
        fold(kind, 2)
        far_copy[kind[0]] = plan(kind, 5, (2, FAR, 3), (4, 0), (behind, gy, gz), back)
        direct_back[kind[0]] = [
            plan(kind, 12 + n, (2, FAR + n, 1), (5, 2 - n), (0, place, gz), back, 14 - n)
            for n, place in three
        ]

        @pl.when(gx != nx - 1)
        def _(made=far_copy[kind[0]]):
            made.start()

        @pl.when(last)
        def _(several=direct_back[kind[0]]):
            for made in several:
                made.start()

    for kind in (features, positions):
        fold(kind, 0)
        pending.append(copy(kind, 0, (2, OWN, 1), (6, 0), (gx, down, gz), back))
        pending.append(copy(kind, 1, (2, OWN + 2, 1), (6, 1), (gx, up, gz), back))
        fold(kind, 1)
    for kind in (features, positions):
        @pl.when(gx != 1)
        def _(kind=kind):
            far_copy[kind[0]].wait_recv()
            kind[2][NEAR : NEAR + 3] += kind[4][...]

        for n, place in ((0, down), (1, gy), (2, up)):
            pending.append(copy(kind, 2 + n, (2, NEAR + n, 1), (6, 4 - n), (near, place, gz), back))
    for made in pending:
        made.wait_recv()

    @pl.when(first)
    def _():
        for kind in (features, positions):
            for made in direct_back[kind[0]]:
                made.wait_recv()
            kind[2][SELF] += kind[5][0] + kind[5][1] + kind[5][2]

    def final(kind, c):
        cut = slice(c, c + 128)
        total = kind[2][SELF, :, cut]
        for n in range(5):
            total = total + kind[6][n, :, cut]
        total = jnp.where(alive, total, 0.0)
        back_home = kind[2][RAW, :, cut]
        for b in range(atoms):
            back_home = back_home + jnp.where(homes[b], total[b : b + 1, :], 0.0)
        return back_home

    homes = [bound_ref[:, b : b + 1] == sub for b in range(atoms)]
    for h in range(halves):
        cs, cv = cotans[h]
        cut = slice(h * 128, h * 128 + 128)
        gscal_ref[:, cut] = final(features, h * 128) + cs
        for a in range(3):
            gvec_ref[a, :, cut] = final(features, (a + 1) * channels + h * 128) + cv[a]
    pull = jnp.sum(d_apart, axis=0) - final(positions, 0)
    for a in range(3):
        forces_ref[a : a + 1, :] = row_of(pull[:, a : a + 1])

    for made in pending:
        made.wait_send()

    @pl.when(gx != nx - 1)
    def _():
        for kind in (features, positions):
            far_copy[kind[0]].wait_send()

    @pl.when(last)
    def _():
        for made in direct_back[0] + direct_back[16]:
            made.wait_send()


def settle(*refs):
    for source, target in zip(refs[:4], refs[4:]):
        target[...] = source[...]


def shards(sizes):
    def run(
        places,
        scalars,
        vectors,
        species,
        bound_rows,
        bound_count,
        neighbour_ids,
        neighbour_count,
        radial_first,
        radial_second,
        radial_third,
        energy_table,
        vector_gains,
    ):
        atoms, channels = scalars.shape
        slots = neighbour_ids.shape[0]
        edges = slots * atoms
        packed = 4 * channels
        vmem = pl.BlockSpec(memory_space=pltpu.VMEM)
        hbm = pl.BlockSpec(memory_space=pl.ANY)
        f32 = jnp.float32
        operands = (
            bound_count,
            places.T,
            scalars,
            vectors.transpose(1, 0, 2),
            species.reshape(1, -1),
            bound_rows.reshape(1, -1),
            neighbour_ids.T,
            neighbour_count.reshape(1, -1),
            radial_first,
            radial_second,
            radial_third,
            energy_table,
            vector_gains.reshape(1, -1),
        )
        landing = [
            pltpu.VMEM(x.shape, x.dtype) for n, x in enumerate(operands) if n not in (0, 2, 3)
        ]
        out_shape = (
            jax.ShapeDtypeStruct((1, atoms), f32),
            jax.ShapeDtypeStruct((3, atoms), f32),
            jax.ShapeDtypeStruct((atoms, channels), f32),
            jax.ShapeDtypeStruct((3, atoms, channels), f32),
        )
        results = pl.pallas_call(
            functools.partial(kernel, sizes),
            out_shape=tuple(pltpu.VMEM(x.shape, x.dtype) for x in out_shape),
            in_specs=[pl.BlockSpec(memory_space=pltpu.SMEM)] + [hbm] * 12,
            out_specs=(vmem,) * 4,
            scratch_shapes=landing
            + [
                pltpu.SemaphoreType.DMA((14,)),
            ]
            + [
                pltpu.VMEM((count, atoms, row), f32)
                for row in (packed, 128)
                for count in (RAW + 1, RAW + 1, 18, 3, 3, 5)
            ]
            + [
                pltpu.VMEM((edges, 8 * (RAW + 1)), f32),
                pltpu.VMEM((8 * (RAW + 1), edges), f32),
                pltpu.VMEM((slots, atoms, 4 * channels), f32),
                pltpu.VMEM((slots, atoms, 6 * channels), f32),
                pltpu.VMEM((3, slots, atoms, 128), f32),
                pltpu.VMEM((3, slots, atoms, 128), f32),
                pltpu.VMEM((edges, 4 * channels), jnp.bfloat16),
                pltpu.VMEM((edges, 6 * channels), jnp.bfloat16),
                pltpu.SemaphoreType.DMA((31,)),
                pltpu.SemaphoreType.DMA((31,)),
                pltpu.SemaphoreType.DMA((31,)),
                pltpu.SemaphoreType.DMA((31,)),
                pltpu.SemaphoreType.REGULAR((3,)),
            ],
            compiler_params=pltpu.CompilerParams(
                collective_id=0, has_side_effects=True, vmem_limit_bytes=56 * 1024 * 1024
            ),
        )(*operands)
        energies, forces, grad_scalars, grad_vectors = pl.pallas_call(
            settle,
            out_shape=out_shape,
            in_specs=[vmem] * 4,
            out_specs=(vmem,) * 4,
            compiler_params=pltpu.CompilerParams(vmem_limit_bytes=1024 * 1024),
        )(*results)
        return energies.reshape(-1), forces.T, grad_scalars, grad_vectors.transpose(1, 0, 2)

    return run


def solution(mesh):
    spread = ("gx", "gy", "gz")
    in_specs = (
        P(spread, None),
        P(spread, None),
        P(spread, None, None),
        P(spread),
        P(spread),
        P(spread),
        P(None, spread),
        P(spread),
        P(),
        P(),
        P(),
        P(),
        P(),
    )
    out_specs = (P(spread), P(spread, None), P(spread, None), P(spread, None, None))
    sizes = tuple(mesh.shape[axis] for axis in spread)
    return jax.shard_map(
        shards(sizes), mesh=mesh, in_specs=in_specs, out_specs=out_specs, check_vma=False
    )
```
